32 devices in a mesh: particle: 4 (over z), tile: 8 (over y, x, core).
Axes of the slice: x: 2, y: 2, z: 4, core: 2. Of those that a mesh axis runs over, the one named last changes fastest.
Arguments:
- biomass: float32 [16, 32768], P('particle', 'tile'), as said below
- water: float32 [16, 32768], P('particle', 'tile'), may hold values from -5 to 5
- flow_blocks: bfloat16 [256, 3, 128, 128], P('tile'), may hold values from -0.15625 to 0.15625
- neighbours: int32 [256, 3], P('tile'), may hold values from 0 to 255, as said below
- rain: float32 [4, 16, 32768], P(None, 'particle', 'tile'), may hold values from -4 to 4
- growth_rate: float32 [32768], P('tile'), may hold values from 0.05 to 0.5
- observations: float32 [2, 32768], P(None, 'tile'), may hold values from -5 to 5
- obs_precision: float32 [32768], P('tile'), as said below
- ancestors: int32 [2, 16], replicated, may hold values from 0 to 15
Outputs:
- means: float32 [2, 2, 32768], P(None, None, 'tile')
- biomass_out: float32 [16, 32768], P('particle', 'tile')
- water_out: float32 [16, 32768], P('particle', 'tile')
The draws below stay inside these ranges and needn't reach their ends.
Inputs may be any that keep to these rules, and one draw needn't show every extreme that they name: `neighbours`: row n lists block n first, then one block 1 to 4 blocks below n and one 1 to 4 blocks above n, each clipped to the grid's ends. `biomass`: every entry lies between 0.5 and 2. `obs_precision`: every entry lies between 0.3 / sqrt(32768) and 3 / sqrt(32768).
All inputs are finite; a program needn't handle non-finite values.
Results may differ from the reference program's by a relative error of at most 0.0019.
Values may be sent and summed in bfloat16 or wider, within the bound.
No kernel may reach another device: no remote copies, remote signals or barrier semaphores. Data moves between devices by JAX's collectives and lax.ppermute only.
A program may use at most 64 MiB of HBM per device.

```python
import math
import jax
import jax.numpy as jnp

BLK = 128
NBR = 3
CYCLES = 2
DAYS = 2
HALO = 4
PARTICLES = 16
CELLS = 32768
BLOCKS = 256


def draw_biomass(key, part):
    unit = jax.random.uniform(key, (PARTICLES, CELLS), jnp.float32)
    return 0.5 + 1.5 * unit


def draw_obs_precision(key, part):
    factor = 1.0 / math.sqrt(CELLS)
    coef = jnp.exp(jax.random.uniform(key, (CELLS,), jnp.float32, math.log(0.3), math.log(3.0)))
    return coef * factor


def draw_neighbours(key, part):
    blocks = jnp.arange(BLOCKS, dtype=jnp.int32)
    key_low, key_high = jax.random.split(jax.random.fold_in(key, 5))
    below = jax.random.randint(key_low, (BLOCKS,), 1, HALO + 1)
    above = jax.random.randint(key_high, (BLOCKS,), 1, HALO + 1)
    lower = jnp.clip(blocks - below, 0, BLOCKS - 1)
    upper = jnp.clip(blocks + above, 0, BLOCKS - 1)
    return jnp.stack([blocks, lower, upper], axis=1).astype(jnp.int32)


def draw_ancestors(key, part):
    rows = []
    for cycle in range(CYCLES):
        sub = jax.random.fold_in(key, cycle + 11)
        k_heavy, k_pick, k_rest, k_first, k_second = jax.random.split(sub, 5)
        heavy = jax.random.randint(k_heavy, (), 0, PARTICLES)
        coin = jax.random.randint(k_pick, (PARTICLES,), 0, 10)
        rest = jax.random.randint(k_rest, (PARTICLES,), 0, PARTICLES)
        row = jnp.where(coin < 3, heavy, rest)
        first = jax.random.randint(k_first, (), 0, PARTICLES)
        second = (first + 1 + jax.random.randint(k_second, (), 0, PARTICLES - 1)) % PARTICLES
        row = row.at[first].set(0)
        row = row.at[second].set(PARTICLES - 1)
        rows.append(row)
    return jnp.stack(rows).astype(jnp.int32)


def block_levels(rng, dims, cuts, low, largest):
    gain = 1.0
    for position, parts in cuts:
        draws = jax.random.uniform(jax.random.fold_in(jax.random.fold_in(rng, 6), position), (parts,), jnp.float32, low / len(cuts), largest / len(cuts))
        gain = gain * jnp.repeat(jnp.exp(draws), dims[position] // parts).reshape((-1,) + (1,) * (len(dims) - 1 - position))
    return gain


def normal_values(stream_key, shape, width, limit, pieces=(), kind=jnp.bfloat16):
    values = width * jax.random.normal(stream_key, shape, jnp.float32)
    if pieces:
        values = values * block_levels(stream_key, shape, pieces, -0.22, 0.18)
    return jnp.clip(values, -limit, limit).astype(kind)


def setup_inputs(seed: int = 0) -> dict:
    key_list = jax.random.split(jax.random.key(seed), 10)
    return {
        "biomass": draw_biomass(jax.random.fold_in(key_list[9], 71), 0),
        "water": normal_values(key_list[1], (PARTICLES, CELLS), 1.0, 5.0, ((0, 4), (1, 8)), jnp.float32),
        "flow_blocks": normal_values(key_list[2], (BLOCKS, NBR, BLK, BLK), (4 * BLK * NBR) ** -0.5, 0.15625, ((0, 8),)),
        "neighbours": draw_neighbours(jax.random.fold_in(key_list[9], 71), 0),
        "rain": normal_values(key_list[4], (CYCLES * DAYS, PARTICLES, CELLS), 0.5, 4.0, ((1, 4), (2, 8)), jnp.float32),
        "growth_rate": jnp.clip(jnp.exp(math.log(0.5) - 2.3025851 * jax.random.uniform(key_list[5], (CELLS,), jnp.float32) ** block_levels(key_list[5], (CELLS,), ((0, 8),), -0.2, 0.2)), 0.05, 0.5),
        "observations": normal_values(key_list[6], (CYCLES, CELLS), 1.0, 5.0, ((1, 8),), jnp.float32),
        "obs_precision": draw_obs_precision(jax.random.fold_in(key_list[9], 71), 0),
        "ancestors": draw_ancestors(jax.random.fold_in(key_list[9], 71), 0),
    }


def advance(bio, wat, flow_blocks, neighbours, rain_day, growth_rate):
    count = bio.shape[0]
    wb = wat.astype(jnp.bfloat16).reshape(count, BLOCKS, BLK)
    nearby = wb[:, neighbours].astype(jnp.float32)
    flux = jnp.einsum("pnkc,nkdc->pnd", nearby, flow_blocks.astype(jnp.float32)).reshape(count, CELLS)
    wet = wat * wat / (1.0 + wat * wat)
    new_bio = bio + growth_rate * bio * (wet - 0.4 * bio)
    new_wat = wat + flux + rain_day - 0.2 * bio * wet
    return new_bio, new_wat


def reference(biomass, water, flow_blocks, neighbours, rain, growth_rate, observations, obs_precision, ancestors):
    bio, wat = biomass, water
    collected = []
    for cycle in range(CYCLES):
        log_weight = -0.5 * jnp.sum(obs_precision * (bio - observations[cycle]) ** 2, axis=1)
        shifted = jnp.exp(log_weight - jnp.max(log_weight))
        weight = shifted / jnp.sum(shifted)
        collected.append(jnp.stack([jnp.sum(weight[:, None] * bio, axis=0), jnp.sum(weight[:, None] * wat, axis=0)]))
        bio = bio[ancestors[cycle]]
        wat = wat[ancestors[cycle]]
        for day in range(DAYS):
            bio, wat = advance(bio, wat, flow_blocks, neighbours, rain[cycle * DAYS + day], growth_rate)
    return jnp.stack(collected), bio, wat
```

```python
import functools

import jax
import jax.numpy as jnp
from jax import lax
from jax.experimental import pallas as pl
from jax.experimental.pallas import tpu as pltpu
from jax.sharding import PartitionSpec as P

BLK = 128
CYCLES = 2
HALO = 4
WIDE = 2 * HALO
BOUNDS = (2.0, 5.0, 4.0, 4.0)
SCALE_STEPS = 32000.0
STEPS = 32767.0
VMEM = pl.BlockSpec(memory_space=pltpu.VMEM)
SMEM = pl.BlockSpec(memory_space=pltpu.SMEM)


def run(count, unroll, step, carry):
    if unroll:
        for n in range(count):
            carry = step(n, carry)
        return carry
    return lax.fori_loop(0, count, step, carry)


def lanes(n):
    if isinstance(n, int):
        return slice(n * BLK, (n + 1) * BLK)
    return pl.ds(pl.multiple_of(n * BLK, BLK), BLK)


def wetness(w):
    sq = w * w
    return sq / (1.0 + sq)


def dot_t(x, f):
    return lax.dot_general(x, f, (((1,), (1,)), ((), ())), preferred_element_type=jnp.float32)


def pack_kernel(bio, wat, rain, wire, held):
    part, cells = bio.shape
    nb = cells // BLK
    held[0:part, :] = bio[...]
    held[part : 2 * part, :] = wat[...]
    held[2 * part : 3 * part, :] = rain[0]
    held[3 * part : 4 * part, :] = rain[1]
    rows = 4 * part
    big = jnp.abs(held[:, 0:BLK])
    for n in range(1, nb):
        big = jnp.maximum(big, jnp.abs(held[:, lanes(n)]))
    top = jnp.max(big, axis=1, keepdims=True)
    field = lax.broadcasted_iota(jnp.int32, (rows, 1), 0) // part
    unit = jnp.where(field == 0, BOUNDS[0], jnp.where(field == 1, BOUNDS[1], BOUNDS[2])) / SCALE_STEPS
    code = jnp.floor(top / unit) + 1.0
    inv = STEPS / (code * unit)
    wire[:, lanes(nb)] = jnp.broadcast_to(code, (rows, BLK)).astype(jnp.int32).astype(jnp.int16)
    for n in range(nb):
        wire[:, lanes(n)] = jnp.round(held[:, lanes(n)] * inv).astype(jnp.int32).astype(jnp.int16)


def sides():
    pos = lax.axis_index("tile")
    return lax.rem(pos, 2) == 0


def open_kernel(members, unroll, *refs):
    pieces = refs[:members]
    anc, growth, prec, obs = refs[members : members + 4]
    wb, v0, b1, r1, bq, wq, miss, pay_a, pay_b = refs[members + 4 : members + 13]
    sel = refs[-1]
    nb = growth.shape[0]
    slots = anc.shape[1]
    rows = pieces[0].shape[0]
    part = rows // 4
    depth = members * rows * 2
    me = lax.axis_index("particle")
    line = lax.broadcasted_iota(jnp.int32, (slots, slots), 0)
    lane = lax.broadcasted_iota(jnp.int32, (slots, slots), 1)
    first = jnp.broadcast_to(anc[0:1, :], (slots, slots)).astype(jnp.float32)
    chosen = jnp.sum(jnp.where(line == lane, first, 0.0), axis=1, keepdims=True)
    own = lax.broadcasted_iota(jnp.int32, (slots, 1), 0).astype(jnp.float32)
    col = lax.broadcasted_iota(jnp.int32, (slots, depth), 1)
    piece = col // (2 * rows)
    high = (col // rows) % 2 == 0
    field = (col // part) % 4
    source = ((piece ^ me) * part + col % part).astype(jnp.float32)
    value = jnp.where(high, 256.0, 1.0)
    for g, f in enumerate((0, 1, 2, 3, 0, 1)):
        want = chosen if g < 2 else own
        hit = jnp.logical_and(field == f, source == want)
        sel[g * slots : (g + 1) * slots, :] = jnp.where(hit, value, 0.0).astype(jnp.bfloat16)

    def decode(n):
        parts = []
        for ref in pieces:
            q = ref[:, lanes(n)].astype(jnp.int32)
            parts.append((q >> 8).astype(jnp.float32).astype(jnp.bfloat16))
            parts.append((q & 255).astype(jnp.float32).astype(jnp.bfloat16))
        return jnp.dot(sel[...], jnp.concatenate(parts, axis=0), preferred_element_type=jnp.float32)

    codes = decode(nb)
    scale = [
        codes[g * slots : (g + 1) * slots] * (BOUNDS[f] / SCALE_STEPS / STEPS)
        for g, f in enumerate((0, 1, 2, 3, 0, 1))
    ]

    def step(n, acc):
        got = decode(n)
        b, w, rain0, rain1, bi, wi = (got[g * slots : (g + 1) * slots] * scale[g] for g in range(6))
        s = wetness(w)
        row = pl.ds(n, 1)
        g = growth[row, :]
        wb[n] = w.astype(jnp.bfloat16)
        v0[n] = w + rain0 - 0.2 * b * s
        b1[n] = b + g * b * (s - 0.4 * b)
        r1[n] = rain1
        bq[n] = bi
        wq[n] = wi
        off = bi - obs[0:1, lanes(n)]
        return acc + prec[row, :] * (off * off)

    miss[...] = run(nb, unroll, step, jnp.zeros((slots, BLK), jnp.float32))
    even = sides()
    for pay, right in ((pay_a, even), (pay_b, jnp.logical_not(even))):
        pay[0:WIDE] = wb[pl.ds(jnp.where(right, nb - WIDE, 0), WIDE)]
        edge = v0[pl.ds(jnp.where(right, nb - HALO, 0), HALO)]
        top = edge.astype(jnp.bfloat16)
        pay[WIDE : WIDE + HALO] = top
        pay[WIDE + HALO : WIDE + 2 * HALO] = (edge - top.astype(jnp.float32)).astype(jnp.bfloat16)


def day0_kernel(
    unroll, wb, v0, b1, r1, got_a, got_b, flow, flow_a, flow_b, ids, ids_a, ids_b, growth, prec, obs, miss,
    wb1, v1, b2, total, ext,
):
    nb = growth.shape[0]
    slots = wb.shape[1]
    pos = lax.axis_index("tile")
    count = lax.axis_size("tile")
    even = sides()
    ext[WIDE : WIDE + nb] = wb[...]
    for got, right in ((got_a, even), (got_b, jnp.logical_not(even))):
        ext[pl.ds(jnp.where(right, nb + WIDE, 0), WIDE)] = got[0:WIDE]
    other = jnp.where(even, lax.rem(pos + count - 1, count), lax.rem(pos + 1, count))
    for got, fl, idx, right, sender in (
        (got_a, flow_a, ids_a, even, pos ^ 1),
        (got_b, flow_b, ids_b, jnp.logical_not(even), other),
    ):
        shift = jnp.where(right, nb, -nb) + WIDE - sender * nb
        spot = jnp.where(right, nb + HALO, 0)
        for m in range(HALO):
            flux = sum(dot_t(ext[idx[m, k] + shift], fl[m, k]) for k in range(3))
            edge = got[WIDE + m].astype(jnp.float32) + got[WIDE + HALO + m].astype(jnp.float32)
            wb1[spot + m] = (edge + flux).astype(jnp.bfloat16)
    base = WIDE - pos * nb

    def step(n, acc):
        flux = (
            dot_t(ext[n + WIDE], flow[n, 0])
            + dot_t(ext[ids[n, 1] + base], flow[n, 1])
            + dot_t(ext[ids[n, 2] + base], flow[n, 2])
        )
        w = v0[n] + flux
        wb1[n + HALO] = w.astype(jnp.bfloat16)
        s = wetness(w)
        row = pl.ds(n, 1)
        b = b1[n]
        v1[n] = w + r1[n] - 0.2 * b * s
        b = b + growth[row, :] * b * (s - 0.4 * b)
        b2[n] = b
        off = b - obs[1:2, lanes(n)]
        return acc + prec[row, :] * (off * off)

    total[0:slots, :] = miss[...]
    total[slots : 2 * slots, :] = run(nb, unroll, step, jnp.zeros((slots, BLK), jnp.float32))


def day1_kernel(unroll, wb1, v1, b2, flow, ids, anc, rain, w2, ws, bs, v2, pay_a, pay_b):
    nb = v1.shape[0]
    part = rain.shape[1]
    pos = lax.axis_index("tile")
    me = lax.axis_index("particle")
    even = sides()
    base = HALO - pos * nb
    picks = [anc[1, me * part + i] for i in range(part)]

    def step(n, carry):
        w2[n] = v1[n] + (
            dot_t(wb1[n + HALO], flow[n, 0])
            + dot_t(wb1[ids[n, 1] + base], flow[n, 1])
            + dot_t(wb1[ids[n, 2] + base], flow[n, 2])
        )
        return carry

    run(nb, unroll, step, 0)

    def pick(n, carry):
        for i in range(part):
            ws[n, i : i + 1, :] = w2[n, pl.ds(picks[i], 1), :]
            bs[n, i : i + 1, :] = b2[n, pl.ds(picks[i], 1), :]
        w = ws[n]
        v2[n] = w + rain[0, :, lanes(n)] - 0.2 * bs[n] * wetness(w)
        return carry

    run(nb, unroll, pick, 0)
    for pay, right in ((pay_a, even), (pay_b, jnp.logical_not(even))):
        pay[0:WIDE] = ws[pl.ds(jnp.where(right, nb - WIDE, 0), WIDE)]
        pay[WIDE : WIDE + HALO] = v2[pl.ds(jnp.where(right, nb - HALO, 0), HALO)]


def close_kernel(
    unroll, ws, bs, v2, got_a, got_b, flow, flow_a, flow_b, ids, ids_a, ids_b, growth, rain,
    bio_out, wat_out, ext, ext3, w3,
):
    nb = growth.shape[0]
    pos = lax.axis_index("tile")
    count = lax.axis_size("tile")
    even = sides()
    half = jnp.bfloat16
    ext[WIDE : WIDE + nb] = ws[...]
    for got, right in ((got_a, even), (got_b, jnp.logical_not(even))):
        ext[pl.ds(jnp.where(right, nb + WIDE, 0), WIDE)] = got[0:WIDE]
    other = jnp.where(even, lax.rem(pos + count - 1, count), lax.rem(pos + 1, count))
    for got, fl, idx, right, sender in (
        (got_a, flow_a, ids_a, even, pos ^ 1),
        (got_b, flow_b, ids_b, jnp.logical_not(even), other),
    ):
        shift = jnp.where(right, nb, -nb) + WIDE - sender * nb
        spot = jnp.where(right, nb + HALO, 0)
        for m in range(HALO):
            flux = sum(dot_t(ext[idx[m, k] + shift].astype(half), fl[m, k]) for k in range(3))
            ext3[spot + m] = got[WIDE + m] + flux
    base = WIDE - pos * nb

    def step2(n, carry):
        ext3[n + HALO] = v2[n] + (
            dot_t(ext[n + WIDE].astype(half), flow[n, 0])
            + dot_t(ext[ids[n, 1] + base].astype(half), flow[n, 1])
            + dot_t(ext[ids[n, 2] + base].astype(half), flow[n, 2])
        )
        return carry

    run(nb, unroll, step2, 0)
    base3 = HALO - pos * nb

    def step3(n, carry):
        g = growth[pl.ds(n, 1), :]
        s = wetness(ws[n])
        b = bs[n]
        b = b + g * b * (s - 0.4 * b)
        w = ext3[n + HALO]
        s = wetness(w)
        flux = (
            dot_t(w.astype(half), flow[n, 0])
            + dot_t(ext3[ids[n, 1] + base3].astype(half), flow[n, 1])
            + dot_t(ext3[ids[n, 2] + base3].astype(half), flow[n, 2])
        )
        wat_out[:, lanes(n)] = w + flux + rain[1, :, lanes(n)] - 0.2 * b * s
        bio_out[:, lanes(n)] = b + g * b * (s - 0.4 * b)
        return carry

    run(nb, unroll, step3, 0)


def means_kernel(unroll, mine, theirs, bq, wq, b2, w2, means):
    nb, slots = bq.shape[:2]
    lw = -0.5 * jnp.sum(mine[...] + theirs[...], axis=1, keepdims=True)
    weights = []
    for c in range(CYCLES):
        x = lw[c * slots : (c + 1) * slots]
        e = jnp.exp(x - jnp.max(x, axis=0, keepdims=True))
        weights.append(jnp.broadcast_to(e / jnp.sum(e, axis=0, keepdims=True), (slots, BLK)))

    def step(n, carry):
        for c, pair in enumerate(((bq, wq), (b2, w2))):
            for f, ref in enumerate(pair):
                means[c, f : f + 1, lanes(n)] = jnp.sum(weights[c] * ref[n], axis=0, keepdims=True)
        return carry

    run(nb, unroll, step, 0)


def call(kernel, out, specs, scratch=(), mib=32):
    return pl.pallas_call(
        kernel,
        out_shape=tuple(jax.ShapeDtypeStruct(s, d) for s, d in out),
        in_specs=specs,
        out_specs=tuple(VMEM for _ in out),
        scratch_shapes=list(scratch),
        compiler_params=pltpu.CompilerParams(vmem_limit_bytes=mib * 2**20),
    )


def body(biomass, water, flow_blocks, neighbours, rain, growth_rate, observations, obs_precision, ancestors):
    part, cells = biomass.shape
    nb = cells // BLK
    members, tiles = lax.axis_size("particle"), lax.axis_size("tile")
    slots = members * part
    unroll = slots <= 16
    f32, bf16 = jnp.float32, jnp.bfloat16
    pos = lax.axis_index("tile")
    even = lax.rem(pos, 2) == 0
    swap_a = [(i, i ^ 1) for i in range(tiles)]
    swap_b = [(i, (i - 1) % tiles if i % 2 == 0 else (i + 1) % tiles) for i in range(tiles)]
    growth = growth_rate.reshape(nb, BLK)
    prec = obs_precision.reshape(nb, BLK)

    wire = pl.pallas_call(
        pack_kernel,
        grid=(1,),
        out_shape=jax.ShapeDtypeStruct((4 * part, cells + BLK), jnp.int16),
        in_specs=[
            pl.BlockSpec((part, cells), lambda i: (0, 0)),
            pl.BlockSpec((part, cells), lambda i: (0, 0)),
            pl.BlockSpec((2, part, cells), lambda i: (0, 0, 0)),
        ],
        out_specs=pl.BlockSpec((4 * part, cells + BLK), lambda i: (0, 0)),
        scratch_shapes=[pltpu.VMEM((4 * part, cells), f32)],
    )(biomass, water, rain)
    pieces = [wire] + [
        lax.ppermute(wire, "particle", [(i, i ^ j) for i in range(members)]) for j in range(1, members)
    ]
    start_a = jnp.where(even, nb - HALO, 0)
    start_b = jnp.where(even, 0, nb - HALO)
    flow_a = lax.ppermute(lax.dynamic_slice_in_dim(flow_blocks, start_a, HALO), "tile", swap_a)
    flow_b = lax.ppermute(lax.dynamic_slice_in_dim(flow_blocks, start_b, HALO), "tile", swap_b)
    ids_a = lax.ppermute(lax.dynamic_slice_in_dim(neighbours, start_a, HALO), "tile", swap_a)
    ids_b = lax.ppermute(lax.dynamic_slice_in_dim(neighbours, start_b, HALO), "tile", swap_b)

    field = ((nb, slots, BLK), f32)
    wb, v0, b1, r1, bq, wq, miss, pay_a, pay_b = call(
        functools.partial(open_kernel, members, unroll),
        [((nb, slots, BLK), bf16), field, field, field, field, field, ((slots, BLK), f32)]
        + [((WIDE + 2 * HALO, slots, BLK), bf16)] * 2,
        [VMEM] * (members + 4),
        [pltpu.VMEM((6 * slots, members * part * 8), bf16)],
    )(*pieces, ancestors, growth, prec, observations)
    got_a = lax.ppermute(pay_a, "tile", swap_a)
    got_b = lax.ppermute(pay_b, "tile", swap_b)
    wb1, v1, b2, total = call(
        functools.partial(day0_kernel, unroll),
        [((nb + WIDE, slots, BLK), bf16), field, field, ((2 * slots, BLK), f32)],
        [VMEM] * 9 + [SMEM] * 3 + [VMEM] * 4,
        [pltpu.VMEM((nb + 2 * WIDE, slots, BLK), bf16)],
    )(wb, v0, b1, r1, got_a, got_b, flow_blocks, flow_a, flow_b, neighbours, ids_a, ids_b, growth, prec, observations, miss)
    few = ((nb, part, BLK), f32)
    w2, ws, bs, v2, end_a, end_b = call(
        functools.partial(day1_kernel, unroll),
        [field, few, few, few] + [((WIDE + HALO, part, BLK), f32)] * 2,
        [VMEM] * 4 + [SMEM] * 2 + [VMEM],
    )(wb1, v1, b2, flow_blocks, neighbours, ancestors, rain[2:])
    last_a = lax.ppermute(end_a, "tile", swap_a)
    last_b = lax.ppermute(end_b, "tile", swap_b)
    span = 1
    theirs = lax.ppermute(total, "tile", swap_a)
    while span * 2 < tiles:
        span *= 2
        total = total + theirs
        theirs = lax.ppermute(total, "tile", [(i, i ^ span) for i in range(tiles)])
    bio_out, wat_out = call(
        functools.partial(close_kernel, unroll),
        [((part, cells), f32)] * 2,
        [VMEM] * 8 + [SMEM] * 3 + [VMEM] * 2,
        [
            pltpu.VMEM((nb + 2 * WIDE, part, BLK), f32),
            pltpu.VMEM((nb + WIDE, part, BLK), f32),
            pltpu.VMEM((8, BLK), f32),
        ],
    )(ws, bs, v2, last_a, last_b, flow_blocks, flow_a, flow_b, neighbours, ids_a, ids_b, growth, rain[2:])
    (means,) = call(
        functools.partial(means_kernel, unroll), [((CYCLES, 2, cells), f32)], [VMEM] * 6
    )(total, theirs, bq, wq, b2, w2)
    return means, bio_out, wat_out


def solution(mesh):
    placed = (
        P("particle", "tile"),
        P("particle", "tile"),
        P("tile", None, None, None),
        P("tile", None),
        P(None, "particle", "tile"),
        P("tile"),
        P(None, "tile"),
        P("tile"),
        P(),
    )
    return jax.shard_map(
        body,
        mesh=mesh,
        in_specs=placed,
        out_specs=(P(None, None, "tile"), P("particle", "tile"), P("particle", "tile")),
        check_vma=False,
    )
```

```python
import functools

import jax
import jax.numpy as jnp
from jax import lax
from jax.experimental import pallas as pl
from jax.experimental.pallas import tpu as pltpu
from jax.sharding import PartitionSpec as P

BLK = 128
CYCLES = 2
HALO = 4
WIDE = 2 * HALO
NBR = 3
BOUNDS = (2.0, 5.0, 4.0)
SCALE_STEPS = 32000.0
STEPS = 32767.0
VMEM = pl.BlockSpec(memory_space=pltpu.VMEM)
SMEM = pl.BlockSpec(memory_space=pltpu.SMEM)
HBM = pl.BlockSpec(memory_space=pltpu.HBM)


def run(count, unroll, step, carry):
    if unroll:
        for n in range(count):
            carry = step(n, carry)
        return carry
    return lax.fori_loop(0, count, step, carry)


def lanes(n, at=0):
    if isinstance(n, int):
        return slice(at + n * BLK, at + (n + 1) * BLK)
    return pl.ds(pl.multiple_of(at + n * BLK, BLK), BLK)


def wetness(w):
    sq = w * w
    return sq / (1.0 + sq)


def flux_of(xs, flow):
    return jnp.dot(jnp.concatenate(xs, axis=1), flow, preferred_element_type=jnp.float32)


def right_first():
    return lax.rem(lax.axis_index("tile"), 2) == 0


def pack_kernel(
    bio, wat, rain, growth, prec, obs, anc,
    wire, later, growth_out, prec_out, obs_out, anc_out, rain_out,
    fields, held, held1, factor, sems,
):
    part, cells = bio.shape
    nb = cells // BLK
    copies = [
        pltpu.make_async_copy(src, dst, sems.at[i])
        for i, (src, dst) in enumerate(
            (
                (bio, fields.at[0]),
                (wat, fields.at[1]),
                (rain.at[0], fields.at[2]),
                (rain.at[1], fields.at[3]),
                (growth, growth_out),
                (prec, prec_out),
                (obs, obs_out),
                (anc, anc_out),
                (rain.at[pl.ds(2, 2)], rain_out),
            )
        )
    ]
    for c in copies:
        c.start()
    half, quarter = cells // 2, cells // 4
    codes = []
    for f in range(4):
        copies[f].wait()
        big = jnp.abs(fields[f, :, 0:BLK])
        for n in range(1, nb):
            big = jnp.maximum(big, jnp.abs(fields[f, :, lanes(n)]))
        unit = BOUNDS[min(f, 2)] / SCALE_STEPS
        code = jnp.floor(jnp.max(big, axis=1, keepdims=True) / unit) + 1.0
        inv = jnp.broadcast_to(STEPS / (code * unit), (part, BLK))
        codes.append(jnp.broadcast_to(code, (part, BLK)))
        if f < 2:
            for h in range(2):
                row = (2 * h + f) * part
                held[row : row + part, 0:half] = fields[f, :, h * half : (h + 1) * half]
                factor[0, row : row + part, :] = inv
        else:
            ref, at = (held, half) if f == 2 else (held1, 0)
            for q in range(4):
                ref[q * part : (q + 1) * part, at : at + quarter] = fields[f, :, q * quarter : (q + 1) * quarter]
                factor[f - 1, q * part : (q + 1) * part, :] = inv
    factor[3] = jnp.zeros(factor.shape[1:], jnp.float32)
    factor[4] = jnp.zeros(factor.shape[1:], jnp.float32)
    for f in range(3):
        factor[3, f * part : (f + 1) * part, :] = codes[f]
    factor[4, 0:part, :] = codes[3]

    def coded(x):
        return jnp.round(x).astype(jnp.int32).astype(jnp.int16)

    pairs, quads = nb // 2, nb // 4
    for n in range(pairs + quads):
        wire[:, lanes(n)] = coded(held[:, lanes(n)] * factor[0 if n < pairs else 1])
    wire[:, lanes(pairs + quads)] = coded(factor[3])
    for n in range(quads):
        later[:, lanes(n)] = coded(held1[:, lanes(n)] * factor[2])
    later[:, lanes(quads)] = coded(factor[4])
    for c in copies[4:]:
        c.wait()


def flow_kernel(after, flow, ids, turned, pay_a, pay_b, raw, sems):
    nb = flow.shape[0]
    chunk = nb // 4
    copies = [
        pltpu.make_async_copy(flow.at[pl.ds(c * chunk, chunk)], raw.at[pl.ds(c * chunk, chunk)], sems.at[c])
        for c in range(4)
    ]
    for c in copies:
        c.start()
    pos = lax.axis_index("tile")
    even = right_first()
    depth = NBR * BLK
    for c in range(4):
        copies[c].wait()
        for n in range(c * chunk, (c + 1) * chunk):
            for k in range(NBR):
                turned[n, k * BLK : (k + 1) * BLK, :] = raw[n, k].T
    line = lax.broadcasted_iota(jnp.int32, (16, BLK), 0)
    for pay, right in ((pay_a, even), (pay_b, jnp.logical_not(even))):
        start = jnp.where(right, nb - HALO, 0)
        away = jnp.zeros((16, BLK), jnp.float32)
        for m in range(HALO):
            pay[m * depth : (m + 1) * depth, :] = turned[start + m]
            n = start + m + pos * nb
            for k, gap in enumerate((n - ids[start + m, 1], ids[start + m, 2] - n)):
                away = jnp.where(line == 2 * m + k, gap.astype(jnp.float32), away)
        pay[HALO * depth : HALO * depth + 16, :] = away.astype(jnp.bfloat16)


def halo_flux(ext, pay, right, nb, m):
    depth = NBR * BLK
    away = pay[HALO * depth : HALO * depth + 16, :].astype(jnp.float32)
    at = jnp.where(right, nb + WIDE + m, HALO + m)
    xs = [ext[at].astype(jnp.bfloat16)]
    for k, sign in enumerate((-1, 1)):
        gap = jnp.broadcast_to(away[2 * m + k : 2 * m + k + 1, :], ext.shape[1:])
        x = jnp.zeros(ext.shape[1:], jnp.float32)
        for d in range(HALO + 1):
            x = jnp.where(gap == d, ext[at + sign * d].astype(jnp.float32), x)
        xs.append(x.astype(jnp.bfloat16))
    return flux_of(xs, pay[m * depth : (m + 1) * depth, :])


def decode(sel, pieces, cols):
    parts = []
    for ref in pieces:
        q = ref[:, cols].astype(jnp.int32)
        parts.append((q >> 8).astype(jnp.float32).astype(jnp.bfloat16))
        parts.append((q & 255).astype(jnp.float32).astype(jnp.bfloat16))
    return jnp.dot(sel, jnp.concatenate(parts, axis=0), preferred_element_type=jnp.float32)


def open_kernel(members, unroll, *refs):
    pieces = refs[:members]
    anc, growth, prec, obs = refs[members : members + 4]
    wb, v0, b1, bq, wq, miss, quad, pay_a, pay_b = refs[members + 4 : members + 13]
    pair, scaler = refs[-2:]
    nb = growth.shape[0]
    slots = anc.shape[1]
    rows = pieces[0].shape[0]
    part = rows // 4
    depth = members * rows * 2
    me = lax.axis_index("particle")
    line = lax.broadcasted_iota(jnp.int32, (slots, slots), 0)
    lane = lax.broadcasted_iota(jnp.int32, (slots, slots), 1)
    first = jnp.broadcast_to(anc[0:1, :], (slots, slots)).astype(jnp.float32)
    chosen = jnp.sum(jnp.where(line == lane, first, 0.0), axis=1, keepdims=True)
    own = lax.broadcasted_iota(jnp.int32, (slots, 1), 0).astype(jnp.float32)
    col = lax.broadcasted_iota(jnp.int32, (slots, depth), 1)
    value = jnp.where((col // rows) % 2 == 0, 256.0, 1.0)
    group = (col % rows) // part
    source = (((col // (2 * rows)) ^ me) * part + col % part).astype(jnp.float32)

    def hits(g, want):
        return jnp.where(jnp.logical_and(group == g, source == want), value, 0.0).astype(jnp.bfloat16)

    for h in range(2):
        for i, want in enumerate((chosen, chosen, own, own)):
            at = (4 * h + i) * slots
            pair[at : at + slots, :] = hits(2 * h + i % 2, want)
    for g in range(4):
        quad[g * slots : (g + 1) * slots, :] = hits(g, own)
    for i, (g, want) in enumerate(((0, chosen), (1, chosen), (0, own), (1, own), (2, own))):
        scaler[i * slots : (i + 1) * slots, :] = hits(g, want)

    pairs, quads = nb // 2, nb // 4
    codes = decode(scaler[...], pieces, lanes(pairs + quads))
    scale = [
        codes[i * slots : (i + 1) * slots] * (BOUNDS[f] / SCALE_STEPS / STEPS) for i, f in enumerate((0, 1, 0, 1, 2))
    ]

    def step(m, acc):
        wet = decode(quad[...], pieces, lanes(m, pairs * BLK))
        for p in range(2):
            got = decode(pair[...], pieces, lanes(m + p * quads))
            for h in range(2):
                q = 2 * h + p
                n = m + q * quads
                b, w, bi, wi = (got[(4 * h + i) * slots : (4 * h + i + 1) * slots] * scale[i] for i in range(4))
                rain0 = wet[q * slots : (q + 1) * slots] * scale[4]
                s = wetness(w)
                row = pl.ds(n, 1)
                wb[n] = w.astype(jnp.bfloat16)
                v0[n] = w + rain0 - 0.2 * b * s
                b1[n] = b + growth[row, :] * b * (s - 0.4 * b)
                bq[n] = bi
                wq[n] = wi
                off = bi - obs[0:1, lanes(n)]
                acc = acc + prec[row, :] * (off * off)
        return acc

    miss[...] = run(quads, unroll, step, jnp.zeros((slots, BLK), jnp.float32))
    even = right_first()
    for pay, right in ((pay_a, even), (pay_b, jnp.logical_not(even))):
        pay[0:WIDE] = wb[pl.ds(jnp.where(right, nb - WIDE, 0), WIDE)]
        edge = v0[pl.ds(jnp.where(right, nb - HALO, 0), HALO)]
        top = edge.astype(jnp.bfloat16)
        pay[WIDE : WIDE + HALO] = top
        pay[WIDE + HALO : WIDE + 2 * HALO] = (edge - top.astype(jnp.float32)).astype(jnp.bfloat16)


def day0_kernel(
    unroll, wb, v0, b1, got_a, got_b, flow, flow_a, flow_b, ids, growth, prec, obs, miss,
    wb1, v1, b2, total, ext,
):
    nb = growth.shape[0]
    slots = wb.shape[1]
    pos = lax.axis_index("tile")
    even = right_first()
    ext[WIDE : WIDE + nb] = wb[...]
    sides = ((got_a, flow_a, even), (got_b, flow_b, jnp.logical_not(even)))
    for got, _, right in sides:
        ext[pl.ds(jnp.where(right, nb + WIDE, 0), WIDE)] = got[0:WIDE]
    base = WIDE - pos * nb

    def step(n, acc):
        w = v0[n] + flux_of((ext[n + WIDE], ext[ids[n, 1] + base], ext[ids[n, 2] + base]), flow[n])
        wb1[n + HALO] = w.astype(jnp.bfloat16)
        s = wetness(w)
        row = pl.ds(n, 1)
        b = b1[n]
        v1[n] = w - 0.2 * b * s
        b = b + growth[row, :] * b * (s - 0.4 * b)
        b2[n] = b
        off = b - obs[1:2, lanes(n)]
        return acc + prec[row, :] * (off * off)

    total[0:slots, :] = miss[...]
    total[slots : 2 * slots, :] = run(nb, unroll, step, jnp.zeros((slots, BLK), jnp.float32))
    for got, pay, right in sides:
        spot = jnp.where(right, nb + HALO, 0)
        for m in range(HALO):
            edge = got[WIDE + m].astype(jnp.float32) + got[WIDE + HALO + m].astype(jnp.float32)
            wb1[spot + m] = (edge + halo_flux(ext, pay, right, nb, m)).astype(jnp.bfloat16)


def day1_kernel(members, unroll, *refs):
    pieces = refs[:members]
    wb1, v1, b2, quad, flow, ids, anc, rain, w2, ws, bs, v2, pay_a, pay_b = refs[members:]
    nb, slots = v1.shape[:2]
    part = rain.shape[1]
    pos = lax.axis_index("tile")
    me = lax.axis_index("particle")
    even = right_first()
    base = HALO - pos * nb
    picks = [anc[1, me * part + i] for i in range(part)]
    quads = nb // 4
    scale = decode(quad[0:slots, :], pieces, lanes(quads)) * (BOUNDS[2] / SCALE_STEPS / STEPS)

    def step(m, carry):
        wet = decode(quad[...], pieces, lanes(m))
        for q in range(4):
            n = m + q * quads
            flux = flux_of((wb1[n + HALO], wb1[ids[n, 1] + base], wb1[ids[n, 2] + base]), flow[n])
            w2[n] = v1[n] + flux + wet[q * slots : (q + 1) * slots] * scale
        return carry

    run(quads, unroll, step, 0)

    def pick(n, carry):
        for i in range(part):
            ws[n, i : i + 1, :] = w2[n, pl.ds(picks[i], 1), :]
            bs[n, i : i + 1, :] = b2[n, pl.ds(picks[i], 1), :]
        w = ws[n]
        v2[n] = w + rain[0, :, lanes(n)] - 0.2 * bs[n] * wetness(w)
        return carry

    run(nb, unroll, pick, 0)
    for pay, right in ((pay_a, even), (pay_b, jnp.logical_not(even))):
        pay[0:WIDE] = ws[pl.ds(jnp.where(right, nb - WIDE, 0), WIDE)]
        pay[WIDE : WIDE + HALO] = v2[pl.ds(jnp.where(right, nb - HALO, 0), HALO)]


def close_kernel(
    unroll, ws, bs, v2, got_a, got_b, flow, flow_a, flow_b, ids, growth, rain, bio_out, wat_out, ext, ext3
):
    nb = growth.shape[0]
    pos = lax.axis_index("tile")
    even = right_first()
    half = jnp.bfloat16
    ext[WIDE : WIDE + nb] = ws[...]
    sides = ((got_a, flow_a, even), (got_b, flow_b, jnp.logical_not(even)))
    for got, _, right in sides:
        ext[pl.ds(jnp.where(right, nb + WIDE, 0), WIDE)] = got[0:WIDE]
    for got, pay, right in sides:
        spot = jnp.where(right, nb + HALO, 0)
        for m in range(HALO):
            ext3[spot + m] = got[WIDE + m] + halo_flux(ext, pay, right, nb, m)

    def near(ref, n, at):
        base = at - pos * nb
        return [ref[i].astype(half) for i in (n + at, ids[n, 1] + base, ids[n, 2] + base)]

    def step2(n, carry):
        ext3[n + HALO] = v2[n] + flux_of(near(ext, n, WIDE), flow[n])
        return carry

    run(nb, unroll, step2, 0)

    def step3(n, carry):
        g = growth[pl.ds(n, 1), :]
        b = bs[n]
        b = b + g * b * (wetness(ws[n]) - 0.4 * b)
        w = ext3[n + HALO]
        s = wetness(w)
        wat_out[:, lanes(n)] = w + flux_of(near(ext3, n, HALO), flow[n]) + rain[1, :, lanes(n)] - 0.2 * b * s
        bio_out[:, lanes(n)] = b + g * b * (s - 0.4 * b)
        return carry

    run(nb, unroll, step3, 0)


def means_kernel(unroll, count, *refs):
    bq, wq, b2, w2, means = refs[count:]
    nb, slots = bq.shape[:2]
    level = [ref[...] for ref in refs[:count]]
    while len(level) > 1:
        level = [a + b for a, b in zip(level[::2], level[1::2])]
    lw = -0.5 * jnp.sum(level[0], axis=1, keepdims=True)
    weights = []
    for c in range(CYCLES):
        x = lw[c * slots : (c + 1) * slots]
        e = jnp.exp(x - jnp.max(x, axis=0, keepdims=True))
        weights.append(jnp.broadcast_to(e / jnp.sum(e, axis=0, keepdims=True), (slots, BLK)))

    def step(n, carry):
        for c, fields in enumerate(((bq, wq), (b2, w2))):
            for f, ref in enumerate(fields):
                means[c, f : f + 1, lanes(n)] = jnp.sum(weights[c] * ref[n], axis=0, keepdims=True)
        return carry

    run(nb, unroll, step, 0)


def call(kernel, out, specs, scratch=(), mib=32):
    return pl.pallas_call(
        kernel,
        out_shape=tuple(jax.ShapeDtypeStruct(s, d) for s, d in out),
        in_specs=specs,
        out_specs=tuple(VMEM for _ in out),
        scratch_shapes=list(scratch),
        compiler_params=pltpu.CompilerParams(vmem_limit_bytes=mib * 2**20),
    )


def body(biomass, water, flow_blocks, neighbours, rain, growth_rate, observations, obs_precision, ancestors):
    part, cells = biomass.shape
    nb = cells // BLK
    members, tiles = lax.axis_size("particle"), lax.axis_size("tile")
    slots = members * part
    unroll = slots <= 16
    f32, bf16, i16 = jnp.float32, jnp.bfloat16, jnp.int16
    swap_a = [(i, i ^ 1) for i in range(tiles)]
    swap_b = [(i, (i - 1) % tiles if i % 2 == 0 else (i + 1) % tiles) for i in range(tiles)]
    pairs, quads = nb // 2, nb // 4
    rows = 4 * part

    wire, later, growth, prec, obs, anc, rain23 = call(
        pack_kernel,
        [
            ((rows, (pairs + quads + 1) * BLK), i16),
            ((rows, (quads + 1) * BLK), i16),
            ((nb, BLK), f32),
            ((nb, BLK), f32),
            (observations.shape, f32),
            (ancestors.shape, jnp.int32),
            ((2, part, cells), f32),
        ],
        [HBM] * 7,
        [
            pltpu.VMEM((4, part, cells), f32),
            pltpu.VMEM((rows, (pairs + quads) * BLK), f32),
            pltpu.VMEM((rows, quads * BLK), f32),
            pltpu.VMEM((5, rows, BLK), f32),
            pltpu.SemaphoreType.DMA((9,)),
        ],
    )(biomass, water, rain, growth_rate.reshape(nb, BLK), obs_precision.reshape(nb, BLK), observations, ancestors)

    def gathered(x):
        return [x] + [lax.ppermute(x, "particle", [(i, i ^ j) for i in range(members)]) for j in range(1, members)]

    pieces = gathered(wire)
    pieces1 = gathered(later)
    depth = NBR * BLK
    edge = ((HALO * depth + 16, BLK), bf16)
    flow, flow_a, flow_b = call(
        flow_kernel,
        [((nb, depth, BLK), bf16), edge, edge],
        [HBM, HBM, SMEM],
        [pltpu.VMEM((nb, NBR, BLK, BLK), bf16), pltpu.SemaphoreType.DMA((4,))],
    )(wire, flow_blocks, neighbours)
    flow_a = lax.ppermute(flow_a, "tile", swap_a)
    flow_b = lax.ppermute(flow_b, "tile", swap_b)

    field = ((nb, slots, BLK), f32)
    wb, v0, b1, bq, wq, miss, quad, pay_a, pay_b = call(
        functools.partial(open_kernel, members, unroll),
        [((nb, slots, BLK), bf16), field, field, field, field, ((slots, BLK), f32), ((4 * slots, members * rows * 2), bf16)]
        + [((WIDE + 2 * HALO, slots, BLK), bf16)] * 2,
        [VMEM] * (members + 4),
        [
            pltpu.VMEM((8 * slots, members * rows * 2), bf16),
            pltpu.VMEM((5 * slots, members * rows * 2), bf16),
        ],
    )(*pieces, anc, growth, prec, obs)
    got_a = lax.ppermute(pay_a, "tile", swap_a)
    got_b = lax.ppermute(pay_b, "tile", swap_b)
    wb1, v1, b2, total = call(
        functools.partial(day0_kernel, unroll),
        [((nb + WIDE, slots, BLK), bf16), field, field, ((2 * slots, BLK), f32)],
        [VMEM] * 8 + [SMEM] + [VMEM] * 4,
        [pltpu.VMEM((nb + 2 * WIDE, slots, BLK), bf16)],
    )(wb, v0, b1, got_a, got_b, flow, flow_a, flow_b, neighbours, growth, prec, obs, miss)
    few = ((nb, part, BLK), f32)
    w2, ws, bs, v2, end_a, end_b = call(
        functools.partial(day1_kernel, members, unroll),
        [field, few, few, few] + [((WIDE + HALO, part, BLK), f32)] * 2,
        [VMEM] * (members + 5) + [SMEM] * 2 + [VMEM],
    )(*pieces1, wb1, v1, b2, quad, flow, neighbours, ancestors, rain23)
    last_a = lax.ppermute(end_a, "tile", swap_a)
    last_b = lax.ppermute(end_b, "tile", swap_b)

    def shared(x, masks):
        return [x] + [lax.ppermute(x, "tile", [(i, i ^ m) for i in range(tiles)]) for m in masks]

    terms = shared(total, [1])
    span = 2
    while span < tiles:
        total = sum(terms[1:], terms[0])
        masks = [span] if span * 2 >= tiles else [span, 2 * span, 3 * span]
        terms = shared(total, masks)
        span *= 2 ** (len(masks) // 2 + 1)
    bio_out, wat_out = call(
        functools.partial(close_kernel, unroll),
        [((part, cells), f32)] * 2,
        [VMEM] * 8 + [SMEM] + [VMEM] * 2,
        [pltpu.VMEM((nb + 2 * WIDE, part, BLK), f32), pltpu.VMEM((nb + WIDE, part, BLK), f32)],
    )(ws, bs, v2, last_a, last_b, flow, flow_a, flow_b, neighbours, growth, rain23)
    (means,) = call(
        functools.partial(means_kernel, unroll, len(terms)), [((CYCLES, 2, cells), f32)], [VMEM] * (len(terms) + 4)
    )(*terms, bq, wq, b2, w2)
    return means, bio_out, wat_out


def solution(mesh):
    placed = (
        P("particle", "tile"),
        P("particle", "tile"),
        P("tile", None, None, None),
        P("tile", None),
        P(None, "particle", "tile"),
        P("tile"),
        P(None, "tile"),
        P("tile"),
        P(),
    )
    return jax.shard_map(
        body,
        mesh=mesh,
        in_specs=placed,
        out_specs=(P(None, None, "tile"), P("particle", "tile"), P("particle", "tile")),
        check_vma=False,
    )
```

```python
import functools

import jax
import jax.numpy as jnp
from jax import lax
from jax.experimental import pallas as pl
from jax.experimental.pallas import tpu as pltpu
from jax.sharding import PartitionSpec as P

BLK = 128
CYCLES = 2
HALO = 4
WIDE = 2 * HALO
NBR = 3
BOUNDS = (2.0, 5.0, 4.0)
SCALE_STEPS = 32000.0
STEPS = 32767.0
VMEM = pl.BlockSpec(memory_space=pltpu.VMEM)
SMEM = pl.BlockSpec(memory_space=pltpu.SMEM)
HBM = pl.BlockSpec(memory_space=pltpu.HBM)


def run(count, unroll, step, carry):
    if unroll:
        for n in range(count):
            carry = step(n, carry)
        return carry
    return lax.fori_loop(0, count, step, carry)


def lanes(n, at=0):
    if isinstance(n, int):
        return slice(at + n * BLK, at + (n + 1) * BLK)
    return pl.ds(pl.multiple_of(at + n * BLK, BLK), BLK)


def wetness(w):
    sq = w * w
    return sq / (1.0 + sq)


def flux_of(xs, flow):
    return jnp.dot(jnp.concatenate(xs, axis=1), flow, preferred_element_type=jnp.float32)


def right_first():
    return lax.rem(lax.axis_index("tile"), 2) == 0


def pack_kernel(
    bio, wat, rain, left, right, ids, wire, pay_a, pay_b, held, factor
):
    part, cells = bio.shape
    nb = cells // BLK
    half, quarter = cells // 2, cells // 4
    codes = []
    for f, field in enumerate((bio, wat, rain.at[0], rain.at[1])):
        big = jnp.abs(field[:, 0:BLK])
        for n in range(1, nb):
            big = jnp.maximum(big, jnp.abs(field[:, lanes(n)]))
        unit = BOUNDS[min(f, 2)] / SCALE_STEPS
        code = jnp.floor(jnp.max(big, axis=1, keepdims=True) / unit) + 1.0
        inv = jnp.broadcast_to(STEPS / (code * unit), (part, BLK))
        codes.append(jnp.broadcast_to(code, (part, BLK)))
        if f < 2:
            for h in range(2):
                row = (2 * h + f) * part
                held[row : row + part, 0:half] = field[:, h * half : (h + 1) * half]
                factor[0, row : row + part, :] = inv
        else:
            at = f * quarter
            for q in range(4):
                held[q * part : (q + 1) * part, at : at + quarter] = field[:, q * quarter : (q + 1) * quarter]
                factor[f - 1, q * part : (q + 1) * part, :] = inv
    for f in range(4):
        factor[3, f * part : (f + 1) * part, :] = codes[f]

    def coded(x):
        return jnp.round(x).astype(jnp.int32).astype(jnp.int16)

    pairs, quads = nb // 2, nb // 4
    for n in range(nb):
        wire[:, lanes(n)] = coded(held[:, lanes(n)] * factor[0 if n < pairs else 1 if n < pairs + quads else 2])
    wire[:, lanes(nb)] = coded(factor[3])
    even = right_first()
    pos = lax.axis_index("tile")
    line = lax.broadcasted_iota(jnp.int32, (16, BLK), 0)

    def edge(pay, block, start):
        away = jnp.zeros((16, BLK), jnp.float32)
        for m in range(HALO):
            n = start + m + pos * nb
            for k in range(NBR):
                at = (m * NBR + k) * BLK
                pay[at : at + BLK, :] = block[m, k]
            for k, gap in enumerate((n - ids[1, start + m], ids[2, start + m] - n)):
                away = jnp.where(line == 2 * m + k, gap.astype(jnp.float32), away)
        at = HALO * NBR * BLK
        pay[at : at + 16, :] = away.astype(jnp.bfloat16)

    @pl.when(even)
    def _():
        edge(pay_a, right, nb - HALO)
        edge(pay_b, left, 0)

    @pl.when(jnp.logical_not(even))
    def _():
        edge(pay_a, left, 0)
        edge(pay_b, right, nb - HALO)


def stage_kernel(after, flow, wire, growth, prec, obs, anc, rain, turned, *held):
    for src, dst in zip((wire, growth, prec, obs, anc), held):
        dst[...] = src[...]
    held[-1][...] = rain[2:4]
    for n in range(flow.shape[0]):
        for k in range(NBR):
            turned[n, k * BLK : (k + 1) * BLK, :] = flow[n, k].T


def halo_flux(ext, pay, right, nb, m):
    depth = NBR * BLK
    away = pay[HALO * depth : HALO * depth + 16, :].astype(jnp.float32)
    at = jnp.where(right, nb + WIDE + m, HALO + m)
    xs = [ext[at].astype(jnp.bfloat16)]
    for k, sign in enumerate((-1, 1)):
        gap = jnp.broadcast_to(away[2 * m + k : 2 * m + k + 1, :], ext.shape[1:])
        x = jnp.zeros(ext.shape[1:], jnp.float32)
        for d in range(HALO + 1):
            x = jnp.where(gap == d, ext[at + sign * d].astype(jnp.float32), x)
        xs.append(x.astype(jnp.bfloat16))
    total = jnp.zeros(ext.shape[1:], jnp.float32)
    for k, x in enumerate(xs):
        at = m * depth + k * BLK
        total += lax.dot_general(
            x, pay[at : at + BLK, :], (((1,), (1,)), ((), ())), preferred_element_type=jnp.float32
        )
    return total


def decode(sel, pieces, cols):
    parts = []
    for ref in pieces:
        q = ref[:, cols].astype(jnp.int32)
        parts.append((q >> 8).astype(jnp.float32).astype(jnp.bfloat16))
        parts.append((q & 255).astype(jnp.float32).astype(jnp.bfloat16))
    return jnp.dot(sel, jnp.concatenate(parts, axis=0), preferred_element_type=jnp.float32)


def open_kernel(members, unroll, *refs):
    pieces = refs[:members]
    anc, growth, prec, obs = refs[members : members + 4]
    wb, v0, b1, bq, wq, miss, quad, unit1, pay_a, pay_b = refs[members + 4 : members + 14]
    pair, scaler = refs[-2:]
    nb = growth.shape[0]
    slots = anc.shape[1]
    rows = pieces[0].shape[0]
    part = rows // 4
    depth = members * rows * 2
    me = lax.axis_index("particle")
    line = lax.broadcasted_iota(jnp.int32, (slots, slots), 0)
    lane = lax.broadcasted_iota(jnp.int32, (slots, slots), 1)
    first = jnp.broadcast_to(anc[0:1, :], (slots, slots)).astype(jnp.float32)
    chosen = jnp.sum(jnp.where(line == lane, first, 0.0), axis=1, keepdims=True)
    own = lax.broadcasted_iota(jnp.int32, (slots, 1), 0).astype(jnp.float32)
    col = lax.broadcasted_iota(jnp.int32, (slots, depth), 1)
    value = jnp.where((col // rows) % 2 == 0, 256.0, 1.0)
    group = (col % rows) // part
    source = (((col // (2 * rows)) ^ me) * part + col % part).astype(jnp.float32)

    def hits(g, want):
        return jnp.where(jnp.logical_and(group == g, source == want), value, 0.0).astype(jnp.bfloat16)

    for h in range(2):
        for i, want in enumerate((chosen, chosen, own, own)):
            at = (4 * h + i) * slots
            pair[at : at + slots, :] = hits(2 * h + i % 2, want)
    for g in range(4):
        quad[g * slots : (g + 1) * slots, :] = hits(g, own)
    for i, (g, want) in enumerate(((0, chosen), (1, chosen), (0, own), (1, own), (2, own), (3, own))):
        scaler[i * slots : (i + 1) * slots, :] = hits(g, want)

    pairs, quads = nb // 2, nb // 4
    codes = decode(scaler[...], pieces, lanes(nb))
    scale = [
        codes[i * slots : (i + 1) * slots] * (BOUNDS[f] / SCALE_STEPS / STEPS) for i, f in enumerate((0, 1, 0, 1, 2, 2))
    ]
    unit1[...] = scale[5]

    def step(m, acc):
        wet = decode(quad[...], pieces, lanes(m, pairs * BLK))
        for p in range(2):
            got = decode(pair[...], pieces, lanes(m + p * quads))
            for h in range(2):
                q = 2 * h + p
                n = m + q * quads
                b, w, bi, wi = (got[(4 * h + i) * slots : (4 * h + i + 1) * slots] * scale[i] for i in range(4))
                rain0 = wet[q * slots : (q + 1) * slots] * scale[4]
                s = wetness(w)
                row = pl.ds(n, 1)
                wb[n] = w.astype(jnp.bfloat16)
                v0[n] = w + rain0 - 0.2 * b * s
                b1[n] = b + growth[row, :] * b * (s - 0.4 * b)
                bq[n] = bi
                wq[n] = wi
                off = bi - obs[0:1, lanes(n)]
                acc = acc + prec[row, :] * (off * off)
        return acc

    miss[...] = run(quads, unroll, step, jnp.zeros((slots, BLK), jnp.float32))
    even = right_first()
    for pay, right in ((pay_a, even), (pay_b, jnp.logical_not(even))):
        pay[0:WIDE] = wb[pl.ds(jnp.where(right, nb - WIDE, 0), WIDE)]
        edge = v0[pl.ds(jnp.where(right, nb - HALO, 0), HALO)]
        top = edge.astype(jnp.bfloat16)
        pay[WIDE : WIDE + HALO] = top
        pay[WIDE + HALO : WIDE + 2 * HALO] = (edge - top.astype(jnp.float32)).astype(jnp.bfloat16)


def day0_kernel(
    unroll, wb, v0, b1, got_a, got_b, flow, flow_a, flow_b, ids, growth, prec, obs, miss,
    wb1, v1, b2, total, ext,
):
    nb = growth.shape[0]
    slots = wb.shape[1]
    pos = lax.axis_index("tile")
    even = right_first()
    ext[WIDE : WIDE + nb] = wb[...]
    sides = ((got_a, flow_a, even), (got_b, flow_b, jnp.logical_not(even)))
    for got, _, right in sides:
        ext[pl.ds(jnp.where(right, nb + WIDE, 0), WIDE)] = got[0:WIDE]
    base = WIDE - pos * nb

    def step(n, acc):
        w = v0[n] + flux_of((ext[n + WIDE], ext[ids[1, n] + base], ext[ids[2, n] + base]), flow[n])
        wb1[n + HALO] = w.astype(jnp.bfloat16)
        s = wetness(w)
        row = pl.ds(n, 1)
        b = b1[n]
        v1[n] = w - 0.2 * b * s
        b = b + growth[row, :] * b * (s - 0.4 * b)
        b2[n] = b
        off = b - obs[1:2, lanes(n)]
        return acc + prec[row, :] * (off * off)

    total[0:slots, :] = miss[...]
    total[slots : 2 * slots, :] = run(nb, unroll, step, jnp.zeros((slots, BLK), jnp.float32))
    for got, pay, right in sides:
        spot = jnp.where(right, nb + HALO, 0)
        for m in range(HALO):
            edge = got[WIDE + m].astype(jnp.float32) + got[WIDE + HALO + m].astype(jnp.float32)
            wb1[spot + m] = (edge + halo_flux(ext, pay, right, nb, m)).astype(jnp.bfloat16)


def day1_kernel(members, unroll, *refs):
    pieces = refs[:members]
    wb1, v1, b2, quad, unit1, flow, ids, anc, rain, w2, ws, bs, v2, pay_a, pay_b = refs[members:]
    nb, slots = v1.shape[:2]
    part = rain.shape[1]
    pos = lax.axis_index("tile")
    me = lax.axis_index("particle")
    even = right_first()
    base = HALO - pos * nb
    picks = [anc[1, me * part + i] for i in range(part)]
    quads = nb // 4
    scale = unit1[...]

    def step(m, carry):
        wet = decode(quad[...], pieces, lanes(m, 3 * quads * BLK))
        for q in range(4):
            n = m + q * quads
            flux = flux_of((wb1[n + HALO], wb1[ids[1, n] + base], wb1[ids[2, n] + base]), flow[n])
            w2[n] = v1[n] + flux + wet[q * slots : (q + 1) * slots] * scale
        return carry

    run(quads, unroll, step, 0)

    def pick(n, carry):
        for i in range(part):
            ws[n, i : i + 1, :] = w2[n, pl.ds(picks[i], 1), :]
            bs[n, i : i + 1, :] = b2[n, pl.ds(picks[i], 1), :]
        w = ws[n]
        v2[n] = w + rain[0, :, lanes(n)] - 0.2 * bs[n] * wetness(w)
        return carry

    run(nb, unroll, pick, 0)
    for pay, right in ((pay_a, even), (pay_b, jnp.logical_not(even))):
        pay[0:WIDE] = ws[pl.ds(jnp.where(right, nb - WIDE, 0), WIDE)]
        pay[WIDE : WIDE + HALO] = v2[pl.ds(jnp.where(right, nb - HALO, 0), HALO)]


def close_kernel(
    unroll, ws, bs, v2, got_a, got_b, flow, flow_a, flow_b, ids, growth, rain, bio_out, wat_out, ext, ext3
):
    nb = growth.shape[0]
    pos = lax.axis_index("tile")
    even = right_first()
    half = jnp.bfloat16
    ext[WIDE : WIDE + nb] = ws[...]
    sides = ((got_a, flow_a, even), (got_b, flow_b, jnp.logical_not(even)))
    for got, _, right in sides:
        ext[pl.ds(jnp.where(right, nb + WIDE, 0), WIDE)] = got[0:WIDE]
    for got, pay, right in sides:
        spot = jnp.where(right, nb + HALO, 0)
        for m in range(HALO):
            ext3[spot + m] = got[WIDE + m] + halo_flux(ext, pay, right, nb, m)

    def near(ref, n, at):
        base = at - pos * nb
        return [ref[i].astype(half) for i in (n + at, ids[1, n] + base, ids[2, n] + base)]

    def step2(n, carry):
        ext3[n + HALO] = v2[n] + flux_of(near(ext, n, WIDE), flow[n])
        return carry

    run(nb, unroll, step2, 0)

    def step3(n, carry):
        g = growth[pl.ds(n, 1), :]
        b = bs[n]
        b = b + g * b * (wetness(ws[n]) - 0.4 * b)
        w = ext3[n + HALO]
        s = wetness(w)
        wat_out[:, lanes(n)] = w + flux_of(near(ext3, n, HALO), flow[n]) + rain[1, :, lanes(n)] - 0.2 * b * s
        bio_out[:, lanes(n)] = b + g * b * (s - 0.4 * b)
        return carry

    run(nb, unroll, step3, 0)


def means_kernel(unroll, count, *refs):
    bq, wq, b2, w2, means = refs[count:]
    nb, slots = bq.shape[:2]
    level = [ref[...] for ref in refs[:count]]
    while len(level) > 1:
        level = [a + b for a, b in zip(level[::2], level[1::2])]
    lw = -0.5 * jnp.sum(level[0], axis=1, keepdims=True)
    weights = []
    for c in range(CYCLES):
        x = lw[c * slots : (c + 1) * slots]
        e = jnp.exp(x - jnp.max(x, axis=0, keepdims=True))
        weights.append(jnp.broadcast_to(e / jnp.sum(e, axis=0, keepdims=True), (slots, BLK)))

    def step(n, carry):
        for c, fields in enumerate(((bq, wq), (b2, w2))):
            for f, ref in enumerate(fields):
                means[c, f : f + 1, lanes(n)] = jnp.sum(weights[c] * ref[n], axis=0, keepdims=True)
        return carry

    run(nb, unroll, step, 0)


def weigh(flops):
    return pl.CostEstimate(flops=flops, bytes_accessed=1, transcendentals=0)


def call(kernel, out, specs, scratch=(), cost=1):
    return pl.pallas_call(
        kernel,
        out_shape=tuple(jax.ShapeDtypeStruct(s, d) for s, d in out),
        in_specs=specs,
        out_specs=tuple(VMEM for _ in out),
        scratch_shapes=list(scratch),
        compiler_params=pltpu.CompilerParams(vmem_limit_bytes=32 * 2**20),
        cost_estimate=weigh(cost),
    )


def body(biomass, water, flow_blocks, neighbours, rain, growth_rate, observations, obs_precision, ancestors):
    part, cells = biomass.shape
    nb = cells // BLK
    members, tiles = lax.axis_size("particle"), lax.axis_size("tile")
    slots = members * part
    unroll = slots <= 16
    f32, bf16, i16 = jnp.float32, jnp.bfloat16, jnp.int16
    swap_a = [(i, i ^ 1) for i in range(tiles)]
    swap_b = [(i, (i - 1) % tiles if i % 2 == 0 else (i + 1) % tiles) for i in range(tiles)]
    rows = 4 * part
    neighbours = neighbours.T

    depth = NBR * BLK
    edge = ((HALO * depth + 16, BLK), bf16)
    tile = (HALO, NBR, BLK, BLK)

    out = [((rows, (nb + 1) * BLK), i16), edge, edge]
    wire, flow_a, flow_b = pl.pallas_call(
        pack_kernel,
        grid=(1,),
        out_shape=tuple(jax.ShapeDtypeStruct(s, d) for s, d in out),
        in_specs=[pl.BlockSpec((part, cells), lambda i: (0, 0))] * 2
        + [pl.BlockSpec((2, part, cells), lambda i: (0, 0, 0))]
        + [pl.BlockSpec(tile, lambda i: (0, 0, 0, 0)), pl.BlockSpec(tile, lambda i: (nb // HALO - 1, 0, 0, 0)), SMEM],
        out_specs=tuple(VMEM for _ in out),
        scratch_shapes=[
            pltpu.VMEM((rows, cells), f32),
            pltpu.VMEM((4, rows, BLK), f32),
        ],
        compiler_params=pltpu.CompilerParams(vmem_limit_bytes=60 * 2**20),
        cost_estimate=weigh(1),
    )(biomass, water, rain, flow_blocks, flow_blocks, neighbours)

    pieces = [wire] + [
        lax.ppermute(wire, "particle", [(i, i ^ j) for i in range(members)]) for j in range(1, members)
    ]
    small = (wire, growth_rate.reshape(nb, BLK), obs_precision.reshape(nb, BLK), observations, ancestors)
    flow, pieces[0], growth, prec, obs, anc, rain23 = call(
        stage_kernel,
        [((nb, depth, BLK), bf16)] + [(x.shape, x.dtype) for x in small] + [((2, part, cells), f32)],
        [HBM] + [VMEM] * 7,
    )(pieces[1], flow_blocks, *small, rain)
    flow_a = lax.ppermute(flow_a, "tile", swap_a)
    flow_b = lax.ppermute(flow_b, "tile", swap_b)

    field = ((nb, slots, BLK), f32)
    wb, v0, b1, bq, wq, miss, quad, unit1, pay_a, pay_b = call(
        functools.partial(open_kernel, members, unroll),
        [((nb, slots, BLK), bf16), field, field, field, field, ((slots, BLK), f32), ((4 * slots, members * rows * 2), bf16), ((slots, BLK), f32)]
        + [((WIDE + 2 * HALO, slots, BLK), bf16)] * 2,
        [VMEM] * (members + 4),
        [
            pltpu.VMEM((8 * slots, members * rows * 2), bf16),
            pltpu.VMEM((6 * slots, members * rows * 2), bf16),
        ],
        cost=10**10,
    )(*pieces, anc, growth, prec, obs)
    got_a = lax.ppermute(pay_a, "tile", swap_a)
    got_b = lax.ppermute(pay_b, "tile", swap_b)
    wb1, v1, b2, total = call(
        functools.partial(day0_kernel, unroll),
        [((nb + WIDE, slots, BLK), bf16), field, field, ((2 * slots, BLK), f32)],
        [VMEM] * 8 + [SMEM] + [VMEM] * 4,
        [pltpu.VMEM((nb + 2 * WIDE, slots, BLK), bf16)],
    )(wb, v0, b1, got_a, got_b, flow, flow_a, flow_b, neighbours, growth, prec, obs, miss)
    few = ((nb, part, BLK), f32)
    w2, ws, bs, v2, end_a, end_b = call(
        functools.partial(day1_kernel, members, unroll),
        [field, few, few, few] + [((WIDE + HALO, part, BLK), f32)] * 2,
        [VMEM] * (members + 6) + [SMEM] * 2 + [VMEM],
    )(*pieces, wb1, v1, b2, quad, unit1, flow, neighbours, ancestors, rain23)
    last_a = lax.ppermute(end_a, "tile", swap_a)
    last_b = lax.ppermute(end_b, "tile", swap_b)

    def shared(x, masks):
        return [x] + [lax.ppermute(x, "tile", [(i, i ^ m) for i in range(tiles)]) for m in masks]

    terms = shared(total, [1])
    span = 2
    while span < tiles:
        total = sum(terms[1:], terms[0])
        masks = [span] if span * 2 >= tiles else [span, 2 * span, 3 * span]
        terms = shared(total, masks)
        span *= 2 ** (len(masks) // 2 + 1)
    bio_out, wat_out = call(
        functools.partial(close_kernel, unroll),
        [((part, cells), f32)] * 2,
        [VMEM] * 8 + [SMEM] + [VMEM] * 2,
        [pltpu.VMEM((nb + 2 * WIDE, part, BLK), f32), pltpu.VMEM((nb + WIDE, part, BLK), f32)],
    )(ws, bs, v2, last_a, last_b, flow, flow_a, flow_b, neighbours, growth, rain23)
    (means,) = call(
        functools.partial(means_kernel, unroll, len(terms)), [((CYCLES, 2, cells), f32)], [VMEM] * (len(terms) + 4)
    )(*terms, bq, wq, b2, w2)
    return means, bio_out, wat_out


def solution(mesh):
    placed = (
        P("particle", "tile"),
        P("particle", "tile"),
        P("tile", None, None, None),
        P("tile", None),
        P(None, "particle", "tile"),
        P("tile"),
        P(None, "tile"),
        P("tile"),
        P(),
    )
    return jax.shard_map(
        body,
        mesh=mesh,
        in_specs=placed,
        out_specs=(P(None, None, "tile"), P("particle", "tile"), P("particle", "tile")),
        check_vma=False,
    )
```

```python
import functools

import jax
import jax.numpy as jnp
from jax import lax
from jax.experimental import pallas as pl
from jax.experimental.pallas import tpu as pltpu
from jax.sharding import PartitionSpec as P

BLK = 128
CYCLES = 2
HALO = 4
WIDE = 2 * HALO
NBR = 3
BOUNDS = (2.0, 5.0, 4.0)
SCALE_STEPS = 32000.0
STEPS = 32767.0
VMEM = pl.BlockSpec(memory_space=pltpu.VMEM)
SMEM = pl.BlockSpec(memory_space=pltpu.SMEM)
HBM = pl.BlockSpec(memory_space=pltpu.HBM)


def run(first, last, unroll, step, carry):
    if unroll:
        for n in range(first, last):
            carry = step(n, carry)
        return carry
    return lax.fori_loop(first, last, step, carry)


def lanes(n, at=0):
    if isinstance(n, int):
        return slice(at + n * BLK, at + (n + 1) * BLK)
    return pl.ds(pl.multiple_of(at + n * BLK, BLK), BLK)


def wetness(w):
    sq = w * w
    return sq / (1.0 + sq)


def flux_of(xs, flow):
    return jnp.dot(jnp.concatenate(xs, axis=1), flow, preferred_element_type=jnp.float32)


def right_first():
    return lax.rem(lax.axis_index("tile"), 2) == 0


def pack_kernel(bio, wat, rain, wire, held, factor):
    part, cells = bio.shape
    nb = cells // BLK
    half, quarter = cells // 2, cells // 4
    codes = []
    for f, field in enumerate((bio, wat, rain.at[0], rain.at[1])):
        big = jnp.abs(field[:, 0:BLK])
        for n in range(1, nb):
            big = jnp.maximum(big, jnp.abs(field[:, lanes(n)]))
        unit = BOUNDS[min(f, 2)] / SCALE_STEPS
        code = jnp.floor(jnp.max(big, axis=1, keepdims=True) / unit) + 1.0
        inv = jnp.broadcast_to(STEPS / (code * unit), (part, BLK))
        codes.append(jnp.broadcast_to(code, (part, BLK)))
        if f < 2:
            for h in range(2):
                row = (2 * h + f) * part
                held[row : row + part, 0:half] = field[:, h * half : (h + 1) * half]
                factor[0, row : row + part, :] = inv
        else:
            at = f * quarter
            for q in range(4):
                held[q * part : (q + 1) * part, at : at + quarter] = field[:, q * quarter : (q + 1) * quarter]
                factor[f - 1, q * part : (q + 1) * part, :] = inv
    for f in range(4):
        factor[3, f * part : (f + 1) * part, :] = codes[f]

    def coded(x):
        return jnp.round(x).astype(jnp.int32).astype(jnp.int16)

    pairs, quads = nb // 2, nb // 4
    for n in range(nb):
        wire[:, lanes(n)] = coded(held[:, lanes(n)] * factor[0 if n < pairs else 1 if n < pairs + quads else 2])
    wire[:, lanes(nb)] = coded(factor[3])


def edge_kernel(after, left, right, ids, pay_a, pay_b):
    nb = ids.shape[1]
    even = right_first()
    pos = lax.axis_index("tile")
    line = lax.broadcasted_iota(jnp.int32, (16, BLK), 0)

    def edge(pay, block, start):
        away = jnp.zeros((16, BLK), jnp.float32)
        for m in range(HALO):
            n = start + m + pos * nb
            for k in range(NBR):
                at = (m * NBR + k) * BLK
                pay[at : at + BLK, :] = block[m, k]
            for k, gap in enumerate((n - ids[1, start + m], ids[2, start + m] - n)):
                away = jnp.where(line == 2 * m + k, gap.astype(jnp.float32), away)
        at = HALO * NBR * BLK
        pay[at : at + 16, :] = away.astype(jnp.bfloat16)

    @pl.when(even)
    def _():
        edge(pay_a, right, nb - HALO)
        edge(pay_b, left, 0)

    @pl.when(jnp.logical_not(even))
    def _():
        edge(pay_a, left, 0)
        edge(pay_b, right, nb - HALO)


def stage_kernel(after, flow, wire, growth, prec, obs, anc, rain, turned, *held):
    for src, dst in zip((wire, growth, prec, obs, anc), held):
        dst[...] = src[...]
    held[-1][...] = rain[2:4]
    for n in range(flow.shape[0]):
        for k in range(NBR):
            turned[n, k * BLK : (k + 1) * BLK, :] = flow[n, k].T


def halo_flux(ext, pay, right, nb, m):
    depth = NBR * BLK
    away = pay[HALO * depth : HALO * depth + 16, :].astype(jnp.float32)
    at = jnp.where(right, nb + WIDE + m, HALO + m)
    xs = [ext[at].astype(jnp.bfloat16)]
    for k, sign in enumerate((-1, 1)):
        gap = jnp.broadcast_to(away[2 * m + k : 2 * m + k + 1, :], ext.shape[1:])
        x = jnp.zeros(ext.shape[1:], jnp.float32)
        for d in range(HALO + 1):
            x = jnp.where(gap == d, ext[at + sign * d].astype(jnp.float32), x)
        xs.append(x.astype(jnp.bfloat16))
    total = jnp.zeros(ext.shape[1:], jnp.float32)
    for k, x in enumerate(xs):
        at = m * depth + k * BLK
        total += lax.dot_general(
            x, pay[at : at + BLK, :], (((1,), (1,)), ((), ())), preferred_element_type=jnp.float32
        )
    return total


def decode(sel, pieces, cols):
    parts = []
    for ref in pieces:
        q = ref[:, cols].astype(jnp.int32)
        parts.append((q >> 8).astype(jnp.float32).astype(jnp.bfloat16))
        parts.append((q & 255).astype(jnp.float32).astype(jnp.bfloat16))
    return jnp.dot(sel, jnp.concatenate(parts, axis=0), preferred_element_type=jnp.float32)


def open_kernel(members, unroll, *refs):
    pieces = refs[:members]
    anc, growth, prec, obs = refs[members : members + 4]
    wb, v0, b1, bq, wq, miss, quad, unit1, pay_a, pay_b = refs[members + 4 : members + 14]
    pair, scaler = refs[-2:]
    nb = growth.shape[0]
    slots = anc.shape[1]
    rows = pieces[0].shape[0]
    part = rows // 4
    depth = members * rows * 2
    me = lax.axis_index("particle")
    line = lax.broadcasted_iota(jnp.int32, (slots, slots), 0)
    lane = lax.broadcasted_iota(jnp.int32, (slots, slots), 1)
    first = jnp.broadcast_to(anc[0:1, :], (slots, slots)).astype(jnp.float32)
    chosen = jnp.sum(jnp.where(line == lane, first, 0.0), axis=1, keepdims=True)
    own = lax.broadcasted_iota(jnp.int32, (slots, 1), 0).astype(jnp.float32)
    col = lax.broadcasted_iota(jnp.int32, (slots, depth), 1)
    value = jnp.where((col // rows) % 2 == 0, 256.0, 1.0)
    group = (col % rows) // part
    source = (((col // (2 * rows)) ^ me) * part + col % part).astype(jnp.float32)

    def hits(g, want):
        return jnp.where(jnp.logical_and(group == g, source == want), value, 0.0).astype(jnp.bfloat16)

    for h in range(2):
        for i, want in enumerate((chosen, chosen, own, own)):
            at = (4 * h + i) * slots
            pair[at : at + slots, :] = hits(2 * h + i % 2, want)
    for g in range(4):
        quad[g * slots : (g + 1) * slots, :] = hits(g, own)
    for i, (g, want) in enumerate(((0, chosen), (1, chosen), (0, own), (1, own), (2, own), (3, own))):
        scaler[i * slots : (i + 1) * slots, :] = hits(g, want)

    pairs, quads = nb // 2, nb // 4
    codes = decode(scaler[...], pieces, lanes(nb))
    scale = [
        codes[i * slots : (i + 1) * slots] * (BOUNDS[f] / SCALE_STEPS / STEPS) for i, f in enumerate((0, 1, 0, 1, 2, 2))
    ]
    unit1[...] = scale[5]

    def step(m, acc):
        wet = decode(quad[...], pieces, lanes(m, pairs * BLK))
        for p in range(2):
            got = decode(pair[...], pieces, lanes(m + p * quads))
            for h in range(2):
                q = 2 * h + p
                n = m + q * quads
                b, w, bi, wi = (got[(4 * h + i) * slots : (4 * h + i + 1) * slots] * scale[i] for i in range(4))
                rain0 = wet[q * slots : (q + 1) * slots] * scale[4]
                s = wetness(w)
                row = pl.ds(n, 1)
                wb[n] = w.astype(jnp.bfloat16)
                v0[n] = w + rain0 - 0.2 * b * s
                b1[n] = b + growth[row, :] * b * (s - 0.4 * b)
                bq[n] = bi
                wq[n] = wi
                off = bi - obs[0:1, lanes(n)]
                acc = acc + prec[row, :] * (off * off)
        return acc

    miss[...] = run(0, quads, unroll, step, jnp.zeros((slots, BLK), jnp.float32))
    even = right_first()
    for pay, right in ((pay_a, even), (pay_b, jnp.logical_not(even))):
        pay[0:WIDE] = wb[pl.ds(jnp.where(right, nb - WIDE, 0), WIDE)]
        edge = v0[pl.ds(jnp.where(right, nb - HALO, 0), HALO)]
        top = edge.astype(jnp.bfloat16)
        pay[WIDE : WIDE + HALO] = top
        pay[WIDE + HALO : WIDE + 2 * HALO] = (edge - top.astype(jnp.float32)).astype(jnp.bfloat16)


def inner01_kernel(members, unroll, *refs):
    pieces = refs[:members]
    wb, v0, b1, quad, unit1, flow, ids, growth, prec, obs, anc, rain = refs[members : members + 12]
    r1, wb1, v1, b2, w2, ws, bs, v2, miss = refs[members + 12 :]
    nb, slots = wb.shape[:2]
    part = rain.shape[1]
    quads = nb // 4
    scale = unit1[...]
    base = lax.axis_index("tile") * nb

    def wet_day(m, carry):
        got = decode(quad[...], pieces, lanes(m, 3 * quads * BLK))
        for q in range(4):
            r1[m + q * quads] = got[q * slots : (q + 1) * slots] * scale
        return carry

    run(0, quads, unroll, wet_day, 0)

    def day0(n, acc):
        w = v0[n] + flux_of((wb[n], wb[ids[1, n] - base], wb[ids[2, n] - base]), flow[n])
        wb1[n - HALO] = w.astype(jnp.bfloat16)
        b, v, acc = settle(n, w, b1, r1, growth, prec, obs, acc)
        b2[n - HALO] = b
        v1[n - HALO] = v
        return acc

    miss[...] = run(HALO, nb - HALO, unroll, day0, jnp.zeros((slots, BLK), jnp.float32))
    base = base + HALO

    def day1(n, carry):
        w2[n - WIDE] = v1[n - HALO] + flux_of((wb1[n - HALO], wb1[ids[1, n] - base], wb1[ids[2, n] - base]), flow[n])
        return carry

    run(WIDE, nb - WIDE, unroll, day1, 0)
    picks = ancestors_of(anc, part)

    def pick(n, carry):
        m = n - WIDE
        choose(picks, w2.at[m], b2.at[n - HALO], rain[0, :, lanes(n)], ws.at[m], bs.at[m], v2.at[m])
        return carry

    run(WIDE, nb - WIDE, unroll, pick, 0)


def settle(n, w, b1, r1, growth, prec, obs, acc):
    s = wetness(w)
    row = pl.ds(n, 1)
    b = b1[n]
    v = w + r1[n] - 0.2 * b * s
    b = b + growth[row, :] * b * (s - 0.4 * b)
    off = b - obs[1:2, lanes(n)]
    return b, v, acc + prec[row, :] * (off * off)


def ancestors_of(anc, part):
    return [anc[1, lax.axis_index("particle") * part + i] for i in range(part)]


def choose(picks, w2, b2, rain, ws, bs, v2):
    for i, p in enumerate(picks):
        ws[i : i + 1, :] = w2[pl.ds(p, 1), :]
        bs[i : i + 1, :] = b2[pl.ds(p, 1), :]
    w = ws[...]
    v2[...] = w + rain - 0.2 * bs[...] * wetness(w)


def outer01_kernel(
    unroll, wb, v0, b1, r1, wb1, v1, b2, wi, bi, vi, miss0, miss1, got_a, got_b, flow, flow_a, flow_b, ids,
    growth, prec, obs, anc, rain, b2_out, w2_out, ws, bs, v2, total, pay_a, pay_b, ext, ext1, v1_out,
):
    nb, slots = wb.shape[:2]
    part = rain.shape[1]
    pos = lax.axis_index("tile")
    even = right_first()
    lows, highs = (0, WIDE + HALO), (nb - WIDE - HALO, nb)
    for lo, hi in (lows, highs):
        ext[WIDE + lo : WIDE + hi] = wb[lo:hi]
    ext1[WIDE : 2 * WIDE] = wb1[0:WIDE]
    ext1[nb - WIDE : nb] = wb1[nb - 2 * HALO - WIDE : nb - 2 * HALO]
    sides = ((got_a, flow_a, even), (got_b, flow_b, jnp.logical_not(even)))
    for got, _, right in sides:
        ext[pl.ds(jnp.where(right, nb + WIDE, 0), WIDE)] = got[0:WIDE]
    base = WIDE - pos * nb

    def day0(n, acc):
        w = v0[n] + flux_of((ext[n + WIDE], ext[ids[1, n] + base], ext[ids[2, n] + base]), flow[n])
        ext1[n + HALO] = w.astype(jnp.bfloat16)
        b, v, acc = settle(n, w, b1, r1, growth, prec, obs, acc)
        m = n if n < HALO else n - (nb - 2 * HALO)
        b2_out[m] = b
        v1_out[m] = v
        return acc

    acc = miss1[...]
    for n in (*range(HALO), *range(nb - HALO, nb)):
        acc = day0(n, acc)
    total[0:slots, :] = miss0[...]
    total[slots : 2 * slots, :] = acc
    for got, pay, right in sides:
        spot = jnp.where(right, nb + HALO, 0)
        for m in range(HALO):
            edge = got[WIDE + m].astype(jnp.float32) + got[WIDE + HALO + m].astype(jnp.float32)
            ext1[spot + m] = (edge + halo_flux(ext, pay, right, nb, m)).astype(jnp.bfloat16)
    base = HALO - pos * nb
    picks = ancestors_of(anc, part)
    ws[WIDE : nb - WIDE] = wi[...]
    bs[WIDE : nb - WIDE] = bi[...]
    v2[WIDE : nb - WIDE] = vi[...]
    for n in (*range(WIDE), *range(nb - WIDE, nb)):
        m = n if n < WIDE else n - (nb - 2 * WIDE)
        if n < HALO or n >= nb - HALO:
            at = n if n < HALO else n - (nb - 2 * HALO)
            v, b = v1_out[at], b2_out.at[at]
        else:
            v, b = v1[n - HALO], b2.at[n - HALO]
        w2_out[m] = v + flux_of((ext1[n + HALO], ext1[ids[1, n] + base], ext1[ids[2, n] + base]), flow[n])
        choose(picks, w2_out.at[m], b, rain[0, :, lanes(n)], ws.at[n], bs.at[n], v2.at[n])
    for pay, right in ((pay_a, even), (pay_b, jnp.logical_not(even))):
        for m in range(WIDE):
            pay[m * part : (m + 1) * part, :] = ws[jnp.where(right, nb - WIDE, 0) + m]
        for m in range(HALO):
            pay[(WIDE + m) * part : (WIDE + m + 1) * part, :] = v2[jnp.where(right, nb - HALO, 0) + m]
    at = (WIDE + HALO) * part
    pay_a[at : at + 2 * slots, :] = total[...]


def inner23_kernel(unroll, ws, bs, v2, flow, ids, growth, rain, w3, wat, bio):
    nb = ws.shape[0]
    base = lax.axis_index("tile") * nb
    half = jnp.bfloat16

    def day2(n, carry):
        xs = [ws[i].astype(half) for i in (n, ids[1, n] - base, ids[2, n] - base)]
        w3[n - HALO] = v2[n] + flux_of(xs, flow[n])
        return carry

    run(HALO, nb - HALO, unroll, day2, 0)

    def day3(n, carry):
        xs = [w3[i - HALO].astype(half) for i in (n, ids[1, n] - base, ids[2, n] - base)]
        m = n - WIDE
        wat[m], bio[m] = final(n, w3[n - HALO], flux_of(xs, flow[n]), ws[n], bs[n], growth, rain)
        return carry

    run(WIDE, nb - WIDE, unroll, day3, 0)


def final(n, w3, flux, w, b, growth, rain):
    g = growth[pl.ds(n, 1), :]
    b = b + g * b * (wetness(w) - 0.4 * b)
    s = wetness(w3)
    return w3 + flux + rain[1, :, lanes(n)] - 0.2 * b * s, b + g * b * (s - 0.4 * b)


def outer23_kernel(
    ws, bs, v2, w3, wat, bio, got_a, got_b, flow, flow_a, flow_b, ids, growth, rain,
    bio_out, wat_out, ext, ext3,
):
    nb, part = ws.shape[:2]
    pos = lax.axis_index("tile")
    even = right_first()
    half = jnp.bfloat16
    for n in range(WIDE, nb - WIDE):
        wat_out[:, lanes(n)] = wat[n - WIDE]
        bio_out[:, lanes(n)] = bio[n - WIDE]
    for lo, hi in ((0, WIDE + HALO), (nb - WIDE - HALO, nb)):
        ext[WIDE + lo : WIDE + hi] = ws[lo:hi]
    ext3[WIDE : 2 * WIDE] = w3[0:WIDE]
    ext3[nb - WIDE : nb] = w3[nb - 2 * HALO - WIDE : nb - 2 * HALO]
    sides = ((got_a, flow_a, even), (got_b, flow_b, jnp.logical_not(even)))
    for got, _, right in sides:
        for m in range(WIDE):
            ext[jnp.where(right, nb + WIDE, 0) + m] = got[m * part : (m + 1) * part, :]
    base = WIDE - pos * nb
    for n in (*range(HALO), *range(nb - HALO, nb)):
        xs = [ext[i].astype(half) for i in (n + WIDE, ids[1, n] + base, ids[2, n] + base)]
        ext3[n + HALO] = v2[n] + flux_of(xs, flow[n])
    for got, pay, right in sides:
        spot = jnp.where(right, nb + HALO, 0)
        for m in range(HALO):
            edge = got[(WIDE + m) * part : (WIDE + m + 1) * part, :]
            ext3[spot + m] = edge + halo_flux(ext, pay, right, nb, m)
    base = HALO - pos * nb
    for n in (*range(WIDE), *range(nb - WIDE, nb)):
        xs = [ext3[i].astype(half) for i in (n + HALO, ids[1, n] + base, ids[2, n] + base)]
        w, b = final(n, ext3[n + HALO], flux_of(xs, flow[n]), ws[n], bs[n], growth, rain)
        wat_out[:, lanes(n)] = w
        bio_out[:, lanes(n)] = b


def means_kernel(unroll, count, *refs):
    bq, wq, b2, w2, b2_edge, w2_edge, means = refs[count:]
    nb, slots = bq.shape[:2]
    level = [ref[...] for ref in refs[:count]]
    while len(level) > 1:
        level = [a + b for a, b in zip(level[::2], level[1::2])]
    lw = -0.5 * jnp.sum(level[0], axis=1, keepdims=True)
    weights = []
    for c in range(CYCLES):
        x = lw[c * slots : (c + 1) * slots]
        e = jnp.exp(x - jnp.max(x, axis=0, keepdims=True))
        weights.append(jnp.broadcast_to(e / jnp.sum(e, axis=0, keepdims=True), (slots, BLK)))

    def mean(c, f, n, x):
        means[c, f : f + 1, lanes(n)] = jnp.sum(weights[c] * x, axis=0, keepdims=True)

    def fill(c, f, ref, first, last, shift):
        def step(n, carry):
            mean(c, f, n, ref[n - shift])
            return carry

        run(first, last, unroll, step, 0)

    fill(0, 0, bq, 0, nb, 0)
    fill(0, 1, wq, 0, nb, 0)
    for f, ref, edge, width in ((0, b2, b2_edge, HALO), (1, w2, w2_edge, WIDE)):
        fill(1, f, ref, width, nb - width, width)
        fill(1, f, edge, 0, width, 0)
        fill(1, f, edge, nb - width, nb, nb - 2 * width)


def weigh(flops):
    return pl.CostEstimate(flops=flops, bytes_accessed=1, transcendentals=0)


def call(kernel, out, specs, scratch=(), cost=1):
    return pl.pallas_call(
        kernel,
        out_shape=tuple(jax.ShapeDtypeStruct(s, d) for s, d in out),
        in_specs=specs,
        out_specs=tuple(VMEM for _ in out),
        scratch_shapes=list(scratch),
        compiler_params=pltpu.CompilerParams(vmem_limit_bytes=32 * 2**20),
        cost_estimate=weigh(cost),
    )


def body(biomass, water, flow_blocks, neighbours, rain, growth_rate, observations, obs_precision, ancestors):
    part, cells = biomass.shape
    nb = cells // BLK
    members, tiles = lax.axis_size("particle"), lax.axis_size("tile")
    slots = members * part
    unroll = slots <= 16
    f32, bf16, i16 = jnp.float32, jnp.bfloat16, jnp.int16
    swap_a = [(i, i ^ 1) for i in range(tiles)]
    swap_b = [(i, (i - 1) % tiles if i % 2 == 0 else (i + 1) % tiles) for i in range(tiles)]
    rows = 4 * part
    neighbours = neighbours.T

    depth = NBR * BLK
    edge = ((HALO * depth + 16, BLK), bf16)
    tile = (HALO, NBR, BLK, BLK)

    wire = pl.pallas_call(
        pack_kernel,
        grid=(1,),
        out_shape=jax.ShapeDtypeStruct((rows, (nb + 1) * BLK), i16),
        in_specs=[pl.BlockSpec((part, cells), lambda i: (0, 0))] * 2
        + [pl.BlockSpec((2, part, cells), lambda i: (0, 0, 0))],
        out_specs=VMEM,
        scratch_shapes=[pltpu.VMEM((rows, cells), f32), pltpu.VMEM((4, rows, BLK), f32)],
        compiler_params=pltpu.CompilerParams(vmem_limit_bytes=60 * 2**20),
        cost_estimate=weigh(1),
    )(biomass, water, rain)
    flow_a, flow_b = pl.pallas_call(
        edge_kernel,
        grid=(1,),
        out_shape=tuple(jax.ShapeDtypeStruct(*edge) for _ in range(2)),
        in_specs=[
            HBM,
            pl.BlockSpec(tile, lambda i: (0, 0, 0, 0)),
            pl.BlockSpec(tile, lambda i: (nb // HALO - 1, 0, 0, 0)),
            SMEM,
        ],
        out_specs=(VMEM, VMEM),
        compiler_params=pltpu.CompilerParams(vmem_limit_bytes=60 * 2**20),
        cost_estimate=weigh(1),
    )(wire, flow_blocks, flow_blocks, neighbours)

    pieces = [wire] + [
        lax.ppermute(wire, "particle", [(i, i ^ j) for i in range(members)]) for j in range(1, members)
    ]
    small = (wire, growth_rate.reshape(nb, BLK), obs_precision.reshape(nb, BLK), observations, ancestors)
    flow, pieces[0], growth, prec, obs, anc, rain23 = call(
        stage_kernel,
        [((nb, depth, BLK), bf16)] + [(x.shape, x.dtype) for x in small] + [((2, part, cells), f32)],
        [HBM] + [VMEM] * 7,
    )(pieces[1], flow_blocks, *small, rain)
    flow_a = lax.ppermute(flow_a, "tile", swap_a)
    flow_b = lax.ppermute(flow_b, "tile", swap_b)

    field = ((nb, slots, BLK), f32)
    wb, v0, b1, bq, wq, miss, quad, unit1, pay_a, pay_b = call(
        functools.partial(open_kernel, members, unroll),
        [((nb, slots, BLK), bf16), field, field, field, field, ((slots, BLK), f32), ((4 * slots, members * rows * 2), bf16), ((slots, BLK), f32)]
        + [((WIDE + 2 * HALO, slots, BLK), bf16)] * 2,
        [VMEM] * (members + 4),
        [
            pltpu.VMEM((8 * slots, members * rows * 2), bf16),
            pltpu.VMEM((6 * slots, members * rows * 2), bf16),
        ],
        cost=10**10,
    )(*pieces, anc, growth, prec, obs)
    got_a = lax.ppermute(pay_a, "tile", swap_a)
    got_b = lax.ppermute(pay_b, "tile", swap_b)
    inner, core = nb - 2 * HALO, nb - 2 * WIDE

    def blocks(count, height=slots, kind=f32):
        return ((count, height, BLK), kind)

    r1, wb1, v1, b2, w2, wi, bi, vi, miss1 = call(
        functools.partial(inner01_kernel, members, unroll),
        [blocks(nb), blocks(inner, kind=bf16), blocks(inner), blocks(inner), blocks(core)]
        + [blocks(core, part)] * 3
        + [((slots, BLK), f32)],
        [VMEM] * (members + 6) + [SMEM] + [VMEM] * 3 + [SMEM, VMEM],
    )(*pieces, wb, v0, b1, quad, unit1, flow, neighbours, growth, prec, obs, ancestors, rain23)
    swap_rows = (WIDE + HALO) * part
    b2_edge, w2_edge, ws, bs, v2, total, end_a, end_b = call(
        functools.partial(outer01_kernel, unroll),
        [blocks(2 * HALO), blocks(2 * WIDE)]
        + [blocks(nb, part)] * 3
        + [((2 * slots, BLK), f32), ((swap_rows + 2 * slots, BLK), f32), ((swap_rows, BLK), f32)],
        [VMEM] * 17 + [SMEM] + [VMEM] * 3 + [SMEM, VMEM],
        [
            pltpu.VMEM((nb + 2 * WIDE, slots, BLK), bf16),
            pltpu.VMEM((nb + WIDE, slots, BLK), bf16),
            pltpu.VMEM((2 * HALO, slots, BLK), f32),
        ],
    )(
        wb, v0, b1, r1, wb1, v1, b2, wi, bi, vi, miss, miss1, got_a, got_b, flow, flow_a, flow_b, neighbours,
        growth, prec, obs, ancestors, rain23,
    )
    last_a = lax.ppermute(end_a, "tile", swap_a)
    last_b = lax.ppermute(end_b, "tile", swap_b)

    terms = [total, last_a[swap_rows:]]
    span = 2
    while span < tiles:
        total = sum(terms[1:], terms[0])
        masks = [span] if span * 2 >= tiles else [span, 2 * span, 3 * span]
        terms = [total] + [lax.ppermute(total, "tile", [(i, i ^ m) for i in range(tiles)]) for m in masks]
        span *= 2 ** (len(masks) // 2 + 1)
    w3, wat, bio = call(
        functools.partial(inner23_kernel, unroll),
        [blocks(inner, part), blocks(core, part), blocks(core, part)],
        [VMEM] * 4 + [SMEM] + [VMEM] * 2,
    )(ws, bs, v2, flow, neighbours, growth, rain23)
    bio_out, wat_out = call(
        outer23_kernel,
        [((part, cells), f32)] * 2,
        [VMEM] * 11 + [SMEM] + [VMEM] * 2,
        [pltpu.VMEM((nb + 2 * WIDE, part, BLK), f32), pltpu.VMEM((nb + WIDE, part, BLK), f32)],
    )(ws, bs, v2, w3, wat, bio, last_a, last_b, flow, flow_a, flow_b, neighbours, growth, rain23)
    (means,) = call(
        functools.partial(means_kernel, unroll, len(terms)), [((CYCLES, 2, cells), f32)], [VMEM] * (len(terms) + 6)
    )(*terms, bq, wq, b2, w2, b2_edge, w2_edge)
    return means, bio_out, wat_out


def solution(mesh):
    placed = (
        P("particle", "tile"),
        P("particle", "tile"),
        P("tile", None, None, None),
        P("tile", None),
        P(None, "particle", "tile"),
        P("tile"),
        P(None, "tile"),
        P("tile"),
        P(),
    )
    return jax.shard_map(
        body,
        mesh=mesh,
        in_specs=placed,
        out_specs=(P(None, None, "tile"), P("particle", "tile"), P("particle", "tile")),
        check_vma=False,
    )
```

```python
import functools

import jax
import jax.numpy as jnp
from jax import lax
from jax.experimental import pallas as pl
from jax.experimental.pallas import tpu as pltpu
from jax.sharding import PartitionSpec as P

BLK = 128
CYCLES = 2
HALO = 4
WIDE = 2 * HALO
NBR = 3
BOUNDS = (2.0, 5.0, 4.0)
SCALE_STEPS = 32000.0
STEPS = 32767.0
VMEM = pl.BlockSpec(memory_space=pltpu.VMEM)
SMEM = pl.BlockSpec(memory_space=pltpu.SMEM)
HBM = pl.BlockSpec(memory_space=pltpu.HBM)


def run(first, last, unroll, step, carry):
    if unroll:
        for n in range(first, last):
            carry = step(n, carry)
        return carry
    return lax.fori_loop(first, last, step, carry)


def lanes(n, at=0):
    if isinstance(n, int):
        return slice(at + n * BLK, at + (n + 1) * BLK)
    return pl.ds(pl.multiple_of(at + n * BLK, BLK), BLK)


def wetness(w):
    sq = w * w
    return sq / (1.0 + sq)


def flux_of(xs, flow):
    return jnp.dot(jnp.concatenate(xs, axis=1), flow, preferred_element_type=jnp.float32)


def right_first():
    return lax.rem(lax.axis_index("tile"), 2) == 0


def pack_kernel(bio, wat, rain, wire, fields, rains, held, factor):
    part, cells = bio.shape
    nb = cells // BLK
    half, quarter = cells // 2, cells // 4
    codes = []
    for f, field in enumerate((bio, wat, rain.at[0], rain.at[1])):
        big = jnp.abs(field[:, 0:BLK])
        for n in range(1, nb):
            big = jnp.maximum(big, jnp.abs(field[:, lanes(n)]))
        unit = BOUNDS[min(f, 2)] / SCALE_STEPS
        code = jnp.floor(jnp.max(big, axis=1, keepdims=True) / unit) + 1.0
        inv = jnp.broadcast_to(STEPS / (code * unit), (part, BLK))
        codes.append(jnp.broadcast_to(code, (part, BLK)))
        if f < 2:
            for h in range(2):
                row = (2 * h + f) * part
                held[row : row + part, 0:half] = field[:, h * half : (h + 1) * half]
                factor[0, row : row + part, :] = inv
        else:
            at = f * quarter
            for q in range(4):
                held[q * part : (q + 1) * part, at : at + quarter] = field[:, q * quarter : (q + 1) * quarter]
                factor[f - 1, q * part : (q + 1) * part, :] = inv
    for f in range(4):
        factor[3, f * part : (f + 1) * part, :] = codes[f]

    def coded(x):
        return jnp.round(x).astype(jnp.int32).astype(jnp.int16)

    pairs, quads = nb // 2, nb // 4
    for n in range(nb):
        x = coded(held[:, lanes(n)] * factor[0 if n < pairs else 1 if n < pairs + quads else 2])
        if n < pairs:
            wire[:, lanes(n)] = x
            fields[:, lanes(n)] = x
        else:
            wire[:, lanes(n + 1)] = x
            rains[:, lanes(n - pairs)] = x
    x = coded(factor[3])
    wire[:, lanes(pairs)] = x
    fields[:, lanes(pairs)] = x


def edge_kernel(after, left, right, ids, pay_a, pay_b):
    nb = ids.shape[1]
    even = right_first()
    pos = lax.axis_index("tile")
    line = lax.broadcasted_iota(jnp.int32, (16, BLK), 0)

    def edge(pay, block, start):
        away = jnp.zeros((16, BLK), jnp.float32)
        for m in range(HALO):
            n = start + m + pos * nb
            for k in range(NBR):
                at = (m * NBR + k) * BLK
                pay[at : at + BLK, :] = block[m, k]
            for k, gap in enumerate((n - ids[1, start + m], ids[2, start + m] - n)):
                away = jnp.where(line == 2 * m + k, gap.astype(jnp.float32), away)
        at = HALO * NBR * BLK
        pay[at : at + 16, :] = away.astype(jnp.bfloat16)

    @pl.when(even)
    def _():
        edge(pay_a, right, nb - HALO)
        edge(pay_b, left, 0)

    @pl.when(jnp.logical_not(even))
    def _():
        edge(pay_a, left, 0)
        edge(pay_b, right, nb - HALO)


def stage_kernel(after, flow, wire, growth, prec, obs, anc, rain, turned, *held):
    for src, dst in zip((wire, growth, prec, obs, anc), held):
        dst[...] = src[...]
    held[-1][...] = rain[2:4]
    for n in range(flow.shape[0]):
        for k in range(NBR):
            turned[n, k * BLK : (k + 1) * BLK, :] = flow[n, k].T


def halo_flux(ext, pay, right, nb, m):
    depth = NBR * BLK
    away = pay[HALO * depth : HALO * depth + 16, :].astype(jnp.float32)
    at = jnp.where(right, nb + WIDE + m, HALO + m)
    xs = [ext[at].astype(jnp.bfloat16)]
    for k, sign in enumerate((-1, 1)):
        gap = jnp.broadcast_to(away[2 * m + k : 2 * m + k + 1, :], ext.shape[1:])
        x = jnp.zeros(ext.shape[1:], jnp.float32)
        for d in range(HALO + 1):
            x = jnp.where(gap == d, ext[at + sign * d].astype(jnp.float32), x)
        xs.append(x.astype(jnp.bfloat16))
    total = jnp.zeros(ext.shape[1:], jnp.float32)
    for k, x in enumerate(xs):
        at = m * depth + k * BLK
        total += lax.dot_general(
            x, pay[at : at + BLK, :], (((1,), (1,)), ((), ())), preferred_element_type=jnp.float32
        )
    return total


def decode(sel, pieces, n):
    parts = []
    for ref, first in pieces:
        q = ref[:, lanes(n + first)].astype(jnp.int32)
        parts.append((q >> 8).astype(jnp.float32).astype(jnp.bfloat16))
        parts.append((q & 255).astype(jnp.float32).astype(jnp.bfloat16))
    return jnp.dot(sel, jnp.concatenate(parts, axis=0), preferred_element_type=jnp.float32)


def split(members, nb, refs):
    both = refs[:2]
    fields = [(r, 0) for r in (*both, *refs[2:members])]
    rains = [(r, nb // 2 + 1) for r in both] + [(r, 0) for r in refs[members : 2 * members - 2]]
    return fields, rains, refs[2 * members - 2 :]


def open_kernel(members, unroll, nb, *refs):
    pieces, rains, refs = split(members, nb, refs)
    anc, growth, prec, obs, wb, v0, b1, bq, wq, miss, quad, unit1, pay_a, pay_b, pair, scaler = refs
    slots = anc.shape[1]
    rows = pieces[0][0].shape[0]
    part = rows // 4
    depth = members * rows * 2
    me = lax.axis_index("particle")
    line = lax.broadcasted_iota(jnp.int32, (slots, slots), 0)
    lane = lax.broadcasted_iota(jnp.int32, (slots, slots), 1)
    first = jnp.broadcast_to(anc[0:1, :], (slots, slots)).astype(jnp.float32)
    chosen = jnp.sum(jnp.where(line == lane, first, 0.0), axis=1, keepdims=True)
    own = lax.broadcasted_iota(jnp.int32, (slots, 1), 0).astype(jnp.float32)
    col = lax.broadcasted_iota(jnp.int32, (slots, depth), 1)
    value = jnp.where((col // rows) % 2 == 0, 256.0, 1.0)
    group = (col % rows) // part
    source = (((col // (2 * rows)) ^ me) * part + col % part).astype(jnp.float32)

    def hits(g, want):
        return jnp.where(jnp.logical_and(group == g, source == want), value, 0.0).astype(jnp.bfloat16)

    for h in range(2):
        for i, want in enumerate((chosen, chosen, own, own)):
            at = (4 * h + i) * slots
            pair[at : at + slots, :] = hits(2 * h + i % 2, want)
    for g in range(4):
        quad[g * slots : (g + 1) * slots, :] = hits(g, own)
    for i, (g, want) in enumerate(((0, chosen), (1, chosen), (0, own), (1, own), (2, own), (3, own))):
        scaler[i * slots : (i + 1) * slots, :] = hits(g, want)

    pairs, quads = nb // 2, nb // 4
    codes = decode(scaler[...], pieces, pairs)
    scale = [
        codes[i * slots : (i + 1) * slots] * (BOUNDS[f] / SCALE_STEPS / STEPS) for i, f in enumerate((0, 1, 0, 1, 2, 2))
    ]
    unit1[...] = scale[5]

    def step(m, acc):
        wet = decode(quad[...], rains, m)
        for p in range(2):
            got = decode(pair[...], pieces, m + p * quads)
            for h in range(2):
                q = 2 * h + p
                n = m + q * quads
                b, w, bi, wi = (got[(4 * h + i) * slots : (4 * h + i + 1) * slots] * scale[i] for i in range(4))
                rain0 = wet[q * slots : (q + 1) * slots] * scale[4]
                s = wetness(w)
                row = pl.ds(n, 1)
                wb[n] = w.astype(jnp.bfloat16)
                v0[n] = w + rain0 - 0.2 * b * s
                b1[n] = b + growth[row, :] * b * (s - 0.4 * b)
                bq[n] = bi
                wq[n] = wi
                off = bi - obs[0:1, lanes(n)]
                acc = acc + prec[row, :] * (off * off)
        return acc

    miss[...] = run(0, quads, unroll, step, jnp.zeros((slots, BLK), jnp.float32))
    even = right_first()
    for pay, right in ((pay_a, even), (pay_b, jnp.logical_not(even))):
        pay[0:WIDE] = wb[pl.ds(jnp.where(right, nb - WIDE, 0), WIDE)]
        edge = v0[pl.ds(jnp.where(right, nb - HALO, 0), HALO)]
        top = edge.astype(jnp.bfloat16)
        pay[WIDE : WIDE + HALO] = top
        pay[WIDE + HALO : WIDE + 2 * HALO] = (edge - top.astype(jnp.float32)).astype(jnp.bfloat16)


def inner01_kernel(members, unroll, *refs):
    (wb, v0, b1, quad, unit1, flow, ids, growth, prec, obs, anc, rain), rains = refs[:12], refs[12 : 12 + members]
    r1, wb1, v1, b2, w2, ws, bs, v2, miss = refs[12 + members :]
    nb, slots = wb.shape[:2]
    rains = [(r, nb // 2 + 1) for r in rains[:2]] + [(r, 0) for r in rains[2:]]
    part = rain.shape[1]
    quads = nb // 4
    scale = unit1[...]
    base = lax.axis_index("tile") * nb

    def wet_day(m, carry):
        got = decode(quad[...], rains, m + quads)
        for q in range(4):
            r1[m + q * quads] = got[q * slots : (q + 1) * slots] * scale
        return carry

    run(0, quads, unroll, wet_day, 0)

    def day0(n, acc):
        w = v0[n] + flux_of((wb[n], wb[ids[1, n] - base], wb[ids[2, n] - base]), flow[n])
        wb1[n - HALO] = w.astype(jnp.bfloat16)
        b, v, acc = settle(n, w, b1, r1, growth, prec, obs, acc)
        b2[n - HALO] = b
        v1[n - HALO] = v
        return acc

    miss[...] = run(HALO, nb - HALO, unroll, day0, jnp.zeros((slots, BLK), jnp.float32))
    base = base + HALO

    def day1(n, carry):
        w2[n - WIDE] = v1[n - HALO] + flux_of((wb1[n - HALO], wb1[ids[1, n] - base], wb1[ids[2, n] - base]), flow[n])
        return carry

    run(WIDE, nb - WIDE, unroll, day1, 0)
    picks = ancestors_of(anc, part)

    def pick(n, carry):
        m = n - WIDE
        choose(picks, w2.at[m], b2.at[n - HALO], rain[0, :, lanes(n)], ws.at[m], bs.at[m], v2.at[m])
        return carry

    run(WIDE, nb - WIDE, unroll, pick, 0)


def settle(n, w, b1, r1, growth, prec, obs, acc):
    s = wetness(w)
    row = pl.ds(n, 1)
    b = b1[n]
    v = w + r1[n] - 0.2 * b * s
    b = b + growth[row, :] * b * (s - 0.4 * b)
    off = b - obs[1:2, lanes(n)]
    return b, v, acc + prec[row, :] * (off * off)


def ancestors_of(anc, part):
    return [anc[1, lax.axis_index("particle") * part + i] for i in range(part)]


def choose(picks, w2, b2, rain, ws, bs, v2):
    for i, p in enumerate(picks):
        ws[i : i + 1, :] = w2[pl.ds(p, 1), :]
        bs[i : i + 1, :] = b2[pl.ds(p, 1), :]
    w = ws[...]
    v2[...] = w + rain - 0.2 * bs[...] * wetness(w)


def outer01_kernel(
    unroll, wb, v0, b1, r1, wb1, v1, b2, wi, bi, vi, miss0, miss1, got_a, got_b, flow, flow_a, flow_b, ids,
    growth, prec, obs, anc, rain, b2_out, w2_out, ws, bs, v2, total, pay_a, pay_b, ext, ext1, v1_out,
):
    nb, slots = wb.shape[:2]
    part = rain.shape[1]
    pos = lax.axis_index("tile")
    even = right_first()
    lows, highs = (0, WIDE + HALO), (nb - WIDE - HALO, nb)
    for lo, hi in (lows, highs):
        ext[WIDE + lo : WIDE + hi] = wb[lo:hi]
    ext1[WIDE : 2 * WIDE] = wb1[0:WIDE]
    ext1[nb - WIDE : nb] = wb1[nb - 2 * HALO - WIDE : nb - 2 * HALO]
    sides = ((got_a, flow_a, even), (got_b, flow_b, jnp.logical_not(even)))
    for got, _, right in sides:
        ext[pl.ds(jnp.where(right, nb + WIDE, 0), WIDE)] = got[0:WIDE]
    base = WIDE - pos * nb

    def day0(n, acc):
        w = v0[n] + flux_of((ext[n + WIDE], ext[ids[1, n] + base], ext[ids[2, n] + base]), flow[n])
        ext1[n + HALO] = w.astype(jnp.bfloat16)
        b, v, acc = settle(n, w, b1, r1, growth, prec, obs, acc)
        m = n if n < HALO else n - (nb - 2 * HALO)
        b2_out[m] = b
        v1_out[m] = v
        return acc

    acc = miss1[...]
    for n in (*range(HALO), *range(nb - HALO, nb)):
        acc = day0(n, acc)
    total[0:slots, :] = miss0[...]
    total[slots : 2 * slots, :] = acc
    for got, pay, right in sides:
        spot = jnp.where(right, nb + HALO, 0)
        for m in range(HALO):
            edge = got[WIDE + m].astype(jnp.float32) + got[WIDE + HALO + m].astype(jnp.float32)
            ext1[spot + m] = (edge + halo_flux(ext, pay, right, nb, m)).astype(jnp.bfloat16)
    base = HALO - pos * nb
    picks = ancestors_of(anc, part)
    ws[WIDE : nb - WIDE] = wi[...]
    bs[WIDE : nb - WIDE] = bi[...]
    v2[WIDE : nb - WIDE] = vi[...]
    for n in (*range(WIDE), *range(nb - WIDE, nb)):
        m = n if n < WIDE else n - (nb - 2 * WIDE)
        if n < HALO or n >= nb - HALO:
            at = n if n < HALO else n - (nb - 2 * HALO)
            v, b = v1_out[at], b2_out.at[at]
        else:
            v, b = v1[n - HALO], b2.at[n - HALO]
        w2_out[m] = v + flux_of((ext1[n + HALO], ext1[ids[1, n] + base], ext1[ids[2, n] + base]), flow[n])
        choose(picks, w2_out.at[m], b, rain[0, :, lanes(n)], ws.at[n], bs.at[n], v2.at[n])
    for pay, right in ((pay_a, even), (pay_b, jnp.logical_not(even))):
        for m in range(WIDE):
            pay[m * part : (m + 1) * part, :] = ws[jnp.where(right, nb - WIDE, 0) + m]
        for m in range(HALO):
            pay[(WIDE + m) * part : (WIDE + m + 1) * part, :] = v2[jnp.where(right, nb - HALO, 0) + m]
    at = (WIDE + HALO) * part
    pay_a[at : at + 2 * slots, :] = total[...]


def inner23_kernel(unroll, ws, bs, v2, flow, ids, growth, rain, w3, wat, bio):
    nb = ws.shape[0]
    base = lax.axis_index("tile") * nb
    half = jnp.bfloat16

    def day2(n, carry):
        xs = [ws[i].astype(half) for i in (n, ids[1, n] - base, ids[2, n] - base)]
        w3[n - HALO] = v2[n] + flux_of(xs, flow[n])
        return carry

    run(HALO, nb - HALO, unroll, day2, 0)

    def day3(n, carry):
        xs = [w3[i - HALO].astype(half) for i in (n, ids[1, n] - base, ids[2, n] - base)]
        m = n - WIDE
        wat[m], bio[m] = final(n, w3[n - HALO], flux_of(xs, flow[n]), ws[n], bs[n], growth, rain)
        return carry

    run(WIDE, nb - WIDE, unroll, day3, 0)


def final(n, w3, flux, w, b, growth, rain):
    g = growth[pl.ds(n, 1), :]
    b = b + g * b * (wetness(w) - 0.4 * b)
    s = wetness(w3)
    return w3 + flux + rain[1, :, lanes(n)] - 0.2 * b * s, b + g * b * (s - 0.4 * b)


def outer23_kernel(
    ws, bs, v2, w3, wat, bio, got_a, got_b, flow, flow_a, flow_b, ids, growth, rain,
    bio_out, wat_out, ext, ext3,
):
    nb, part = ws.shape[:2]
    pos = lax.axis_index("tile")
    even = right_first()
    half = jnp.bfloat16
    for n in range(WIDE, nb - WIDE):
        wat_out[:, lanes(n)] = wat[n - WIDE]
        bio_out[:, lanes(n)] = bio[n - WIDE]
    for lo, hi in ((0, WIDE + HALO), (nb - WIDE - HALO, nb)):
        ext[WIDE + lo : WIDE + hi] = ws[lo:hi]
    ext3[WIDE : 2 * WIDE] = w3[0:WIDE]
    ext3[nb - WIDE : nb] = w3[nb - 2 * HALO - WIDE : nb - 2 * HALO]
    sides = ((got_a, flow_a, even), (got_b, flow_b, jnp.logical_not(even)))
    for got, _, right in sides:
        for m in range(WIDE):
            ext[jnp.where(right, nb + WIDE, 0) + m] = got[m * part : (m + 1) * part, :]
    base = WIDE - pos * nb
    for n in (*range(HALO), *range(nb - HALO, nb)):
        xs = [ext[i].astype(half) for i in (n + WIDE, ids[1, n] + base, ids[2, n] + base)]
        ext3[n + HALO] = v2[n] + flux_of(xs, flow[n])
    for got, pay, right in sides:
        spot = jnp.where(right, nb + HALO, 0)
        for m in range(HALO):
            edge = got[(WIDE + m) * part : (WIDE + m + 1) * part, :]
            ext3[spot + m] = edge + halo_flux(ext, pay, right, nb, m)
    base = HALO - pos * nb
    for n in (*range(WIDE), *range(nb - WIDE, nb)):
        xs = [ext3[i].astype(half) for i in (n + HALO, ids[1, n] + base, ids[2, n] + base)]
        w, b = final(n, ext3[n + HALO], flux_of(xs, flow[n]), ws[n], bs[n], growth, rain)
        wat_out[:, lanes(n)] = w
        bio_out[:, lanes(n)] = b


def means_kernel(unroll, count, *refs):
    bq, wq, b2, w2, b2_edge, w2_edge, means = refs[count:]
    nb, slots = bq.shape[:2]
    level = [ref[...] for ref in refs[:count]]
    while len(level) > 1:
        level = [a + b for a, b in zip(level[::2], level[1::2])]
    lw = -0.5 * jnp.sum(level[0], axis=1, keepdims=True)
    weights = []
    for c in range(CYCLES):
        x = lw[c * slots : (c + 1) * slots]
        e = jnp.exp(x - jnp.max(x, axis=0, keepdims=True))
        weights.append(jnp.broadcast_to(e / jnp.sum(e, axis=0, keepdims=True), (slots, BLK)))

    def mean(c, f, n, x):
        means[c, f : f + 1, lanes(n)] = jnp.sum(weights[c] * x, axis=0, keepdims=True)

    def fill(c, f, ref, first, last, shift):
        def step(n, carry):
            mean(c, f, n, ref[n - shift])
            return carry

        run(first, last, unroll, step, 0)

    fill(0, 0, bq, 0, nb, 0)
    fill(0, 1, wq, 0, nb, 0)
    for f, ref, edge, width in ((0, b2, b2_edge, HALO), (1, w2, w2_edge, WIDE)):
        fill(1, f, ref, width, nb - width, width)
        fill(1, f, edge, 0, width, 0)
        fill(1, f, edge, nb - width, nb, nb - 2 * width)


def weigh(flops):
    return pl.CostEstimate(flops=flops, bytes_accessed=1, transcendentals=0)


def call(kernel, out, specs, scratch=(), cost=1):
    return pl.pallas_call(
        kernel,
        out_shape=tuple(jax.ShapeDtypeStruct(s, d) for s, d in out),
        in_specs=specs,
        out_specs=tuple(VMEM for _ in out),
        scratch_shapes=list(scratch),
        compiler_params=pltpu.CompilerParams(vmem_limit_bytes=32 * 2**20),
        cost_estimate=weigh(cost),
    )


def body(biomass, water, flow_blocks, neighbours, rain, growth_rate, observations, obs_precision, ancestors):
    part, cells = biomass.shape
    nb = cells // BLK
    members, tiles = lax.axis_size("particle"), lax.axis_size("tile")
    slots = members * part
    unroll = slots <= 16
    f32, bf16, i16 = jnp.float32, jnp.bfloat16, jnp.int16
    swap_a = [(i, i ^ 1) for i in range(tiles)]
    swap_b = [(i, (i - 1) % tiles if i % 2 == 0 else (i + 1) % tiles) for i in range(tiles)]
    rows = 4 * part
    neighbours = neighbours.T

    depth = NBR * BLK
    edge = ((HALO * depth + 16, BLK), bf16)
    tile = (HALO, NBR, BLK, BLK)

    wire, fields, rains = pl.pallas_call(
        pack_kernel,
        grid=(1,),
        out_shape=tuple(
            jax.ShapeDtypeStruct((rows, n * BLK), i16) for n in (nb + 1, nb // 2 + 1, nb // 2)
        ),
        in_specs=[pl.BlockSpec((part, cells), lambda i: (0, 0))] * 2
        + [pl.BlockSpec((2, part, cells), lambda i: (0, 0, 0))],
        out_specs=(VMEM, VMEM, VMEM),
        scratch_shapes=[pltpu.VMEM((rows, cells), f32), pltpu.VMEM((4, rows, BLK), f32)],
        compiler_params=pltpu.CompilerParams(vmem_limit_bytes=60 * 2**20),
        cost_estimate=weigh(1),
    )(biomass, water, rain)
    def over(x, j):
        return lax.ppermute(x, "particle", [(i, i ^ j) for i in range(members)])

    flow_a, flow_b = pl.pallas_call(
        edge_kernel,
        grid=(1,),
        out_shape=tuple(jax.ShapeDtypeStruct(*edge) for _ in range(2)),
        in_specs=[
            HBM,
            pl.BlockSpec(tile, lambda i: (0, 0, 0, 0)),
            pl.BlockSpec(tile, lambda i: (nb // HALO - 1, 0, 0, 0)),
            SMEM,
        ],
        out_specs=(VMEM, VMEM),
        compiler_params=pltpu.CompilerParams(vmem_limit_bytes=60 * 2**20),
        cost_estimate=weigh(1),
    )(wire, flow_blocks, flow_blocks, neighbours)

    beside = over(wire, 1)
    far_rains = []
    for j in range(2, members):
        if j % 2 == 0:
            far_rains.append(over(rains, j))
        else:
            got, flow_a = lax.optimization_barrier((far_rains[-1], flow_a))
            far_rains.append(over(got, 1))
    far_fields = [over(fields, j) for j in range(2, members)]
    small = (wire, growth_rate.reshape(nb, BLK), obs_precision.reshape(nb, BLK), observations, ancestors)
    flow, wire, growth, prec, obs, anc, rain23 = call(
        stage_kernel,
        [((nb, depth, BLK), bf16)] + [(x.shape, x.dtype) for x in small] + [((2, part, cells), f32)],
        [HBM] + [VMEM] * 7,
    )(beside, flow_blocks, *small, rain)
    flow_a = lax.ppermute(flow_a, "tile", swap_a)
    flow_b = lax.ppermute(flow_b, "tile", swap_b)

    field = ((nb, slots, BLK), f32)
    wb, v0, b1, bq, wq, miss, quad, unit1, pay_a, pay_b = call(
        functools.partial(open_kernel, members, unroll, nb),
        [((nb, slots, BLK), bf16), field, field, field, field, ((slots, BLK), f32), ((4 * slots, members * rows * 2), bf16), ((slots, BLK), f32)]
        + [((WIDE + 2 * HALO, slots, BLK), bf16)] * 2,
        [VMEM] * (2 * members + 2),
        [
            pltpu.VMEM((8 * slots, members * rows * 2), bf16),
            pltpu.VMEM((6 * slots, members * rows * 2), bf16),
        ],
        cost=10**10,
    )(wire, beside, *far_fields, *far_rains, anc, growth, prec, obs)
    got_a = lax.ppermute(pay_a, "tile", swap_a)
    got_b = lax.ppermute(pay_b, "tile", swap_b)
    inner, core = nb - 2 * HALO, nb - 2 * WIDE

    def blocks(count, height=slots, kind=f32):
        return ((count, height, BLK), kind)

    r1, wb1, v1, b2, w2, wi, bi, vi, miss1 = call(
        functools.partial(inner01_kernel, members, unroll),
        [blocks(nb), blocks(inner, kind=bf16), blocks(inner), blocks(inner), blocks(core)]
        + [blocks(core, part)] * 3
        + [((slots, BLK), f32)],
        [VMEM] * 6 + [SMEM] + [VMEM] * 3 + [SMEM] + [VMEM] * (1 + members),
    )(
        wb, v0, b1, quad, unit1, flow, neighbours, growth, prec, obs, ancestors, rain23, wire, beside, *far_rains
    )
    swap_rows = (WIDE + HALO) * part
    b2_edge, w2_edge, ws, bs, v2, total, end_a, end_b = call(
        functools.partial(outer01_kernel, unroll),
        [blocks(2 * HALO), blocks(2 * WIDE)]
        + [blocks(nb, part)] * 3
        + [((2 * slots, BLK), f32), ((swap_rows + 2 * slots, BLK), f32), ((swap_rows, BLK), f32)],
        [VMEM] * 17 + [SMEM] + [VMEM] * 3 + [SMEM, VMEM],
        [
            pltpu.VMEM((nb + 2 * WIDE, slots, BLK), bf16),
            pltpu.VMEM((nb + WIDE, slots, BLK), bf16),
            pltpu.VMEM((2 * HALO, slots, BLK), f32),
        ],
    )(
        wb, v0, b1, r1, wb1, v1, b2, wi, bi, vi, miss, miss1, got_a, got_b, flow, flow_a, flow_b, neighbours,
        growth, prec, obs, ancestors, rain23,
    )
    last_a = lax.ppermute(end_a, "tile", swap_a)
    last_b = lax.ppermute(end_b, "tile", swap_b)

    terms = [total, last_a[swap_rows:]]
    span = 2
    while span < tiles:
        total = sum(terms[1:], terms[0])
        masks = [span] if span * 2 >= tiles else [span, 2 * span, 3 * span]
        terms = [total] + [lax.ppermute(total, "tile", [(i, i ^ m) for i in range(tiles)]) for m in masks]
        span *= 2 ** (len(masks) // 2 + 1)
    w3, wat, bio = call(
        functools.partial(inner23_kernel, unroll),
        [blocks(inner, part), blocks(core, part), blocks(core, part)],
        [VMEM] * 4 + [SMEM] + [VMEM] * 2,
    )(ws, bs, v2, flow, neighbours, growth, rain23)
    bio_out, wat_out = call(
        outer23_kernel,
        [((part, cells), f32)] * 2,
        [VMEM] * 11 + [SMEM] + [VMEM] * 2,
        [pltpu.VMEM((nb + 2 * WIDE, part, BLK), f32), pltpu.VMEM((nb + WIDE, part, BLK), f32)],
    )(ws, bs, v2, w3, wat, bio, last_a, last_b, flow, flow_a, flow_b, neighbours, growth, rain23)
    (means,) = call(
        functools.partial(means_kernel, unroll, len(terms)), [((CYCLES, 2, cells), f32)], [VMEM] * (len(terms) + 6)
    )(*terms, bq, wq, b2, w2, b2_edge, w2_edge)
    return means, bio_out, wat_out


def solution(mesh):
    placed = (
        P("particle", "tile"),
        P("particle", "tile"),
        P("tile", None, None, None),
        P("tile", None),
        P(None, "particle", "tile"),
        P("tile"),
        P(None, "tile"),
        P("tile"),
        P(),
    )
    return jax.shard_map(
        body,
        mesh=mesh,
        in_specs=placed,
        out_specs=(P(None, None, "tile"), P("particle", "tile"), P("particle", "tile")),
        check_vma=False,
    )
```

```python
import functools

import jax
import jax.numpy as jnp
from jax import lax
from jax.experimental import pallas as pl
from jax.experimental.pallas import tpu as pltpu
from jax.sharding import PartitionSpec as P

BLK = 128
CYCLES = 2
HALO = 4
WIDE = 2 * HALO
NBR = 3
BOUNDS = (2.0, 5.0, 4.0)
SCALE_STEPS = 32000.0
STEPS = 32767.0
VMEM = pl.BlockSpec(memory_space=pltpu.VMEM)
SMEM = pl.BlockSpec(memory_space=pltpu.SMEM)
HBM = pl.BlockSpec(memory_space=pltpu.HBM)


def run(first, last, unroll, step, carry):
    if unroll:
        for n in range(first, last):
            carry = step(n, carry)
        return carry
    return lax.fori_loop(first, last, step, carry)


def lanes(n, at=0):
    if isinstance(n, int):
        return slice(at + n * BLK, at + (n + 1) * BLK)
    return pl.ds(pl.multiple_of(at + n * BLK, BLK), BLK)


def wetness(w):
    sq = w * w
    return sq / (1.0 + sq)


def flux_of(xs, flow):
    return jnp.dot(jnp.concatenate(xs, axis=1), flow, preferred_element_type=jnp.float32)


def right_first():
    return lax.rem(lax.axis_index("tile"), 2) == 0


def pack_kernel(bio, wat, rain, flow, ids, wire, pay_a, pay_b, held, factor, gaps, sems):
    nb = ids.shape[1]
    depth = NBR * BLK
    span = HALO * depth
    even = right_first()
    pos = lax.axis_index("tile")
    line = lax.broadcasted_iota(jnp.int32, (16, BLK), 0)
    copies = []
    for i, (pay, right) in enumerate(((pay_a, even), (pay_b, jnp.logical_not(even)))):
        start = jnp.where(right, nb - HALO, 0)
        away = jnp.zeros((16, BLK), jnp.float32)
        for m in range(HALO):
            n = start + m + pos * nb
            for k, gap in enumerate((n - ids[1, start + m], ids[2, start + m] - n)):
                away = jnp.where(line == 2 * m + k, gap.astype(jnp.float32), away)
        gaps[i] = away.astype(jnp.bfloat16)
        at = pl.multiple_of(start * depth, depth)
        copies.append(pltpu.make_async_copy(flow.at[pl.ds(at, span)], pay.at[pl.ds(0, span)], sems.at[2 * i]))
        copies.append(pltpu.make_async_copy(gaps.at[i], pay.at[pl.ds(span, 16)], sems.at[2 * i + 1]))
    for c in copies:
        c.start()
    part, cells = bio.shape
    nb = cells // BLK
    half, quarter = cells // 2, cells // 4
    codes = []
    for f, field in enumerate((bio, wat, rain.at[0], rain.at[1])):
        big = jnp.abs(field[:, 0:BLK])
        for n in range(1, nb):
            big = jnp.maximum(big, jnp.abs(field[:, lanes(n)]))
        unit = BOUNDS[min(f, 2)] / SCALE_STEPS
        code = jnp.floor(jnp.max(big, axis=1, keepdims=True) / unit) + 1.0
        inv = jnp.broadcast_to(STEPS / (code * unit), (part, BLK))
        codes.append(jnp.broadcast_to(code, (part, BLK)))
        if f < 2:
            for h in range(2):
                row = (2 * h + f) * part
                held[row : row + part, 0:half] = field[:, h * half : (h + 1) * half]
                factor[0, row : row + part, :] = inv
        else:
            at = f * quarter
            for q in range(4):
                held[q * part : (q + 1) * part, at : at + quarter] = field[:, q * quarter : (q + 1) * quarter]
                factor[f - 1, q * part : (q + 1) * part, :] = inv
    for f in range(4):
        factor[3, f * part : (f + 1) * part, :] = codes[f]

    def coded(x):
        return jnp.round(x).astype(jnp.int32).astype(jnp.int16)

    pairs, quads = nb // 2, nb // 4
    for n in range(nb):
        wire[:, lanes(n)] = coded(held[:, lanes(n)] * factor[0 if n < pairs else 1 if n < pairs + quads else 2])
    wire[:, lanes(nb)] = coded(factor[3])
    for c in copies:
        c.wait()


def stage_kernel(after, flow, wire, growth, prec, obs, anc, rain, turned, *held):
    for src, dst in zip((wire, growth, prec, obs, anc), held):
        dst[...] = src[...]
    held[-1][...] = rain[2:4]
    for n in range(flow.shape[0]):
        for k in range(NBR):
            turned[n, k * BLK : (k + 1) * BLK, :] = flow[n, k].T


def halo_flux(ext, pay, right, nb, m):
    depth = NBR * BLK
    away = pay[HALO * depth : HALO * depth + 16, :].astype(jnp.float32)
    at = jnp.where(right, nb + WIDE + m, HALO + m)
    xs = [ext[at].astype(jnp.bfloat16)]
    for k, sign in enumerate((-1, 1)):
        gap = jnp.broadcast_to(away[2 * m + k : 2 * m + k + 1, :], ext.shape[1:])
        x = jnp.zeros(ext.shape[1:], jnp.float32)
        for d in range(HALO + 1):
            x = jnp.where(gap == d, ext[at + sign * d].astype(jnp.float32), x)
        xs.append(x.astype(jnp.bfloat16))
    return flux_of(xs, pay[m * depth : (m + 1) * depth, :])


def decode(sel, pieces, cols):
    parts = []
    for ref in pieces:
        q = ref[:, cols].astype(jnp.int32)
        parts.append((q >> 8).astype(jnp.float32).astype(jnp.bfloat16))
        parts.append((q & 255).astype(jnp.float32).astype(jnp.bfloat16))
    return jnp.dot(sel, jnp.concatenate(parts, axis=0), preferred_element_type=jnp.float32)


def open_kernel(members, unroll, *refs):
    pieces = refs[:members]
    anc, growth, prec, obs = refs[members : members + 4]
    wb, v0, b1, bq, wq, miss, quad, unit1, pay_a, pay_b = refs[members + 4 : members + 14]
    pair, scaler = refs[-2:]
    nb = growth.shape[0]
    slots = anc.shape[1]
    rows = pieces[0].shape[0]
    part = rows // 4
    depth = members * rows * 2
    me = lax.axis_index("particle")
    line = lax.broadcasted_iota(jnp.int32, (slots, slots), 0)
    lane = lax.broadcasted_iota(jnp.int32, (slots, slots), 1)
    first = jnp.broadcast_to(anc[0:1, :], (slots, slots)).astype(jnp.float32)
    chosen = jnp.sum(jnp.where(line == lane, first, 0.0), axis=1, keepdims=True)
    own = lax.broadcasted_iota(jnp.int32, (slots, 1), 0).astype(jnp.float32)
    col = lax.broadcasted_iota(jnp.int32, (slots, depth), 1)
    value = jnp.where((col // rows) % 2 == 0, 256.0, 1.0)
    group = (col % rows) // part
    source = (((col // (2 * rows)) ^ me) * part + col % part).astype(jnp.float32)

    def hits(g, want):
        return jnp.where(jnp.logical_and(group == g, source == want), value, 0.0).astype(jnp.bfloat16)

    for h in range(2):
        for i, want in enumerate((chosen, chosen, own, own)):
            at = (4 * h + i) * slots
            pair[at : at + slots, :] = hits(2 * h + i % 2, want)
    for g in range(4):
        quad[g * slots : (g + 1) * slots, :] = hits(g, own)
    for i, (g, want) in enumerate(((0, chosen), (1, chosen), (0, own), (1, own), (2, own), (3, own))):
        scaler[i * slots : (i + 1) * slots, :] = hits(g, want)

    pairs, quads = nb // 2, nb // 4
    codes = decode(scaler[...], pieces, lanes(nb))
    scale = [
        codes[i * slots : (i + 1) * slots] * (BOUNDS[f] / SCALE_STEPS / STEPS) for i, f in enumerate((0, 1, 0, 1, 2, 2))
    ]
    unit1[...] = scale[5]

    def step(m, acc):
        wet = decode(quad[...], pieces, lanes(m, pairs * BLK))
        for p in range(2):
            got = decode(pair[...], pieces, lanes(m + p * quads))
            for h in range(2):
                q = 2 * h + p
                n = m + q * quads
                b, w, bi, wi = (got[(4 * h + i) * slots : (4 * h + i + 1) * slots] * scale[i] for i in range(4))
                rain0 = wet[q * slots : (q + 1) * slots] * scale[4]
                s = wetness(w)
                row = pl.ds(n, 1)
                wb[n] = w.astype(jnp.bfloat16)
                v0[n] = w + rain0 - 0.2 * b * s
                b1[n] = b + growth[row, :] * b * (s - 0.4 * b)
                bq[n] = bi
                wq[n] = wi
                off = bi - obs[0:1, lanes(n)]
                acc = acc + prec[row, :] * (off * off)
        return acc

    miss[...] = run(0, quads, unroll, step, jnp.zeros((slots, BLK), jnp.float32))
    even = right_first()
    for pay, right in ((pay_a, even), (pay_b, jnp.logical_not(even))):
        pay[0:WIDE] = wb[pl.ds(jnp.where(right, nb - WIDE, 0), WIDE)]
        edge = v0[pl.ds(jnp.where(right, nb - HALO, 0), HALO)]
        top = edge.astype(jnp.bfloat16)
        pay[WIDE : WIDE + HALO] = top
        pay[WIDE + HALO : WIDE + 2 * HALO] = (edge - top.astype(jnp.float32)).astype(jnp.bfloat16)


def inner01_kernel(members, unroll, *refs):
    pieces = refs[:members]
    wb, v0, b1, quad, unit1, flow, ids, growth, prec, obs, anc, rain, flow_a, flow_b = refs[members : members + 14]
    r1, wb1, v1, b2, w2, ws, bs, v2, miss, turn_a, turn_b = refs[members + 14 :]
    nb, slots = wb.shape[:2]
    part = rain.shape[1]
    quads = nb // 4
    scale = unit1[...]
    base = lax.axis_index("tile") * nb

    def wet_day(m, carry):
        got = decode(quad[...], pieces, lanes(m, 3 * quads * BLK))
        for q in range(4):
            r1[m + q * quads] = got[q * slots : (q + 1) * slots] * scale
        return carry

    run(0, quads, unroll, wet_day, 0)

    def day0(n, acc):
        w = v0[n] + flux_of((wb[n], wb[ids[1, n] - base], wb[ids[2, n] - base]), flow[n])
        wb1[n - HALO] = w.astype(jnp.bfloat16)
        b, v, acc = settle(n, w, b1, r1, growth, prec, obs, acc)
        b2[n - HALO] = b
        v1[n - HALO] = v
        return acc

    miss[...] = run(HALO, nb - HALO, unroll, day0, jnp.zeros((slots, BLK), jnp.float32))
    base = base + HALO

    def day1(n, carry):
        w2[n - WIDE] = v1[n - HALO] + flux_of((wb1[n - HALO], wb1[ids[1, n] - base], wb1[ids[2, n] - base]), flow[n])
        return carry

    run(WIDE, nb - WIDE, unroll, day1, 0)
    picks = ancestors_of(anc, part)

    def pick(n, carry):
        m = n - WIDE
        choose(picks, w2.at[m], b2.at[n - HALO], rain[0, :, lanes(n)], ws.at[m], bs.at[m], v2.at[m])
        return carry

    run(WIDE, nb - WIDE, unroll, pick, 0)
    for raw, turned in ((flow_a, turn_a), (flow_b, turn_b)):
        for at in range(0, HALO * NBR * BLK, BLK):
            turned[at : at + BLK, :] = raw[at : at + BLK, :].T
        turned[HALO * NBR * BLK :, :] = raw[HALO * NBR * BLK :, :]


def settle(n, w, b1, r1, growth, prec, obs, acc):
    s = wetness(w)
    row = pl.ds(n, 1)
    b = b1[n]
    v = w + r1[n] - 0.2 * b * s
    b = b + growth[row, :] * b * (s - 0.4 * b)
    off = b - obs[1:2, lanes(n)]
    return b, v, acc + prec[row, :] * (off * off)


def ancestors_of(anc, part):
    return [anc[1, lax.axis_index("particle") * part + i] for i in range(part)]


def choose(picks, w2, b2, rain, ws, bs, v2):
    for i, p in enumerate(picks):
        ws[i : i + 1, :] = w2[pl.ds(p, 1), :]
        bs[i : i + 1, :] = b2[pl.ds(p, 1), :]
    w = ws[...]
    v2[...] = w + rain - 0.2 * bs[...] * wetness(w)


def outer01_kernel(
    unroll, wb, v0, b1, r1, wb1, v1, b2, wi, bi, vi, miss0, miss1, got_a, got_b, flow, flow_a, flow_b, ids,
    growth, prec, obs, anc, rain, b2_out, w2_out, ws, bs, v2, total, pay_a, pay_b, ext, ext1, v1_out,
):
    nb, slots = wb.shape[:2]
    part = rain.shape[1]
    pos = lax.axis_index("tile")
    even = right_first()
    lows, highs = (0, WIDE + HALO), (nb - WIDE - HALO, nb)
    for lo, hi in (lows, highs):
        ext[WIDE + lo : WIDE + hi] = wb[lo:hi]
    ext1[WIDE : 2 * WIDE] = wb1[0:WIDE]
    ext1[nb - WIDE : nb] = wb1[nb - 2 * HALO - WIDE : nb - 2 * HALO]
    sides = ((got_a, flow_a, even), (got_b, flow_b, jnp.logical_not(even)))
    for got, _, right in sides:
        ext[pl.ds(jnp.where(right, nb + WIDE, 0), WIDE)] = got[0:WIDE]
    base = WIDE - pos * nb

    def day0(n, acc):
        w = v0[n] + flux_of((ext[n + WIDE], ext[ids[1, n] + base], ext[ids[2, n] + base]), flow[n])
        ext1[n + HALO] = w.astype(jnp.bfloat16)
        b, v, acc = settle(n, w, b1, r1, growth, prec, obs, acc)
        m = n if n < HALO else n - (nb - 2 * HALO)
        b2_out[m] = b
        v1_out[m] = v
        return acc

    acc = miss1[...]
    for n in (*range(HALO), *range(nb - HALO, nb)):
        acc = day0(n, acc)
    total[0:slots, :] = miss0[...]
    total[slots : 2 * slots, :] = acc
    for got, pay, right in sides:
        spot = jnp.where(right, nb + HALO, 0)
        for m in range(HALO):
            edge = got[WIDE + m].astype(jnp.float32) + got[WIDE + HALO + m].astype(jnp.float32)
            ext1[spot + m] = (edge + halo_flux(ext, pay, right, nb, m)).astype(jnp.bfloat16)
    base = HALO - pos * nb
    picks = ancestors_of(anc, part)
    ws[WIDE : nb - WIDE] = wi[...]
    bs[WIDE : nb - WIDE] = bi[...]
    v2[WIDE : nb - WIDE] = vi[...]
    for n in (*range(WIDE), *range(nb - WIDE, nb)):
        m = n if n < WIDE else n - (nb - 2 * WIDE)
        if n < HALO or n >= nb - HALO:
            at = n if n < HALO else n - (nb - 2 * HALO)
            v, b = v1_out[at], b2_out.at[at]
        else:
            v, b = v1[n - HALO], b2.at[n - HALO]
        w2_out[m] = v + flux_of((ext1[n + HALO], ext1[ids[1, n] + base], ext1[ids[2, n] + base]), flow[n])
        choose(picks, w2_out.at[m], b, rain[0, :, lanes(n)], ws.at[n], bs.at[n], v2.at[n])
    for pay, right in ((pay_a, even), (pay_b, jnp.logical_not(even))):
        for m in range(WIDE):
            pay[m * part : (m + 1) * part, :] = ws[jnp.where(right, nb - WIDE, 0) + m]
        for m in range(HALO):
            pay[(WIDE + m) * part : (WIDE + m + 1) * part, :] = v2[jnp.where(right, nb - HALO, 0) + m]
    at = (WIDE + HALO) * part
    pay_a[at : at + 2 * slots, :] = total[...]


def inner23_kernel(unroll, ws, bs, v2, flow, ids, growth, rain, w3, wat, bio):
    nb = ws.shape[0]
    base = lax.axis_index("tile") * nb
    half = jnp.bfloat16

    def day2(n, carry):
        xs = [ws[i].astype(half) for i in (n, ids[1, n] - base, ids[2, n] - base)]
        w3[n - HALO] = v2[n] + flux_of(xs, flow[n])
        return carry

    run(HALO, nb - HALO, unroll, day2, 0)

    def day3(n, carry):
        xs = [w3[i - HALO].astype(half) for i in (n, ids[1, n] - base, ids[2, n] - base)]
        m = n - WIDE
        wat[m], bio[m] = final(n, w3[n - HALO], flux_of(xs, flow[n]), ws[n], bs[n], growth, rain)
        return carry

    run(WIDE, nb - WIDE, unroll, day3, 0)


def final(n, w3, flux, w, b, growth, rain):
    g = growth[pl.ds(n, 1), :]
    b = b + g * b * (wetness(w) - 0.4 * b)
    s = wetness(w3)
    return w3 + flux + rain[1, :, lanes(n)] - 0.2 * b * s, b + g * b * (s - 0.4 * b)


def outer23_kernel(
    ws, bs, v2, w3, wat, bio, got_a, got_b, flow, flow_a, flow_b, ids, growth, rain,
    bio_out, wat_out, ext, ext3,
):
    nb, part = ws.shape[:2]
    pos = lax.axis_index("tile")
    even = right_first()
    half = jnp.bfloat16
    for n in range(WIDE, nb - WIDE):
        wat_out[:, lanes(n)] = wat[n - WIDE]
        bio_out[:, lanes(n)] = bio[n - WIDE]
    for lo, hi in ((0, WIDE + HALO), (nb - WIDE - HALO, nb)):
        ext[WIDE + lo : WIDE + hi] = ws[lo:hi]
    ext3[WIDE : 2 * WIDE] = w3[0:WIDE]
    ext3[nb - WIDE : nb] = w3[nb - 2 * HALO - WIDE : nb - 2 * HALO]
    sides = ((got_a, flow_a, even), (got_b, flow_b, jnp.logical_not(even)))
    for got, _, right in sides:
        for m in range(WIDE):
            ext[jnp.where(right, nb + WIDE, 0) + m] = got[m * part : (m + 1) * part, :]
    base = WIDE - pos * nb
    for n in (*range(HALO), *range(nb - HALO, nb)):
        xs = [ext[i].astype(half) for i in (n + WIDE, ids[1, n] + base, ids[2, n] + base)]
        ext3[n + HALO] = v2[n] + flux_of(xs, flow[n])
    for got, pay, right in sides:
        spot = jnp.where(right, nb + HALO, 0)
        for m in range(HALO):
            edge = got[(WIDE + m) * part : (WIDE + m + 1) * part, :]
            ext3[spot + m] = edge + halo_flux(ext, pay, right, nb, m)
    base = HALO - pos * nb
    for n in (*range(WIDE), *range(nb - WIDE, nb)):
        xs = [ext3[i].astype(half) for i in (n + HALO, ids[1, n] + base, ids[2, n] + base)]
        w, b = final(n, ext3[n + HALO], flux_of(xs, flow[n]), ws[n], bs[n], growth, rain)
        wat_out[:, lanes(n)] = w
        bio_out[:, lanes(n)] = b


def means_kernel(unroll, count, *refs):
    bq, wq, b2, w2, b2_edge, w2_edge, means = refs[count:]
    nb, slots = bq.shape[:2]
    level = [ref[...] for ref in refs[:count]]
    while len(level) > 1:
        level = [a + b for a, b in zip(level[::2], level[1::2])]
    lw = -0.5 * jnp.sum(level[0], axis=1, keepdims=True)
    weights = []
    for c in range(CYCLES):
        x = lw[c * slots : (c + 1) * slots]
        e = jnp.exp(x - jnp.max(x, axis=0, keepdims=True))
        weights.append(jnp.broadcast_to(e / jnp.sum(e, axis=0, keepdims=True), (slots, BLK)))

    def mean(c, f, n, x):
        means[c, f : f + 1, lanes(n)] = jnp.sum(weights[c] * x, axis=0, keepdims=True)

    def fill(c, f, ref, first, last, shift):
        def step(n, carry):
            mean(c, f, n, ref[n - shift])
            return carry

        run(first, last, unroll, step, 0)

    fill(0, 0, bq, 0, nb, 0)
    fill(0, 1, wq, 0, nb, 0)
    for f, ref, edge, width in ((0, b2, b2_edge, HALO), (1, w2, w2_edge, WIDE)):
        fill(1, f, ref, width, nb - width, width)
        fill(1, f, edge, 0, width, 0)
        fill(1, f, edge, nb - width, nb, nb - 2 * width)


def weigh(flops):
    return pl.CostEstimate(flops=flops, bytes_accessed=1, transcendentals=0)


def call(kernel, out, specs, scratch=(), cost=1):
    return pl.pallas_call(
        kernel,
        out_shape=tuple(jax.ShapeDtypeStruct(s, d) for s, d in out),
        in_specs=specs,
        out_specs=tuple(VMEM for _ in out),
        scratch_shapes=list(scratch),
        compiler_params=pltpu.CompilerParams(vmem_limit_bytes=32 * 2**20),
        cost_estimate=weigh(cost),
    )


def body(biomass, water, flow_blocks, neighbours, rain, growth_rate, observations, obs_precision, ancestors):
    part, cells = biomass.shape
    nb = cells // BLK
    members, tiles = lax.axis_size("particle"), lax.axis_size("tile")
    slots = members * part
    unroll = slots <= 16
    f32, bf16, i16 = jnp.float32, jnp.bfloat16, jnp.int16
    swap_a = [(i, i ^ 1) for i in range(tiles)]
    swap_b = [(i, (i - 1) % tiles if i % 2 == 0 else (i + 1) % tiles) for i in range(tiles)]
    rows = 4 * part
    neighbours = neighbours.T

    depth = NBR * BLK
    edge = ((HALO * depth + 16, BLK), bf16)
    wire, flow_a, flow_b = pl.pallas_call(
        pack_kernel,
        grid=(1,),
        out_shape=(jax.ShapeDtypeStruct((rows, (nb + 1) * BLK), i16), *(jax.ShapeDtypeStruct(*edge) for _ in range(2))),
        in_specs=[pl.BlockSpec((part, cells), lambda i: (0, 0))] * 2
        + [pl.BlockSpec((2, part, cells), lambda i: (0, 0, 0)), HBM, SMEM],
        out_specs=(VMEM, HBM, HBM),
        scratch_shapes=[
            pltpu.VMEM((rows, cells), f32),
            pltpu.VMEM((4, rows, BLK), f32),
            pltpu.VMEM((2, 16, BLK), bf16),
            pltpu.SemaphoreType.DMA((4,)),
        ],
        compiler_params=pltpu.CompilerParams(vmem_limit_bytes=60 * 2**20),
        cost_estimate=weigh(1),
    )(biomass, water, rain, flow_blocks.reshape(nb * depth, BLK), neighbours)

    pieces = [wire] + [
        lax.ppermute(wire, "particle", [(i, i ^ j) for i in range(members)]) for j in range(1, members)
    ]
    small = (wire, growth_rate.reshape(nb, BLK), obs_precision.reshape(nb, BLK), observations, ancestors)
    flow, pieces[0], growth, prec, obs, anc, rain23 = call(
        stage_kernel,
        [((nb, depth, BLK), bf16)] + [(x.shape, x.dtype) for x in small] + [((2, part, cells), f32)],
        [HBM] + [VMEM] * 7,
    )(pieces[1], flow_blocks, *small, rain)
    flow_a = lax.ppermute(flow_a, "tile", swap_a)
    flow_b = lax.ppermute(flow_b, "tile", swap_b)

    field = ((nb, slots, BLK), f32)
    wb, v0, b1, bq, wq, miss, quad, unit1, pay_a, pay_b = call(
        functools.partial(open_kernel, members, unroll),
        [((nb, slots, BLK), bf16), field, field, field, field, ((slots, BLK), f32), ((4 * slots, members * rows * 2), bf16), ((slots, BLK), f32)]
        + [((WIDE + 2 * HALO, slots, BLK), bf16)] * 2,
        [VMEM] * (members + 4),
        [
            pltpu.VMEM((8 * slots, members * rows * 2), bf16),
            pltpu.VMEM((6 * slots, members * rows * 2), bf16),
        ],
        cost=10**10,
    )(*pieces, anc, growth, prec, obs)
    got_a = lax.ppermute(pay_a, "tile", swap_a)
    got_b = lax.ppermute(pay_b, "tile", swap_b)
    inner, core = nb - 2 * HALO, nb - 2 * WIDE

    def blocks(count, height=slots, kind=f32):
        return ((count, height, BLK), kind)

    r1, wb1, v1, b2, w2, wi, bi, vi, miss1, turn_a, turn_b = call(
        functools.partial(inner01_kernel, members, unroll),
        [blocks(nb), blocks(inner, kind=bf16), blocks(inner), blocks(inner), blocks(core)]
        + [blocks(core, part)] * 3
        + [((slots, BLK), f32), edge, edge],
        [VMEM] * (members + 6) + [SMEM] + [VMEM] * 3 + [SMEM] + [VMEM] * 3,
    )(
        *pieces, wb, v0, b1, quad, unit1, flow, neighbours, growth, prec, obs, ancestors, rain23, flow_a, flow_b
    )
    swap_rows = (WIDE + HALO) * part
    b2_edge, w2_edge, ws, bs, v2, total, end_a, end_b = call(
        functools.partial(outer01_kernel, unroll),
        [blocks(2 * HALO), blocks(2 * WIDE)]
        + [blocks(nb, part)] * 3
        + [((2 * slots, BLK), f32), ((swap_rows + 2 * slots, BLK), f32), ((swap_rows, BLK), f32)],
        [VMEM] * 17 + [SMEM] + [VMEM] * 3 + [SMEM, VMEM],
        [
            pltpu.VMEM((nb + 2 * WIDE, slots, BLK), bf16),
            pltpu.VMEM((nb + WIDE, slots, BLK), bf16),
            pltpu.VMEM((2 * HALO, slots, BLK), f32),
        ],
    )(
        wb, v0, b1, r1, wb1, v1, b2, wi, bi, vi, miss, miss1, got_a, got_b, flow, turn_a, turn_b, neighbours,
        growth, prec, obs, ancestors, rain23,
    )
    last_a = lax.ppermute(end_a, "tile", swap_a)
    last_b = lax.ppermute(end_b, "tile", swap_b)

    terms = [total, last_a[swap_rows:]]
    span = 2
    while span < tiles:
        total = sum(terms[1:], terms[0])
        masks = [span] if span * 2 >= tiles else [span, 2 * span, 3 * span]
        terms = [total] + [lax.ppermute(total, "tile", [(i, i ^ m) for i in range(tiles)]) for m in masks]
        span *= 2 ** (len(masks) // 2 + 1)
    w3, wat, bio = call(
        functools.partial(inner23_kernel, unroll),
        [blocks(inner, part), blocks(core, part), blocks(core, part)],
        [VMEM] * 4 + [SMEM] + [VMEM] * 2,
    )(ws, bs, v2, flow, neighbours, growth, rain23)
    bio_out, wat_out = call(
        outer23_kernel,
        [((part, cells), f32)] * 2,
        [VMEM] * 11 + [SMEM] + [VMEM] * 2,
        [pltpu.VMEM((nb + 2 * WIDE, part, BLK), f32), pltpu.VMEM((nb + WIDE, part, BLK), f32)],
    )(ws, bs, v2, w3, wat, bio, last_a, last_b, flow, turn_a, turn_b, neighbours, growth, rain23)
    (means,) = call(
        functools.partial(means_kernel, unroll, len(terms)), [((CYCLES, 2, cells), f32)], [VMEM] * (len(terms) + 6)
    )(*terms, bq, wq, b2, w2, b2_edge, w2_edge)
    return means, bio_out, wat_out


def solution(mesh):
    placed = (
        P("particle", "tile"),
        P("particle", "tile"),
        P("tile", None, None, None),
        P("tile", None),
        P(None, "particle", "tile"),
        P("tile"),
        P(None, "tile"),
        P("tile"),
        P(),
    )
    return jax.shard_map(
        body,
        mesh=mesh,
        in_specs=placed,
        out_specs=(P(None, None, "tile"), P("particle", "tile"), P("particle", "tile")),
        check_vma=False,
    )
```

```python
import functools

import jax
import jax.numpy as jnp
from jax import lax
from jax.experimental import pallas as pl
from jax.experimental.pallas import tpu as pltpu
from jax.sharding import PartitionSpec as P

BLK = 128
CYCLES = 2
HALO = 4
WIDE = 2 * HALO
NBR = 3
BOUNDS = (2.0, 5.0, 4.0)
SCALE_STEPS = 32000.0
STEPS = 32767.0
VMEM = pl.BlockSpec(memory_space=pltpu.VMEM)
SMEM = pl.BlockSpec(memory_space=pltpu.SMEM)
HBM = pl.BlockSpec(memory_space=pltpu.HBM)


def run(first, last, unroll, step, carry):
    if unroll:
        for n in range(first, last):
            carry = step(n, carry)
        return carry
    return lax.fori_loop(first, last, step, carry)


def lanes(n, at=0):
    if isinstance(n, int):
        return slice(at + n * BLK, at + (n + 1) * BLK)
    return pl.ds(pl.multiple_of(at + n * BLK, BLK), BLK)


def wetness(w):
    sq = w * w
    return sq / (1.0 + sq)


def flux_of(xs, flow):
    return jnp.dot(jnp.concatenate(xs, axis=1), flow, preferred_element_type=jnp.float32)


def right_first():
    return lax.rem(lax.axis_index("tile"), 2) == 0


def pack_kernel(bio, wat, rain, wire, held, factor):
    part, cells = bio.shape
    nb = cells // BLK
    half, quarter = cells // 2, cells // 4
    codes = []
    for f, field in enumerate((bio, wat, rain.at[0], rain.at[1])):
        big = jnp.abs(field[:, 0:BLK])
        for n in range(1, nb):
            big = jnp.maximum(big, jnp.abs(field[:, lanes(n)]))
        unit = BOUNDS[min(f, 2)] / SCALE_STEPS
        code = jnp.floor(jnp.max(big, axis=1, keepdims=True) / unit) + 1.0
        inv = jnp.broadcast_to(STEPS / (code * unit), (part, BLK))
        codes.append(jnp.broadcast_to(code, (part, BLK)))
        if f < 2:
            for h in range(2):
                row = (2 * h + f) * part
                held[row : row + part, 0:half] = field[:, h * half : (h + 1) * half]
                factor[0, row : row + part, :] = inv
        else:
            at = f * quarter
            for q in range(4):
                held[q * part : (q + 1) * part, at : at + quarter] = field[:, q * quarter : (q + 1) * quarter]
                factor[f - 1, q * part : (q + 1) * part, :] = inv
    for f in range(4):
        factor[3, f * part : (f + 1) * part, :] = codes[f]

    def coded(x):
        return jnp.round(x).astype(jnp.int32).astype(jnp.int16)

    pairs, quads = nb // 2, nb // 4
    for n in range(nb):
        wire[:, lanes(n)] = coded(held[:, lanes(n)] * factor[0 if n < pairs else 1 if n < pairs + quads else 2])
    wire[:, lanes(nb)] = coded(factor[3])


def edge_kernel(after, left, right, ids, pay_a, pay_b):
    nb = ids.shape[1]
    even = right_first()
    pos = lax.axis_index("tile")
    line = lax.broadcasted_iota(jnp.int32, (16, BLK), 0)

    def edge(pay, block, start):
        away = jnp.zeros((16, BLK), jnp.float32)
        for m in range(HALO):
            n = start + m + pos * nb
            for k in range(NBR):
                at = (m * NBR + k) * BLK
                pay[at : at + BLK, :] = block[m, k]
            for k, gap in enumerate((n - ids[1, start + m], ids[2, start + m] - n)):
                away = jnp.where(line == 2 * m + k, gap.astype(jnp.float32), away)
        at = HALO * NBR * BLK
        pay[at : at + 16, :] = away.astype(jnp.bfloat16)

    @pl.when(even)
    def _():
        edge(pay_a, right, nb - HALO)
        edge(pay_b, left, 0)

    @pl.when(jnp.logical_not(even))
    def _():
        edge(pay_a, left, 0)
        edge(pay_b, right, nb - HALO)


def stage_kernel(after, flow, wire, growth, prec, obs, anc, rain, turned, *held):
    for src, dst in zip((wire, growth, prec, obs, anc), held):
        dst[...] = src[...]
    held[-1][...] = rain[2:4]
    for n in range(flow.shape[0]):
        for k in range(NBR):
            turned[n, k * BLK : (k + 1) * BLK, :] = flow[n, k].T


def halo_flux(ext, pay, right, nb, m):
    depth = NBR * BLK
    away = pay[HALO * depth : HALO * depth + 16, :].astype(jnp.float32)
    at = jnp.where(right, nb + WIDE + m, HALO + m)
    xs = [ext[at].astype(jnp.bfloat16)]
    for k, sign in enumerate((-1, 1)):
        gap = jnp.broadcast_to(away[2 * m + k : 2 * m + k + 1, :], ext.shape[1:])
        x = jnp.zeros(ext.shape[1:], jnp.float32)
        for d in range(HALO + 1):
            x = jnp.where(gap == d, ext[at + sign * d].astype(jnp.float32), x)
        xs.append(x.astype(jnp.bfloat16))
    return flux_of(xs, pay[m * depth : (m + 1) * depth, :])


def decode(sel, pieces, cols):
    parts = []
    for ref in pieces:
        q = ref[:, cols].astype(jnp.int32)
        parts.append((q >> 8).astype(jnp.float32).astype(jnp.bfloat16))
        parts.append((q & 255).astype(jnp.float32).astype(jnp.bfloat16))
    return jnp.dot(sel, jnp.concatenate(parts, axis=0), preferred_element_type=jnp.float32)


def open_kernel(members, unroll, *refs):
    pieces = refs[:members]
    anc, growth, prec, obs = refs[members : members + 4]
    wb, v0, b1, bq, wq, miss, quad, unit1, pay_a, pay_b = refs[members + 4 : members + 14]
    pair, scaler = refs[-2:]
    nb = growth.shape[0]
    slots = anc.shape[1]
    rows = pieces[0].shape[0]
    part = rows // 4
    depth = members * rows * 2
    me = lax.axis_index("particle")
    line = lax.broadcasted_iota(jnp.int32, (slots, slots), 0)
    lane = lax.broadcasted_iota(jnp.int32, (slots, slots), 1)
    first = jnp.broadcast_to(anc[0:1, :], (slots, slots)).astype(jnp.float32)
    chosen = jnp.sum(jnp.where(line == lane, first, 0.0), axis=1, keepdims=True)
    own = lax.broadcasted_iota(jnp.int32, (slots, 1), 0).astype(jnp.float32)
    col = lax.broadcasted_iota(jnp.int32, (slots, depth), 1)
    value = jnp.where((col // rows) % 2 == 0, 256.0, 1.0)
    group = (col % rows) // part
    source = (((col // (2 * rows)) ^ me) * part + col % part).astype(jnp.float32)

    def hits(g, want):
        return jnp.where(jnp.logical_and(group == g, source == want), value, 0.0).astype(jnp.bfloat16)

    for h in range(2):
        for i, want in enumerate((chosen, chosen, own, own)):
            at = (4 * h + i) * slots
            pair[at : at + slots, :] = hits(2 * h + i % 2, want)
    for g in range(4):
        quad[g * slots : (g + 1) * slots, :] = hits(g, own)
    for i, (g, want) in enumerate(((0, chosen), (1, chosen), (0, own), (1, own), (2, own), (3, own))):
        scaler[i * slots : (i + 1) * slots, :] = hits(g, want)

    pairs, quads = nb // 2, nb // 4
    codes = decode(scaler[...], pieces, lanes(nb))
    scale = [
        codes[i * slots : (i + 1) * slots] * (BOUNDS[f] / SCALE_STEPS / STEPS) for i, f in enumerate((0, 1, 0, 1, 2, 2))
    ]
    unit1[...] = scale[5]

    def step(m, acc):
        wet = decode(quad[...], pieces, lanes(m, pairs * BLK))
        for p in range(2):
            got = decode(pair[...], pieces, lanes(m + p * quads))
            for h in range(2):
                q = 2 * h + p
                n = m + q * quads
                b, w, bi, wi = (got[(4 * h + i) * slots : (4 * h + i + 1) * slots] * scale[i] for i in range(4))
                rain0 = wet[q * slots : (q + 1) * slots] * scale[4]
                s = wetness(w)
                row = pl.ds(n, 1)
                wb[n] = w.astype(jnp.bfloat16)
                v0[n] = w + rain0 - 0.2 * b * s
                b1[n] = b + growth[row, :] * b * (s - 0.4 * b)
                bq[n] = bi
                wq[n] = wi
                off = bi - obs[0:1, lanes(n)]
                acc = acc + prec[row, :] * (off * off)
        return acc

    miss[...] = run(0, quads, unroll, step, jnp.zeros((slots, BLK), jnp.float32))
    even = right_first()
    for pay, right in ((pay_a, even), (pay_b, jnp.logical_not(even))):
        pay[0:WIDE] = wb[pl.ds(jnp.where(right, nb - WIDE, 0), WIDE)]
        edge = v0[pl.ds(jnp.where(right, nb - HALO, 0), HALO)]
        top = edge.astype(jnp.bfloat16)
        pay[WIDE : WIDE + HALO] = top
        pay[WIDE + HALO : WIDE + 2 * HALO] = (edge - top.astype(jnp.float32)).astype(jnp.bfloat16)


def inner01_kernel(members, unroll, *refs):
    pieces = refs[:members]
    wb, v0, b1, quad, unit1, flow, ids, growth, prec, obs, anc, rain, flow_a, flow_b = refs[members : members + 14]
    r1, wb1, v1, b2, w2, ws, bs, v2, miss, turn_a, turn_b = refs[members + 14 :]
    nb, slots = wb.shape[:2]
    part = rain.shape[1]
    quads = nb // 4
    scale = unit1[...]
    base = lax.axis_index("tile") * nb

    def wet_day(m, carry):
        got = decode(quad[...], pieces, lanes(m, 3 * quads * BLK))
        for q in range(4):
            r1[m + q * quads] = got[q * slots : (q + 1) * slots] * scale
        return carry

    run(0, quads, unroll, wet_day, 0)

    def day0(n, acc):
        w = v0[n] + flux_of((wb[n], wb[ids[1, n] - base], wb[ids[2, n] - base]), flow[n])
        wb1[n - HALO] = w.astype(jnp.bfloat16)
        b, v, acc = settle(n, w, b1, r1, growth, prec, obs, acc)
        b2[n - HALO] = b
        v1[n - HALO] = v
        return acc

    miss[...] = run(HALO, nb - HALO, unroll, day0, jnp.zeros((slots, BLK), jnp.float32))
    base = base + HALO

    def day1(n, carry):
        w2[n - WIDE] = v1[n - HALO] + flux_of((wb1[n - HALO], wb1[ids[1, n] - base], wb1[ids[2, n] - base]), flow[n])
        return carry

    run(WIDE, nb - WIDE, unroll, day1, 0)
    picks = ancestors_of(anc, part)

    def pick(n, carry):
        m = n - WIDE
        choose(picks, w2.at[m], b2.at[n - HALO], rain[0, :, lanes(n)], ws.at[m], bs.at[m], v2.at[m])
        return carry

    run(WIDE, nb - WIDE, unroll, pick, 0)
    for raw, turned in ((flow_a, turn_a), (flow_b, turn_b)):
        for at in range(0, HALO * NBR * BLK, BLK):
            turned[at : at + BLK, :] = raw[at : at + BLK, :].T
        turned[HALO * NBR * BLK :, :] = raw[HALO * NBR * BLK :, :]


def settle(n, w, b1, r1, growth, prec, obs, acc):
    s = wetness(w)
    row = pl.ds(n, 1)
    b = b1[n]
    v = w + r1[n] - 0.2 * b * s
    b = b + growth[row, :] * b * (s - 0.4 * b)
    off = b - obs[1:2, lanes(n)]
    return b, v, acc + prec[row, :] * (off * off)


def ancestors_of(anc, part):
    return [anc[1, lax.axis_index("particle") * part + i] for i in range(part)]


def choose(picks, w2, b2, rain, ws, bs, v2):
    for i, p in enumerate(picks):
        ws[i : i + 1, :] = w2[pl.ds(p, 1), :]
        bs[i : i + 1, :] = b2[pl.ds(p, 1), :]
    w = ws[...]
    v2[...] = w + rain - 0.2 * bs[...] * wetness(w)


def outer01_kernel(
    unroll, wb, v0, b1, r1, wb1, v1, b2, wi, bi, vi, miss0, miss1, got_a, got_b, flow, flow_a, flow_b, ids,
    growth, prec, obs, anc, rain, b2_out, w2_out, ws, bs, v2, total, pay_a, pay_b, ext, ext1, v1_out,
):
    nb, slots = wb.shape[:2]
    part = rain.shape[1]
    pos = lax.axis_index("tile")
    even = right_first()
    lows, highs = (0, WIDE + HALO), (nb - WIDE - HALO, nb)
    for lo, hi in (lows, highs):
        ext[WIDE + lo : WIDE + hi] = wb[lo:hi]
    ext1[WIDE : 2 * WIDE] = wb1[0:WIDE]
    ext1[nb - WIDE : nb] = wb1[nb - 2 * HALO - WIDE : nb - 2 * HALO]
    sides = ((got_a, flow_a, even), (got_b, flow_b, jnp.logical_not(even)))
    for got, _, right in sides:
        ext[pl.ds(jnp.where(right, nb + WIDE, 0), WIDE)] = got[0:WIDE]
    base = WIDE - pos * nb

    def day0(n, acc):
        w = v0[n] + flux_of((ext[n + WIDE], ext[ids[1, n] + base], ext[ids[2, n] + base]), flow[n])
        ext1[n + HALO] = w.astype(jnp.bfloat16)
        b, v, acc = settle(n, w, b1, r1, growth, prec, obs, acc)
        m = n if n < HALO else n - (nb - 2 * HALO)
        b2_out[m] = b
        v1_out[m] = v
        return acc

    acc = miss1[...]
    for n in (*range(HALO), *range(nb - HALO, nb)):
        acc = day0(n, acc)
    total[0:slots, :] = miss0[...]
    total[slots : 2 * slots, :] = acc
    for got, pay, right in sides:
        spot = jnp.where(right, nb + HALO, 0)
        for m in range(HALO):
            edge = got[WIDE + m].astype(jnp.float32) + got[WIDE + HALO + m].astype(jnp.float32)
            ext1[spot + m] = (edge + halo_flux(ext, pay, right, nb, m)).astype(jnp.bfloat16)
    base = HALO - pos * nb
    picks = ancestors_of(anc, part)
    ws[WIDE : nb - WIDE] = wi[...]
    bs[WIDE : nb - WIDE] = bi[...]
    v2[WIDE : nb - WIDE] = vi[...]
    for n in (*range(WIDE), *range(nb - WIDE, nb)):
        m = n if n < WIDE else n - (nb - 2 * WIDE)
        if n < HALO or n >= nb - HALO:
            at = n if n < HALO else n - (nb - 2 * HALO)
            v, b = v1_out[at], b2_out.at[at]
        else:
            v, b = v1[n - HALO], b2.at[n - HALO]
        w2_out[m] = v + flux_of((ext1[n + HALO], ext1[ids[1, n] + base], ext1[ids[2, n] + base]), flow[n])
        choose(picks, w2_out.at[m], b, rain[0, :, lanes(n)], ws.at[n], bs.at[n], v2.at[n])
    for pay, right in ((pay_a, even), (pay_b, jnp.logical_not(even))):
        for m in range(WIDE):
            pay[m * part : (m + 1) * part, :] = ws[jnp.where(right, nb - WIDE, 0) + m]
        for m in range(HALO):
            pay[(WIDE + m) * part : (WIDE + m + 1) * part, :] = v2[jnp.where(right, nb - HALO, 0) + m]
    at = (WIDE + HALO) * part
    pay_a[at : at + 2 * slots, :] = total[...]


def final(n, w3, flux, w, b, growth, rain):
    g = growth[pl.ds(n, 1), :]
    b = b + g * b * (wetness(w) - 0.4 * b)
    s = wetness(w3)
    return w3 + flux + rain[1, :, lanes(n)] - 0.2 * b * s, b + g * b * (s - 0.4 * b)


def close_kernel(
    unroll, ws, bs, v2, got_a, got_b, flow, flow_a, flow_b, ids, growth, rain, bio_out, wat_out, ext, ext3
):
    nb, part = ws.shape[:2]
    pos = lax.axis_index("tile")
    even = right_first()
    half = jnp.bfloat16
    ext[WIDE : WIDE + nb] = ws[...]
    sides = ((got_a, flow_a, even), (got_b, flow_b, jnp.logical_not(even)))
    for got, _, right in sides:
        for m in range(WIDE):
            ext[jnp.where(right, nb + WIDE, 0) + m] = got[m * part : (m + 1) * part, :]
    for got, pay, right in sides:
        spot = jnp.where(right, nb + HALO, 0)
        for m in range(HALO):
            edge = got[(WIDE + m) * part : (WIDE + m + 1) * part, :]
            ext3[spot + m] = edge + halo_flux(ext, pay, right, nb, m)

    def near(ref, n, at):
        base = at - pos * nb
        return [ref[i].astype(half) for i in (n + at, ids[1, n] + base, ids[2, n] + base)]

    def day2(n, carry):
        ext3[n + HALO] = v2[n] + flux_of(near(ext, n, WIDE), flow[n])
        return carry

    run(0, nb, unroll, day2, 0)

    def day3(n, carry):
        flux = flux_of(near(ext3, n, HALO), flow[n])
        wat_out[:, lanes(n)], bio_out[:, lanes(n)] = final(n, ext3[n + HALO], flux, ws[n], bs[n], growth, rain)
        return carry

    run(0, nb, unroll, day3, 0)


def means_kernel(unroll, count, *refs):
    bq, wq, b2, w2, b2_edge, w2_edge, means = refs[count:]
    nb, slots = bq.shape[:2]
    level = [ref[...] for ref in refs[:count]]
    while len(level) > 1:
        level = [a + b for a, b in zip(level[::2], level[1::2])]
    lw = -0.5 * jnp.sum(level[0], axis=1, keepdims=True)
    weights = []
    for c in range(CYCLES):
        x = lw[c * slots : (c + 1) * slots]
        e = jnp.exp(x - jnp.max(x, axis=0, keepdims=True))
        weights.append(jnp.broadcast_to(e / jnp.sum(e, axis=0, keepdims=True), (slots, BLK)))

    def mean(c, f, n, x):
        means[c, f : f + 1, lanes(n)] = jnp.sum(weights[c] * x, axis=0, keepdims=True)

    def fill(c, f, ref, first, last, shift):
        def step(n, carry):
            mean(c, f, n, ref[n - shift])
            return carry

        run(first, last, unroll, step, 0)

    fill(0, 0, bq, 0, nb, 0)
    fill(0, 1, wq, 0, nb, 0)
    for f, ref, edge, width in ((0, b2, b2_edge, HALO), (1, w2, w2_edge, WIDE)):
        fill(1, f, ref, width, nb - width, width)
        fill(1, f, edge, 0, width, 0)
        fill(1, f, edge, nb - width, nb, nb - 2 * width)


def weigh(flops):
    return pl.CostEstimate(flops=flops, bytes_accessed=1, transcendentals=0)


def call(kernel, out, specs, scratch=(), cost=1):
    return pl.pallas_call(
        kernel,
        out_shape=tuple(jax.ShapeDtypeStruct(s, d) for s, d in out),
        in_specs=specs,
        out_specs=tuple(VMEM for _ in out),
        scratch_shapes=list(scratch),
        compiler_params=pltpu.CompilerParams(vmem_limit_bytes=32 * 2**20),
        cost_estimate=weigh(cost),
    )


def body(biomass, water, flow_blocks, neighbours, rain, growth_rate, observations, obs_precision, ancestors):
    part, cells = biomass.shape
    nb = cells // BLK
    members, tiles = lax.axis_size("particle"), lax.axis_size("tile")
    slots = members * part
    unroll = slots <= 16
    f32, bf16, i16 = jnp.float32, jnp.bfloat16, jnp.int16
    swap_a = [(i, i ^ 1) for i in range(tiles)]
    swap_b = [(i, (i - 1) % tiles if i % 2 == 0 else (i + 1) % tiles) for i in range(tiles)]
    rows = 4 * part
    neighbours = neighbours.T

    depth = NBR * BLK
    edge = ((HALO * depth + 16, BLK), bf16)
    tile = (HALO, NBR, BLK, BLK)
    wire = pl.pallas_call(
        pack_kernel,
        grid=(1,),
        out_shape=jax.ShapeDtypeStruct((rows, (nb + 1) * BLK), i16),
        in_specs=[pl.BlockSpec((part, cells), lambda i: (0, 0))] * 2
        + [pl.BlockSpec((2, part, cells), lambda i: (0, 0, 0))],
        out_specs=VMEM,
        scratch_shapes=[pltpu.VMEM((rows, cells), f32), pltpu.VMEM((4, rows, BLK), f32)],
        compiler_params=pltpu.CompilerParams(vmem_limit_bytes=60 * 2**20),
        cost_estimate=weigh(1),
    )(biomass, water, rain)
    flow_a, flow_b = pl.pallas_call(
        edge_kernel,
        grid=(1,),
        out_shape=tuple(jax.ShapeDtypeStruct(*edge) for _ in range(2)),
        in_specs=[
            HBM,
            pl.BlockSpec(tile, lambda i: (0, 0, 0, 0)),
            pl.BlockSpec(tile, lambda i: (nb // HALO - 1, 0, 0, 0)),
            SMEM,
        ],
        out_specs=(VMEM, VMEM),
        compiler_params=pltpu.CompilerParams(vmem_limit_bytes=60 * 2**20),
        cost_estimate=weigh(1),
    )(wire, flow_blocks, flow_blocks, neighbours)

    pieces = {0: wire}
    for j in reversed(range(1, members)):
        pieces[j] = lax.ppermute(wire, "particle", [(i, i ^ j) for i in range(members)])
    small = (wire, growth_rate.reshape(nb, BLK), obs_precision.reshape(nb, BLK), observations, ancestors)
    flow, pieces[0], growth, prec, obs, anc, rain23 = call(
        stage_kernel,
        [((nb, depth, BLK), bf16)] + [(x.shape, x.dtype) for x in small] + [((2, part, cells), f32)],
        [HBM] + [VMEM] * 7,
    )(wire, flow_blocks, *small, rain)
    pieces = [pieces[j] for j in range(members)]
    flow_a = lax.ppermute(flow_a, "tile", swap_a)
    flow_b = lax.ppermute(flow_b, "tile", swap_b)

    field = ((nb, slots, BLK), f32)
    wb, v0, b1, bq, wq, miss, quad, unit1, pay_a, pay_b = call(
        functools.partial(open_kernel, members, unroll),
        [((nb, slots, BLK), bf16), field, field, field, field, ((slots, BLK), f32), ((4 * slots, members * rows * 2), bf16), ((slots, BLK), f32)]
        + [((WIDE + 2 * HALO, slots, BLK), bf16)] * 2,
        [VMEM] * (members + 4),
        [
            pltpu.VMEM((8 * slots, members * rows * 2), bf16),
            pltpu.VMEM((6 * slots, members * rows * 2), bf16),
        ],
        cost=10**10,
    )(*pieces, anc, growth, prec, obs)
    got_a = lax.ppermute(pay_a, "tile", swap_a)
    got_b = lax.ppermute(pay_b, "tile", swap_b)
    inner, core = nb - 2 * HALO, nb - 2 * WIDE

    def blocks(count, height=slots, kind=f32):
        return ((count, height, BLK), kind)

    r1, wb1, v1, b2, w2, wi, bi, vi, miss1, turn_a, turn_b = call(
        functools.partial(inner01_kernel, members, unroll),
        [blocks(nb), blocks(inner, kind=bf16), blocks(inner), blocks(inner), blocks(core)]
        + [blocks(core, part)] * 3
        + [((slots, BLK), f32), edge, edge],
        [VMEM] * (members + 6) + [SMEM] + [VMEM] * 3 + [SMEM] + [VMEM] * 3,
    )(
        *pieces, wb, v0, b1, quad, unit1, flow, neighbours, growth, prec, obs, ancestors, rain23, flow_a, flow_b
    )
    swap_rows = (WIDE + HALO) * part
    b2_edge, w2_edge, ws, bs, v2, total, end_a, end_b = call(
        functools.partial(outer01_kernel, unroll),
        [blocks(2 * HALO), blocks(2 * WIDE)]
        + [blocks(nb, part)] * 3
        + [((2 * slots, BLK), f32), ((swap_rows + 2 * slots, BLK), f32), ((swap_rows, BLK), f32)],
        [VMEM] * 17 + [SMEM] + [VMEM] * 3 + [SMEM, VMEM],
        [
            pltpu.VMEM((nb + 2 * WIDE, slots, BLK), bf16),
            pltpu.VMEM((nb + WIDE, slots, BLK), bf16),
            pltpu.VMEM((2 * HALO, slots, BLK), f32),
        ],
    )(
        wb, v0, b1, r1, wb1, v1, b2, wi, bi, vi, miss, miss1, got_a, got_b, flow, turn_a, turn_b, neighbours,
        growth, prec, obs, ancestors, rain23,
    )
    last_a = lax.ppermute(end_a, "tile", swap_a)
    last_b = lax.ppermute(end_b, "tile", swap_b)

    terms = [total, last_a[swap_rows:]]
    span = 2
    while span < tiles:
        total = sum(terms[1:], terms[0])
        masks = [span] if span * 2 >= tiles else [span, 2 * span, 3 * span]
        terms = [total] + [lax.ppermute(total, "tile", [(i, i ^ m) for i in range(tiles)]) for m in masks]
        span *= 2 ** (len(masks) // 2 + 1)
    bio_out, wat_out = call(
        functools.partial(close_kernel, unroll),
        [((part, cells), f32)] * 2,
        [VMEM] * 8 + [SMEM] + [VMEM] * 2,
        [pltpu.VMEM((nb + 2 * WIDE, part, BLK), f32), pltpu.VMEM((nb + WIDE, part, BLK), f32)],
    )(ws, bs, v2, last_a, last_b, flow, turn_a, turn_b, neighbours, growth, rain23)
    (means,) = call(
        functools.partial(means_kernel, unroll, len(terms)), [((CYCLES, 2, cells), f32)], [VMEM] * (len(terms) + 6)
    )(*terms, bq, wq, b2, w2, b2_edge, w2_edge)
    return means, bio_out, wat_out


def solution(mesh):
    placed = (
        P("particle", "tile"),
        P("particle", "tile"),
        P("tile", None, None, None),
        P("tile", None),
        P(None, "particle", "tile"),
        P("tile"),
        P(None, "tile"),
        P("tile"),
        P(),
    )
    return jax.shard_map(
        body,
        mesh=mesh,
        in_specs=placed,
        out_specs=(P(None, None, "tile"), P("particle", "tile"), P("particle", "tile")),
        check_vma=False,
    )
```

```python
import functools

import jax
import jax.numpy as jnp
from jax import lax
from jax.experimental import pallas as pl
from jax.experimental.pallas import tpu as pltpu
from jax.sharding import PartitionSpec as P

BLK = 128
CYCLES = 2
HALO = 4
WIDE = 2 * HALO
NBR = 3
BOUNDS = (2.0, 5.0, 4.0)
SCALE_STEPS = 32000.0
STEPS = 32767.0
VMEM = pl.BlockSpec(memory_space=pltpu.VMEM)
SMEM = pl.BlockSpec(memory_space=pltpu.SMEM)
HBM = pl.BlockSpec(memory_space=pltpu.HBM)


def run(first, last, unroll, step, carry):
    if unroll:
        for n in range(first, last):
            carry = step(n, carry)
        return carry
    return lax.fori_loop(first, last, step, carry)


def lanes(n, at=0):
    if isinstance(n, int):
        return slice(at + n * BLK, at + (n + 1) * BLK)
    return pl.ds(pl.multiple_of(at + n * BLK, BLK), BLK)


def wetness(w):
    sq = w * w
    return sq / (1.0 + sq)


def flux_of(xs, flow):
    return jnp.dot(jnp.concatenate(xs, axis=1), flow, preferred_element_type=jnp.float32)


def right_first():
    return lax.rem(lax.axis_index("tile"), 2) == 0


def pack_kernel(bio, wat, rain, wire, held, factor):
    part, cells = bio.shape
    nb = cells // BLK
    half, quarter = cells // 2, cells // 4
    codes = []
    for f, field in enumerate((bio, wat, rain.at[0], rain.at[1])):
        big = jnp.abs(field[:, 0:BLK])
        for n in range(1, nb):
            big = jnp.maximum(big, jnp.abs(field[:, lanes(n)]))
        unit = BOUNDS[min(f, 2)] / SCALE_STEPS
        code = jnp.floor(jnp.max(big, axis=1, keepdims=True) / unit) + 1.0
        inv = jnp.broadcast_to(STEPS / (code * unit), (part, BLK))
        codes.append(jnp.broadcast_to(code, (part, BLK)))
        if f < 2:
            for h in range(2):
                row = (2 * h + f) * part
                held[row : row + part, 0:half] = field[:, h * half : (h + 1) * half]
                factor[0, row : row + part, :] = inv
        else:
            at = f * quarter
            for q in range(4):
                held[q * part : (q + 1) * part, at : at + quarter] = field[:, q * quarter : (q + 1) * quarter]
                factor[f - 1, q * part : (q + 1) * part, :] = inv
    for f in range(4):
        factor[3, f * part : (f + 1) * part, :] = codes[f]

    def coded(x):
        return jnp.round(x).astype(jnp.int32).astype(jnp.int16)

    pairs, quads = nb // 2, nb // 4
    for n in range(nb):
        wire[:, lanes(n)] = coded(held[:, lanes(n)] * factor[0 if n < pairs else 1 if n < pairs + quads else 2])
    wire[:, lanes(nb)] = coded(factor[3])


def edge_kernel(after, left, right, ids, pay_a, pay_b):
    nb = ids.shape[1]
    even = right_first()
    pos = lax.axis_index("tile")
    line = lax.broadcasted_iota(jnp.int32, (16, BLK), 0)

    def edge(pay, block, start, k):
        away = jnp.zeros((16, BLK), jnp.float32)
        for m in range(HALO):
            pay[m * BLK : (m + 1) * BLK, :] = block[m, 0]
            gap = jnp.abs(ids[k, start + m] - (start + m + pos * nb))
            away = jnp.where(line == m, gap.astype(jnp.float32), away)
        pay[HALO * BLK : HALO * BLK + 16, :] = away.astype(jnp.bfloat16)

    @pl.when(even)
    def _():
        edge(pay_a, right, nb - HALO, 2)
        edge(pay_b, left, 0, 1)

    @pl.when(jnp.logical_not(even))
    def _():
        edge(pay_a, left, 0, 1)
        edge(pay_b, right, nb - HALO, 2)


def stage_kernel(after, flow, wire, growth, prec, obs, anc, rain, ids, turned, *held):
    held, gaps, few_gaps = held[:-2], held[-2], held[-1]
    nb = ids.shape[1]
    pos = lax.axis_index("tile")

    def measure(n, carry):
        for k in range(2):
            gap = jnp.abs(ids[k + 1, n] - (n + pos * nb)).astype(jnp.float32)
            gaps[2 * n + k] = jnp.full(gaps.shape[1:], gap, jnp.float32).astype(jnp.bfloat16)
            few_gaps[2 * n + k] = jnp.full(few_gaps.shape[1:], gap, jnp.float32)
        return carry

    run(0, nb, True, measure, 0)
    for src, dst in zip((wire, growth, prec, obs, anc), held):
        dst[...] = src[...]
    held[-1][...] = rain[2:4]
    for n in range(flow.shape[0]):
        for k in range(NBR):
            turned[n, k * BLK : (k + 1) * BLK, :] = flow[n, k].T


def halo_flux(inside, pay, right, nb, m):
    away = pay[HALO * BLK : HALO * BLK + 16, :].astype(jnp.float32)
    gap = jnp.broadcast_to(away[m : m + 1, :], inside.shape[1:])
    at = jnp.where(right, nb + HALO + m, m)
    x = jnp.zeros(inside.shape[1:], jnp.float32)
    for d in range(1, HALO + 1):
        x = jnp.where(gap == d, inside[at + jnp.where(right, -d, d)].astype(jnp.float32), x)
    return flux_of([x.astype(jnp.bfloat16)], pay[m * BLK : (m + 1) * BLK, :])


def nearby(cells, at, n, gaps):
    xs = [cells[at]]
    for k, sign in enumerate((-1, 1)):
        gap = gaps[2 * n + k]
        x = xs[0]
        for d in range(1, HALO + 1):
            x = jnp.where(gap == d, cells[at + sign * d], x)
        xs.append(x)
    return [x.astype(jnp.bfloat16) for x in xs]


def clear_ends(ref):
    for m in (*range(HALO), *range(ref.shape[0] - HALO, ref.shape[0])):
        ref[m] = jnp.zeros(ref.shape[1:], ref.dtype)


def decode(sel, pieces, cols):
    parts = []
    for ref in pieces:
        q = ref[:, cols].astype(jnp.int32)
        parts.append((q >> 8).astype(jnp.float32).astype(jnp.bfloat16))
        parts.append((q & 255).astype(jnp.float32).astype(jnp.bfloat16))
    return jnp.dot(sel, jnp.concatenate(parts, axis=0), preferred_element_type=jnp.float32)


def open_kernel(members, unroll, *refs):
    pieces = refs[:members]
    anc, growth, prec, obs, flow, gaps = refs[members : members + 6]
    wb, v0, b1, bq, wq, miss, quad, unit1, pay_a, pay_b = refs[members + 6 : members + 16]
    pair, scaler, parts = refs[-3:]
    nb = growth.shape[0]
    slots = anc.shape[1]
    rows = pieces[0].shape[0]
    part = rows // 4
    depth = members * rows * 2
    me = lax.axis_index("particle")
    line = lax.broadcasted_iota(jnp.int32, (slots, slots), 0)
    lane = lax.broadcasted_iota(jnp.int32, (slots, slots), 1)
    first = jnp.broadcast_to(anc[0:1, :], (slots, slots)).astype(jnp.float32)
    chosen = jnp.sum(jnp.where(line == lane, first, 0.0), axis=1, keepdims=True)
    own = lax.broadcasted_iota(jnp.int32, (slots, 1), 0).astype(jnp.float32)
    col = lax.broadcasted_iota(jnp.int32, (slots, depth), 1)
    value = jnp.where((col // rows) % 2 == 0, 256.0, 1.0)
    group = (col % rows) // part
    source = (((col // (2 * rows)) ^ me) * part + col % part).astype(jnp.float32)

    def hits(g, want):
        return jnp.where(jnp.logical_and(group == g, source == want), value, 0.0).astype(jnp.bfloat16)

    for h in range(2):
        for i, want in enumerate((chosen, chosen, own, own)):
            at = (4 * h + i) * slots
            pair[at : at + slots, :] = hits(2 * h + i % 2, want)
    for g in range(4):
        quad[g * slots : (g + 1) * slots, :] = hits(g, own)
    for i, (g, want) in enumerate(((0, chosen), (1, chosen), (0, own), (1, own), (2, own), (3, own))):
        scaler[i * slots : (i + 1) * slots, :] = hits(g, want)

    pairs, quads = nb // 2, nb // 4
    codes = decode(scaler[...], pieces, lanes(nb))
    scale = [
        codes[i * slots : (i + 1) * slots] * (BOUNDS[f] / SCALE_STEPS / STEPS) for i, f in enumerate((0, 1, 0, 1, 2, 2))
    ]
    unit1[...] = scale[5]

    def step(m, acc):
        wet = decode(quad[...], pieces, lanes(m, pairs * BLK))
        for p in range(2):
            got = decode(pair[...], pieces, lanes(m + p * quads))
            for h in range(2):
                q = 2 * h + p
                n = m + q * quads
                b, w, bi, wi = (got[(4 * h + i) * slots : (4 * h + i + 1) * slots] * scale[i] for i in range(4))
                rain0 = wet[q * slots : (q + 1) * slots] * scale[4]
                s = wetness(w)
                row = pl.ds(n, 1)
                wb[n + HALO] = w.astype(jnp.bfloat16)
                v0[n] = w + rain0 - 0.2 * b * s
                b1[n] = b + growth[row, :] * b * (s - 0.4 * b)
                bq[n] = bi
                wq[n] = wi
                off = bi - obs[0:1, lanes(n)]
                acc = acc + prec[row, :] * (off * off)
        return acc

    clear_ends(wb)
    miss[...] = run(0, quads, unroll, step, jnp.zeros((slots, BLK), jnp.float32))
    for m, n in enumerate((*range(HALO), *range(nb - HALO, nb))):
        edge = v0[n] + flux_of(nearby(wb, n + HALO, n, gaps), flow[n])
        top = edge.astype(jnp.bfloat16)
        parts[0, m] = top
        parts[1, m] = (edge - top.astype(jnp.float32)).astype(jnp.bfloat16)
    even = right_first()
    for pay, right in ((pay_a, even), (pay_b, jnp.logical_not(even))):
        pay[0:HALO] = wb[pl.ds(jnp.where(right, nb, HALO), HALO)]
        for i in range(2):
            pay[(i + 1) * HALO : (i + 2) * HALO] = parts[i, pl.ds(jnp.where(right, HALO, 0), HALO)]


def inner01_kernel(members, unroll, *refs):
    pieces = refs[:members]
    wb, v0, b1, quad, unit1, flow, gaps, growth, prec, obs, heirs, rain, flow_a, flow_b = refs[members : members + 14]
    r1, wb1, v1, b2, w2, ws, bs, v2, miss, turn_a, turn_b, anc, sem = refs[members + 14 :]
    early = pltpu.make_async_copy(heirs, anc, sem)
    early.start()
    nb, slots = v0.shape[:2]
    part = rain.shape[1]
    quads = nb // 4
    scale = unit1[...]

    def wet_day(m, carry):
        got = decode(quad[...], pieces, lanes(m, 3 * quads * BLK))
        for q in range(4):
            r1[m + q * quads] = got[q * slots : (q + 1) * slots] * scale
        return carry

    run(0, quads, unroll, wet_day, 0)
    early.wait()

    def day0(n, acc):
        w = v0[n] + flux_of(nearby(wb, n + HALO, n, gaps), flow[n])
        wb1[n - HALO] = w.astype(jnp.bfloat16)
        b, v, acc = settle(n, w, b1, r1, growth, prec, obs, acc)
        b2[n - HALO] = b
        v1[n - HALO] = v
        return acc

    miss[...] = run(HALO, nb - HALO, unroll, day0, jnp.zeros((slots, BLK), jnp.float32))
    def day1(n, carry):
        w2[n - WIDE] = v1[n - HALO] + flux_of(nearby(wb1, n - HALO, n, gaps), flow[n])
        return carry

    run(WIDE, nb - WIDE, unroll, day1, 0)
    picks = ancestors_of(anc, part)

    def pick(n, carry):
        m = n - WIDE
        choose(picks, w2.at[m], b2.at[n - HALO], rain[0, :, lanes(n)], ws.at[m], bs.at[m], v2.at[m])
        return carry

    run(WIDE, nb - WIDE, unroll, pick, 0)
    for raw, turned in ((flow_a, turn_a), (flow_b, turn_b)):
        for at in range(0, HALO * BLK, BLK):
            turned[at : at + BLK, :] = raw[at : at + BLK, :].T
        turned[HALO * BLK :, :] = raw[HALO * BLK :, :]


def settle(n, w, b1, r1, growth, prec, obs, acc):
    s = wetness(w)
    row = pl.ds(n, 1)
    b = b1[n]
    v = w + r1[n] - 0.2 * b * s
    b = b + growth[row, :] * b * (s - 0.4 * b)
    off = b - obs[1:2, lanes(n)]
    return b, v, acc + prec[row, :] * (off * off)


def ancestors_of(anc, part):
    return [anc[1, lax.axis_index("particle") * part + i] for i in range(part)]


def choose(picks, w2, b2, rain, ws, bs, v2):
    for i, p in enumerate(picks):
        ws[i : i + 1, :] = w2[pl.ds(p, 1), :]
        bs[i : i + 1, :] = b2[pl.ds(p, 1), :]
    w = ws[...]
    v2[...] = w + rain - 0.2 * bs[...] * wetness(w)


def outer01_kernel(
    unroll, wb, v0, b1, r1, wb1, v1, b2, wi, bi, vi, miss0, miss1, got_a, got_b, flow, flow_a, flow_b, gaps, few_gaps,
    growth, prec, obs, heirs, rain, b2_out, w2_out, ws, bs, v2, total, pay_a, pay_b, ext, ext1, v1_out, anc, sem, parts,
):
    early = pltpu.make_async_copy(heirs, anc, sem)
    early.start()
    nb, slots = v0.shape[:2]
    part = rain.shape[1]
    even = right_first()
    for lo, hi in ((0, WIDE), (nb - WIDE, nb)):
        ext[HALO + lo : HALO + hi] = wb[HALO + lo : HALO + hi]
    ext1[WIDE : 2 * WIDE] = wb1[0:WIDE]
    ext1[nb - WIDE : nb] = wb1[nb - 2 * HALO - WIDE : nb - 2 * HALO]
    sides = ((got_a, flow_a, even), (got_b, flow_b, jnp.logical_not(even)))
    for got, _, right in sides:
        ext[pl.ds(jnp.where(right, nb + HALO, 0), HALO)] = got[0:HALO]
    for got, pay, right in sides:
        spot = jnp.where(right, nb + HALO, 0)
        for m in range(HALO):
            edge = got[HALO + m].astype(jnp.float32) + got[2 * HALO + m].astype(jnp.float32)
            ext1[spot + m] = (edge + halo_flux(wb, pay, right, nb, m)).astype(jnp.bfloat16)
    early.wait()
    def day0(n, acc):
        w = v0[n] + flux_of(nearby(ext, n + HALO, n, gaps), flow[n])
        ext1[n + HALO] = w.astype(jnp.bfloat16)
        b, v, acc = settle(n, w, b1, r1, growth, prec, obs, acc)
        m = n if n < HALO else n - (nb - 2 * HALO)
        b2_out[m] = b
        v1_out[m] = v
        return acc

    acc = miss1[...]
    for n in (*range(HALO), *range(nb - HALO, nb)):
        acc = day0(n, acc)
    total[0:slots, :] = miss0[...]
    total[slots : 2 * slots, :] = acc
    picks = ancestors_of(anc, part)
    clear_ends(ws)
    ws[HALO + WIDE : HALO + nb - WIDE] = wi[...]
    bs[WIDE : nb - WIDE] = bi[...]
    v2[WIDE : nb - WIDE] = vi[...]
    for n in (*range(WIDE), *range(nb - WIDE, nb)):
        m = n if n < WIDE else n - (nb - 2 * WIDE)
        if n < HALO or n >= nb - HALO:
            at = n if n < HALO else n - (nb - 2 * HALO)
            v, b = v1_out[at], b2_out.at[at]
        else:
            v, b = v1[n - HALO], b2.at[n - HALO]
        w2_out[m] = v + flux_of(nearby(ext1, n + HALO, n, gaps), flow[n])
        choose(picks, w2_out.at[m], b, rain[0, :, lanes(n)], ws.at[n + HALO], bs.at[n], v2.at[n])
    for m, n in enumerate((*range(HALO), *range(nb - HALO, nb))):
        parts[m] = v2[n] + flux_of(nearby(ws, n + HALO, n, few_gaps), flow[n])
    for pay, right in ((pay_a, even), (pay_b, jnp.logical_not(even))):
        for m in range(HALO):
            pay[m * part : (m + 1) * part, :] = ws[jnp.where(right, nb, HALO) + m]
            pay[(HALO + m) * part : (HALO + m + 1) * part, :] = parts[jnp.where(right, HALO, 0) + m]
    at = 2 * HALO * part
    pay_a[at : at + 2 * slots, :] = total[...]


def final(n, w3, flux, w, b, growth, rain):
    g = growth[pl.ds(n, 1), :]
    b = b + g * b * (wetness(w) - 0.4 * b)
    s = wetness(w3)
    return w3 + flux + rain[1, :, lanes(n)] - 0.2 * b * s, b + g * b * (s - 0.4 * b)


def close_kernel(
    unroll, ws, bs, v2, got_a, got_b, flow, flow_a, flow_b, gaps, growth, rain, bio_out, wat_out, ext, ext3
):
    nb, part = bs.shape[:2]
    even = right_first()
    ext[HALO : HALO + nb] = ws[HALO : HALO + nb]
    sides = ((got_a, flow_a, even), (got_b, flow_b, jnp.logical_not(even)))
    for got, _, right in sides:
        for m in range(HALO):
            ext[jnp.where(right, nb + HALO, 0) + m] = got[m * part : (m + 1) * part, :]
    for got, pay, right in sides:
        spot = jnp.where(right, nb + HALO, 0)
        for m in range(HALO):
            edge = got[(HALO + m) * part : (HALO + m + 1) * part, :]
            ext3[spot + m] = edge + halo_flux(ws, pay, right, nb, m)

    def day2(n, carry):
        ext3[n + HALO] = v2[n] + flux_of(nearby(ext, n + HALO, n, gaps), flow[n])
        return carry

    run(0, nb, unroll, day2, 0)

    def day3(n, carry):
        flux = flux_of(nearby(ext3, n + HALO, n, gaps), flow[n])
        wat_out[:, lanes(n)], bio_out[:, lanes(n)] = final(n, ext3[n + HALO], flux, ws[n + HALO], bs[n], growth, rain)
        return carry

    run(0, nb, unroll, day3, 0)


def means_kernel(unroll, count, *refs):
    bq, wq, b2, w2, b2_edge, w2_edge, means = refs[count:]
    nb, slots = bq.shape[:2]
    level = [ref[...] for ref in refs[:count]]
    while len(level) > 1:
        level = [a + b for a, b in zip(level[::2], level[1::2])]
    lw = -0.5 * jnp.sum(level[0], axis=1, keepdims=True)
    weights = []
    for c in range(CYCLES):
        x = lw[c * slots : (c + 1) * slots]
        e = jnp.exp(x - jnp.max(x, axis=0, keepdims=True))
        weights.append(jnp.broadcast_to(e / jnp.sum(e, axis=0, keepdims=True), (slots, BLK)))

    def mean(c, f, n, x):
        means[c, f : f + 1, lanes(n)] = jnp.sum(weights[c] * x, axis=0, keepdims=True)

    def fill(c, f, ref, first, last, shift):
        def step(n, carry):
            mean(c, f, n, ref[n - shift])
            return carry

        run(first, last, unroll, step, 0)

    fill(0, 0, bq, 0, nb, 0)
    fill(0, 1, wq, 0, nb, 0)
    for f, ref, edge, width in ((0, b2, b2_edge, HALO), (1, w2, w2_edge, WIDE)):
        fill(1, f, ref, width, nb - width, width)
        fill(1, f, edge, 0, width, 0)
        fill(1, f, edge, nb - width, nb, nb - 2 * width)


def weigh(flops):
    return pl.CostEstimate(flops=flops, bytes_accessed=1, transcendentals=0)


def call(kernel, out, specs, scratch=(), cost=1):
    return pl.pallas_call(
        kernel,
        out_shape=tuple(jax.ShapeDtypeStruct(s, d) for s, d in out),
        in_specs=specs,
        out_specs=tuple(VMEM for _ in out),
        scratch_shapes=list(scratch),
        compiler_params=pltpu.CompilerParams(vmem_limit_bytes=32 * 2**20),
        cost_estimate=weigh(cost),
    )


def body(biomass, water, flow_blocks, neighbours, rain, growth_rate, observations, obs_precision, ancestors):
    part, cells = biomass.shape
    nb = cells // BLK
    members, tiles = lax.axis_size("particle"), lax.axis_size("tile")
    slots = members * part
    unroll = slots <= 16
    f32, bf16, i16 = jnp.float32, jnp.bfloat16, jnp.int16
    swap_a = [(i, i ^ 1) for i in range(tiles)]
    swap_b = [(i, (i - 1) % tiles if i % 2 == 0 else (i + 1) % tiles) for i in range(tiles)]
    rows = 4 * part
    neighbours = neighbours.T

    depth = NBR * BLK
    edge = ((HALO * BLK + 16, BLK), bf16)
    tile = (HALO, 1, BLK, BLK)
    wire = pl.pallas_call(
        pack_kernel,
        grid=(1,),
        out_shape=jax.ShapeDtypeStruct((rows, (nb + 1) * BLK), i16),
        in_specs=[pl.BlockSpec((part, cells), lambda i: (0, 0))] * 2
        + [pl.BlockSpec((2, part, cells), lambda i: (0, 0, 0))],
        out_specs=VMEM,
        scratch_shapes=[pltpu.VMEM((rows, cells), f32), pltpu.VMEM((4, rows, BLK), f32)],
        compiler_params=pltpu.CompilerParams(vmem_limit_bytes=60 * 2**20),
        cost_estimate=weigh(1),
    )(biomass, water, rain)
    flow_a, flow_b = pl.pallas_call(
        edge_kernel,
        grid=(1,),
        out_shape=tuple(jax.ShapeDtypeStruct(*edge) for _ in range(2)),
        in_specs=[
            HBM,
            pl.BlockSpec(tile, lambda i: (0, 1, 0, 0)),
            pl.BlockSpec(tile, lambda i: (nb // HALO - 1, 2, 0, 0)),
            SMEM,
        ],
        out_specs=(VMEM, VMEM),
        compiler_params=pltpu.CompilerParams(vmem_limit_bytes=60 * 2**20),
        cost_estimate=weigh(1),
    )(wire, flow_blocks, flow_blocks, neighbours)

    def over(x, j):
        return lax.ppermute(x, "particle", [(i, i ^ j) for i in range(members)])

    pieces = {j: over(wire, j) for j in range(members - 2, 0, -2)}
    pieces[1] = over(wire, 1)
    pieces[0] = wire
    for j in range(3, members, 2):
        got, flow_a = lax.optimization_barrier((pieces[j - 1], flow_a))
        pieces[j] = over(got, 1)
    small = (wire, growth_rate.reshape(nb, BLK), obs_precision.reshape(nb, BLK), observations, ancestors)
    flow, pieces[0], growth, prec, obs, anc, rain23, gaps, few_gaps = call(
        stage_kernel,
        [((nb, depth, BLK), bf16)]
        + [(x.shape, x.dtype) for x in small]
        + [((2, part, cells), f32), ((2 * nb, slots, BLK), bf16), ((2 * nb, part, BLK), f32)],
        [HBM] + [VMEM] * 7 + [SMEM],
    )(wire, flow_blocks, *small, rain, neighbours)
    pieces = [pieces[j] for j in range(members)]
    flow_a = lax.ppermute(flow_a, "tile", swap_a)
    flow_b = lax.ppermute(flow_b, "tile", swap_b)

    field = ((nb, slots, BLK), f32)
    wb, v0, b1, bq, wq, miss, quad, unit1, pay_a, pay_b = call(
        functools.partial(open_kernel, members, unroll),
        [((nb + 2 * HALO, slots, BLK), bf16), field, field, field, field, ((slots, BLK), f32), ((4 * slots, members * rows * 2), bf16), ((slots, BLK), f32)]
        + [((3 * HALO, slots, BLK), bf16)] * 2,
        [VMEM] * (members + 6),
        [
            pltpu.VMEM((8 * slots, members * rows * 2), bf16),
            pltpu.VMEM((6 * slots, members * rows * 2), bf16),
            pltpu.VMEM((2, 2 * HALO, slots, BLK), bf16),
        ],
        cost=10**10,
    )(*pieces, anc, growth, prec, obs, flow, gaps)
    got_a = lax.ppermute(pay_a, "tile", swap_a)
    got_b = lax.ppermute(pay_b, "tile", swap_b)
    inner, core = nb - 2 * HALO, nb - 2 * WIDE
    indices = [
        pltpu.SMEM(ancestors.shape, jnp.int32),
        pltpu.SemaphoreType.DMA,
    ]

    def blocks(count, height=slots, kind=f32):
        return ((count, height, BLK), kind)

    r1, wb1, v1, b2, w2, wi, bi, vi, miss1, turn_a, turn_b = call(
        functools.partial(inner01_kernel, members, unroll),
        [blocks(nb), blocks(inner, kind=bf16), blocks(inner), blocks(inner), blocks(core)]
        + [blocks(core, part)] * 3
        + [((slots, BLK), f32), edge, edge],
        [VMEM] * (members + 14),
        indices,
    )(
        *pieces, wb, v0, b1, quad, unit1, flow, gaps, growth, prec, obs, anc, rain23, flow_a, flow_b
    )
    swap_rows = 2 * HALO * part
    b2_edge, w2_edge, ws, bs, v2, total, end_a, end_b = call(
        functools.partial(outer01_kernel, unroll),
        [blocks(2 * HALO), blocks(2 * WIDE)]
        + [blocks(nb + 2 * HALO, part), blocks(nb, part), blocks(nb, part)]
        + [((2 * slots, BLK), f32), ((swap_rows + 2 * slots, BLK), f32), ((swap_rows, BLK), f32)],
        [VMEM] * 24,
        [
            pltpu.VMEM((nb + 2 * HALO, slots, BLK), bf16),
            pltpu.VMEM((nb + 2 * HALO, slots, BLK), bf16),
            pltpu.VMEM((2 * HALO, slots, BLK), f32),
        ]
        + indices
        + [pltpu.VMEM((2 * HALO, part, BLK), f32)],
    )(
        wb, v0, b1, r1, wb1, v1, b2, wi, bi, vi, miss, miss1, got_a, got_b, flow, turn_a, turn_b, gaps, few_gaps,
        growth, prec, obs, anc, rain23,
    )
    last_a = lax.ppermute(end_a, "tile", swap_a)
    last_b = lax.ppermute(end_b, "tile", swap_b)

    terms = [total, last_a[swap_rows:]]
    span = 2
    while span < tiles:
        total = sum(terms[1:], terms[0])
        masks = [span] if span * 2 >= tiles else [span, 2 * span, 3 * span]
        terms = [total] + [lax.ppermute(total, "tile", [(i, i ^ m) for i in range(tiles)]) for m in masks]
        span *= 2 ** (len(masks) // 2 + 1)
    bio_out, wat_out = call(
        functools.partial(close_kernel, unroll),
        [((part, cells), f32)] * 2,
        [VMEM] * 11,
        [pltpu.VMEM((nb + 2 * HALO, part, BLK), f32)] * 2,
    )(ws, bs, v2, last_a, last_b, flow, turn_a, turn_b, few_gaps, growth, rain23)
    (means,) = call(
        functools.partial(means_kernel, unroll, len(terms)), [((CYCLES, 2, cells), f32)], [VMEM] * (len(terms) + 6)
    )(*terms, bq, wq, b2, w2, b2_edge, w2_edge)
    return means, bio_out, wat_out


def solution(mesh):
    placed = (
        P("particle", "tile"),
        P("particle", "tile"),
        P("tile", None, None, None),
        P("tile", None),
        P(None, "particle", "tile"),
        P("tile"),
        P(None, "tile"),
        P("tile"),
        P(),
    )
    return jax.shard_map(
        body,
        mesh=mesh,
        in_specs=placed,
        out_specs=(P(None, None, "tile"), P("particle", "tile"), P("particle", "tile")),
        check_vma=False,
    )
```

```python
import functools

import jax
import jax.numpy as jnp
from jax import lax
from jax.experimental import pallas as pl
from jax.experimental.pallas import tpu as pltpu
from jax.sharding import PartitionSpec as P

BLK = 128
CYCLES = 2
HALO = 4
WIDE = 2 * HALO
NBR = 3
BOUNDS = (2.0, 5.0, 4.0)
SCALE_STEPS = 32000.0
STEPS = 32767.0
VMEM = pl.BlockSpec(memory_space=pltpu.VMEM)
SMEM = pl.BlockSpec(memory_space=pltpu.SMEM)
HBM = pl.BlockSpec(memory_space=pltpu.HBM)


def run(first, last, unroll, step, carry):
    if unroll:
        for n in range(first, last):
            carry = step(n, carry)
        return carry
    return lax.fori_loop(first, last, step, carry)


def lanes(n, at=0):
    if isinstance(n, int):
        return slice(at + n * BLK, at + (n + 1) * BLK)
    return pl.ds(pl.multiple_of(at + n * BLK, BLK), BLK)


def wetness(w):
    sq = w * w
    return sq / (1.0 + sq)


def flux_of(xs, flow):
    return jnp.dot(jnp.concatenate(xs, axis=1), flow, preferred_element_type=jnp.float32)


def right_first():
    return lax.rem(lax.axis_index("tile"), 2) == 0


def pack_kernel(bio, wat, rain, wire, early, late, held, factor):
    part, cells = bio.shape
    nb = cells // BLK
    half, quarter = cells // 2, cells // 4
    codes = []
    for f, field in enumerate((bio, wat, rain.at[0], rain.at[1])):
        big = jnp.abs(field[:, 0:BLK])
        for n in range(1, nb):
            big = jnp.maximum(big, jnp.abs(field[:, lanes(n)]))
        unit = BOUNDS[min(f, 2)] / SCALE_STEPS
        code = jnp.floor(jnp.max(big, axis=1, keepdims=True) / unit) + 1.0
        inv = jnp.broadcast_to(STEPS / (code * unit), (part, BLK))
        codes.append(jnp.broadcast_to(code, (part, BLK)))
        if f < 2:
            for h in range(2):
                row = (2 * h + f) * part
                held[row : row + part, 0:half] = field[:, h * half : (h + 1) * half]
                factor[0, row : row + part, :] = inv
        else:
            at = f * quarter
            for q in range(4):
                held[q * part : (q + 1) * part, at : at + quarter] = field[:, q * quarter : (q + 1) * quarter]
                factor[f - 1, q * part : (q + 1) * part, :] = inv
    for f in range(4):
        factor[3, f * part : (f + 1) * part, :] = codes[f]

    def coded(x):
        return jnp.round(x).astype(jnp.int32).astype(jnp.int16)

    pairs, quads = nb // 2, nb // 4
    for n in range(pairs + 1):
        x = coded(factor[3] if n == pairs else held[:, lanes(n)] * factor[0])
        wire[:, lanes(n)] = x
        early[:, lanes(n)] = x
    for n in range(pairs):
        x = coded(held[:, lanes(pairs + n)] * factor[1 if n < quads else 2])
        wire[:, lanes(pairs + 1 + n)] = x
        late[:, lanes(n)] = x


def edge_kernel(after, left, right, ids, pay_a, pay_b):
    nb = ids.shape[1]
    even = right_first()
    pos = lax.axis_index("tile")
    line = lax.broadcasted_iota(jnp.int32, (16, BLK), 0)

    def edge(pay, block, start, k):
        away = jnp.zeros((16, BLK), jnp.float32)
        for m in range(HALO):
            pay[m * BLK : (m + 1) * BLK, :] = block[m, 0]
            gap = jnp.abs(ids[k, start + m] - (start + m + pos * nb))
            away = jnp.where(line == m, gap.astype(jnp.float32), away)
        pay[HALO * BLK : HALO * BLK + 16, :] = away.astype(jnp.bfloat16)

    @pl.when(even)
    def _():
        edge(pay_a, right, nb - HALO, 2)
        edge(pay_b, left, 0, 1)

    @pl.when(jnp.logical_not(even))
    def _():
        edge(pay_a, left, 0, 1)
        edge(pay_b, right, nb - HALO, 2)


def stage_kernel(after, flow, wire, growth, prec, obs, anc, rain, ids, turned, *held):
    held, gaps, few_gaps = held[:-2], held[-2], held[-1]
    nb = ids.shape[1]
    pos = lax.axis_index("tile")

    def measure(n, carry):
        for k in range(2):
            gap = jnp.abs(ids[k + 1, n] - (n + pos * nb)).astype(jnp.float32)
            gaps[2 * n + k] = jnp.full(gaps.shape[1:], gap, jnp.float32).astype(jnp.bfloat16)
            few_gaps[2 * n + k] = jnp.full(few_gaps.shape[1:], gap, jnp.float32)
        return carry

    run(0, nb, True, measure, 0)
    for src, dst in zip((wire, growth, prec, obs, anc), held):
        dst[...] = src[...]
    held[-1][...] = rain[2:4]
    for n in range(flow.shape[0]):
        for k in range(NBR):
            turned[n, k * BLK : (k + 1) * BLK, :] = flow[n, k].T


def halo_flux(inside, pay, right, nb, m):
    away = pay[HALO * BLK : HALO * BLK + 16, :].astype(jnp.float32)
    gap = jnp.broadcast_to(away[m : m + 1, :], inside.shape[1:])
    at = jnp.where(right, nb + HALO + m, m)
    x = jnp.zeros(inside.shape[1:], jnp.float32)
    for d in range(1, HALO + 1):
        x = jnp.where(gap == d, inside[at + jnp.where(right, -d, d)].astype(jnp.float32), x)
    return flux_of([x.astype(jnp.bfloat16)], pay[m * BLK : (m + 1) * BLK, :])


def nearby(cells, at, n, gaps):
    xs = [cells[at]]
    for k, sign in enumerate((-1, 1)):
        gap = gaps[2 * n + k]
        x = xs[0]
        for d in range(1, HALO + 1):
            x = jnp.where(gap == d, cells[at + sign * d], x)
        xs.append(x)
    return [x.astype(jnp.bfloat16) for x in xs]


def clear_ends(ref):
    for m in (*range(HALO), *range(ref.shape[0] - HALO, ref.shape[0])):
        ref[m] = jnp.zeros(ref.shape[1:], ref.dtype)


def decode(sel, pieces, n):
    parts = []
    for ref, first in pieces:
        q = ref[:, lanes(n + first)].astype(jnp.int32)
        parts.append((q >> 8).astype(jnp.float32).astype(jnp.bfloat16))
        parts.append((q & 255).astype(jnp.float32).astype(jnp.bfloat16))
    return jnp.dot(sel, jnp.concatenate(parts, axis=0), preferred_element_type=jnp.float32)


def rain_of(both, others):
    return [(r, (r.shape[1] // BLK + 1) // 2) for r in both] + [(r, 0) for r in others]


def open_kernel(members, unroll, *refs):
    pieces, rains, refs = [(r, 0) for r in refs[:members]], rain_of(refs[:2], refs[members : 2 * members - 2]), refs[members - 2 :]
    anc, growth, prec, obs, flow, gaps = refs[members : members + 6]
    wb, v0, b1, bq, wq, miss, quad, unit1, pay_a, pay_b = refs[members + 6 : members + 16]
    pair, scaler, parts = refs[-3:]
    nb = growth.shape[0]
    slots = anc.shape[1]
    rows = pieces[0][0].shape[0]
    part = rows // 4
    depth = members * rows * 2
    me = lax.axis_index("particle")
    line = lax.broadcasted_iota(jnp.int32, (slots, slots), 0)
    lane = lax.broadcasted_iota(jnp.int32, (slots, slots), 1)
    first = jnp.broadcast_to(anc[0:1, :], (slots, slots)).astype(jnp.float32)
    chosen = jnp.sum(jnp.where(line == lane, first, 0.0), axis=1, keepdims=True)
    own = lax.broadcasted_iota(jnp.int32, (slots, 1), 0).astype(jnp.float32)
    col = lax.broadcasted_iota(jnp.int32, (slots, depth), 1)
    value = jnp.where((col // rows) % 2 == 0, 256.0, 1.0)
    group = (col % rows) // part
    source = (((col // (2 * rows)) ^ me) * part + col % part).astype(jnp.float32)

    def hits(g, want):
        return jnp.where(jnp.logical_and(group == g, source == want), value, 0.0).astype(jnp.bfloat16)

    for h in range(2):
        for i, want in enumerate((chosen, chosen, own, own)):
            at = (4 * h + i) * slots
            pair[at : at + slots, :] = hits(2 * h + i % 2, want)
    for g in range(4):
        quad[g * slots : (g + 1) * slots, :] = hits(g, own)
    for i, (g, want) in enumerate(((0, chosen), (1, chosen), (0, own), (1, own), (2, own), (3, own))):
        scaler[i * slots : (i + 1) * slots, :] = hits(g, want)

    pairs, quads = nb // 2, nb // 4
    codes = decode(scaler[...], pieces, pairs)
    scale = [
        codes[i * slots : (i + 1) * slots] * (BOUNDS[f] / SCALE_STEPS / STEPS) for i, f in enumerate((0, 1, 0, 1, 2, 2))
    ]
    unit1[...] = scale[5]

    def step(m, acc):
        wet = decode(quad[...], rains, m)
        for p in range(2):
            got = decode(pair[...], pieces, m + p * quads)
            for h in range(2):
                q = 2 * h + p
                n = m + q * quads
                b, w, bi, wi = (got[(4 * h + i) * slots : (4 * h + i + 1) * slots] * scale[i] for i in range(4))
                rain0 = wet[q * slots : (q + 1) * slots] * scale[4]
                s = wetness(w)
                row = pl.ds(n, 1)
                wb[n + HALO] = w.astype(jnp.bfloat16)
                v0[n] = w + rain0 - 0.2 * b * s
                b1[n] = b + growth[row, :] * b * (s - 0.4 * b)
                bq[n] = bi
                wq[n] = wi
                off = bi - obs[0:1, lanes(n)]
                acc = acc + prec[row, :] * (off * off)
        return acc

    clear_ends(wb)
    miss[...] = run(0, quads, unroll, step, jnp.zeros((slots, BLK), jnp.float32))
    for m, n in enumerate((*range(HALO), *range(nb - HALO, nb))):
        edge = v0[n] + flux_of(nearby(wb, n + HALO, n, gaps), flow[n])
        top = edge.astype(jnp.bfloat16)
        parts[0, m] = top
        parts[1, m] = (edge - top.astype(jnp.float32)).astype(jnp.bfloat16)
    even = right_first()
    for pay, right in ((pay_a, even), (pay_b, jnp.logical_not(even))):
        pay[0:HALO] = wb[pl.ds(jnp.where(right, nb, HALO), HALO)]
        for i in range(2):
            pay[(i + 1) * HALO : (i + 2) * HALO] = parts[i, pl.ds(jnp.where(right, HALO, 0), HALO)]


def inner01_kernel(members, unroll, *refs):
    pieces = rain_of(refs[:2], refs[2:members])
    wb, v0, b1, quad, unit1, flow, gaps, growth, prec, obs, heirs, rain, flow_a, flow_b = refs[members : members + 14]
    r1, wb1, v1, b2, w2, ws, bs, v2, miss, turn_a, turn_b, anc, sem = refs[members + 14 :]
    early = pltpu.make_async_copy(heirs, anc, sem)
    early.start()
    nb, slots = v0.shape[:2]
    part = rain.shape[1]
    quads = nb // 4
    scale = unit1[...]

    def wet_day(m, carry):
        got = decode(quad[...], pieces, m + quads)
        for q in range(4):
            r1[m + q * quads] = got[q * slots : (q + 1) * slots] * scale
        return carry

    run(0, quads, unroll, wet_day, 0)
    early.wait()

    def day0(n, acc):
        w = v0[n] + flux_of(nearby(wb, n + HALO, n, gaps), flow[n])
        wb1[n - HALO] = w.astype(jnp.bfloat16)
        b, v, acc = settle(n, w, b1, r1, growth, prec, obs, acc)
        b2[n - HALO] = b
        v1[n - HALO] = v
        return acc

    miss[...] = run(HALO, nb - HALO, unroll, day0, jnp.zeros((slots, BLK), jnp.float32))
    def day1(n, carry):
        w2[n - WIDE] = v1[n - HALO] + flux_of(nearby(wb1, n - HALO, n, gaps), flow[n])
        return carry

    run(WIDE, nb - WIDE, unroll, day1, 0)
    picks = ancestors_of(anc, part)

    def pick(n, carry):
        m = n - WIDE
        choose(picks, w2.at[m], b2.at[n - HALO], rain[0, :, lanes(n)], ws.at[m], bs.at[m], v2.at[m])
        return carry

    run(WIDE, nb - WIDE, unroll, pick, 0)
    for raw, turned in ((flow_a, turn_a), (flow_b, turn_b)):
        for at in range(0, HALO * BLK, BLK):
            turned[at : at + BLK, :] = raw[at : at + BLK, :].T
        turned[HALO * BLK :, :] = raw[HALO * BLK :, :]


def settle(n, w, b1, r1, growth, prec, obs, acc):
    s = wetness(w)
    row = pl.ds(n, 1)
    b = b1[n]
    v = w + r1[n] - 0.2 * b * s
    b = b + growth[row, :] * b * (s - 0.4 * b)
    off = b - obs[1:2, lanes(n)]
    return b, v, acc + prec[row, :] * (off * off)


def ancestors_of(anc, part):
    return [anc[1, lax.axis_index("particle") * part + i] for i in range(part)]


def choose(picks, w2, b2, rain, ws, bs, v2):
    for i, p in enumerate(picks):
        ws[i : i + 1, :] = w2[pl.ds(p, 1), :]
        bs[i : i + 1, :] = b2[pl.ds(p, 1), :]
    w = ws[...]
    v2[...] = w + rain - 0.2 * bs[...] * wetness(w)


def outer01_kernel(
    unroll, wb, v0, b1, r1, wb1, v1, b2, wi, bi, vi, miss0, miss1, got_a, got_b, flow, flow_a, flow_b, gaps, few_gaps,
    growth, prec, obs, heirs, rain, b2_out, w2_out, ws, bs, v2, total, pay_a, pay_b, ext, ext1, v1_out, anc, sem, parts,
):
    early = pltpu.make_async_copy(heirs, anc, sem)
    early.start()
    nb, slots = v0.shape[:2]
    part = rain.shape[1]
    even = right_first()
    for lo, hi in ((0, WIDE), (nb - WIDE, nb)):
        ext[HALO + lo : HALO + hi] = wb[HALO + lo : HALO + hi]
    ext1[WIDE : 2 * WIDE] = wb1[0:WIDE]
    ext1[nb - WIDE : nb] = wb1[nb - 2 * HALO - WIDE : nb - 2 * HALO]
    sides = ((got_a, flow_a, even), (got_b, flow_b, jnp.logical_not(even)))
    for got, _, right in sides:
        ext[pl.ds(jnp.where(right, nb + HALO, 0), HALO)] = got[0:HALO]
    for got, pay, right in sides:
        spot = jnp.where(right, nb + HALO, 0)
        for m in range(HALO):
            edge = got[HALO + m].astype(jnp.float32) + got[2 * HALO + m].astype(jnp.float32)
            ext1[spot + m] = (edge + halo_flux(wb, pay, right, nb, m)).astype(jnp.bfloat16)
    early.wait()
    def day0(n, acc):
        w = v0[n] + flux_of(nearby(ext, n + HALO, n, gaps), flow[n])
        ext1[n + HALO] = w.astype(jnp.bfloat16)
        b, v, acc = settle(n, w, b1, r1, growth, prec, obs, acc)
        m = n if n < HALO else n - (nb - 2 * HALO)
        b2_out[m] = b
        v1_out[m] = v
        return acc

    acc = miss1[...]
    for n in (*range(HALO), *range(nb - HALO, nb)):
        acc = day0(n, acc)
    total[0:slots, :] = miss0[...]
    total[slots : 2 * slots, :] = acc
    picks = ancestors_of(anc, part)
    clear_ends(ws)
    ws[HALO + WIDE : HALO + nb - WIDE] = wi[...]
    bs[WIDE : nb - WIDE] = bi[...]
    v2[WIDE : nb - WIDE] = vi[...]
    for n in (*range(WIDE), *range(nb - WIDE, nb)):
        m = n if n < WIDE else n - (nb - 2 * WIDE)
        if n < HALO or n >= nb - HALO:
            at = n if n < HALO else n - (nb - 2 * HALO)
            v, b = v1_out[at], b2_out.at[at]
        else:
            v, b = v1[n - HALO], b2.at[n - HALO]
        w2_out[m] = v + flux_of(nearby(ext1, n + HALO, n, gaps), flow[n])
        choose(picks, w2_out.at[m], b, rain[0, :, lanes(n)], ws.at[n + HALO], bs.at[n], v2.at[n])
    for m, n in enumerate((*range(HALO), *range(nb - HALO, nb))):
        parts[m] = v2[n] + flux_of(nearby(ws, n + HALO, n, few_gaps), flow[n])
    for pay, right in ((pay_a, even), (pay_b, jnp.logical_not(even))):
        for m in range(HALO):
            pay[m * part : (m + 1) * part, :] = ws[jnp.where(right, nb, HALO) + m]
            pay[(HALO + m) * part : (HALO + m + 1) * part, :] = parts[jnp.where(right, HALO, 0) + m]
    at = 2 * HALO * part
    pay_a[at : at + 2 * slots, :] = total[...]


def final(n, w3, flux, w, b, growth, rain):
    g = growth[pl.ds(n, 1), :]
    b = b + g * b * (wetness(w) - 0.4 * b)
    s = wetness(w3)
    return w3 + flux + rain[1, :, lanes(n)] - 0.2 * b * s, b + g * b * (s - 0.4 * b)


def close_kernel(
    unroll, ws, bs, v2, got_a, got_b, flow, flow_a, flow_b, gaps, growth, rain, bio_out, wat_out, ext, ext3
):
    nb, part = bs.shape[:2]
    even = right_first()
    ext[HALO : HALO + nb] = ws[HALO : HALO + nb]
    sides = ((got_a, flow_a, even), (got_b, flow_b, jnp.logical_not(even)))
    for got, _, right in sides:
        for m in range(HALO):
            ext[jnp.where(right, nb + HALO, 0) + m] = got[m * part : (m + 1) * part, :]
    for got, pay, right in sides:
        spot = jnp.where(right, nb + HALO, 0)
        for m in range(HALO):
            edge = got[(HALO + m) * part : (HALO + m + 1) * part, :]
            ext3[spot + m] = edge + halo_flux(ws, pay, right, nb, m)

    def day2(n, carry):
        ext3[n + HALO] = v2[n] + flux_of(nearby(ext, n + HALO, n, gaps), flow[n])
        return carry

    run(0, nb, unroll, day2, 0)

    def day3(n, carry):
        flux = flux_of(nearby(ext3, n + HALO, n, gaps), flow[n])
        wat_out[:, lanes(n)], bio_out[:, lanes(n)] = final(n, ext3[n + HALO], flux, ws[n + HALO], bs[n], growth, rain)
        return carry

    run(0, nb, unroll, day3, 0)


def means_kernel(unroll, count, *refs):
    bq, wq, b2, w2, b2_edge, w2_edge, means = refs[count:]
    nb, slots = bq.shape[:2]
    level = [ref[...] for ref in refs[:count]]
    while len(level) > 1:
        level = [a + b for a, b in zip(level[::2], level[1::2])]
    lw = -0.5 * jnp.sum(level[0], axis=1, keepdims=True)
    weights = []
    for c in range(CYCLES):
        x = lw[c * slots : (c + 1) * slots]
        e = jnp.exp(x - jnp.max(x, axis=0, keepdims=True))
        weights.append(jnp.broadcast_to(e / jnp.sum(e, axis=0, keepdims=True), (slots, BLK)))

    def mean(c, f, n, x):
        means[c, f : f + 1, lanes(n)] = jnp.sum(weights[c] * x, axis=0, keepdims=True)

    def fill(c, f, ref, first, last, shift):
        def step(n, carry):
            mean(c, f, n, ref[n - shift])
            return carry

        run(first, last, unroll, step, 0)

    fill(0, 0, bq, 0, nb, 0)
    fill(0, 1, wq, 0, nb, 0)
    for f, ref, edge, width in ((0, b2, b2_edge, HALO), (1, w2, w2_edge, WIDE)):
        fill(1, f, ref, width, nb - width, width)
        fill(1, f, edge, 0, width, 0)
        fill(1, f, edge, nb - width, nb, nb - 2 * width)


def weigh(flops):
    return pl.CostEstimate(flops=flops, bytes_accessed=1, transcendentals=0)


def call(kernel, out, specs, scratch=(), cost=1):
    return pl.pallas_call(
        kernel,
        out_shape=tuple(jax.ShapeDtypeStruct(s, d) for s, d in out),
        in_specs=specs,
        out_specs=tuple(VMEM for _ in out),
        scratch_shapes=list(scratch),
        compiler_params=pltpu.CompilerParams(vmem_limit_bytes=32 * 2**20),
        cost_estimate=weigh(cost),
    )


def body(biomass, water, flow_blocks, neighbours, rain, growth_rate, observations, obs_precision, ancestors):
    part, cells = biomass.shape
    nb = cells // BLK
    members, tiles = lax.axis_size("particle"), lax.axis_size("tile")
    slots = members * part
    unroll = slots <= 16
    f32, bf16, i16 = jnp.float32, jnp.bfloat16, jnp.int16
    swap_a = [(i, i ^ 1) for i in range(tiles)]
    swap_b = [(i, (i - 1) % tiles if i % 2 == 0 else (i + 1) % tiles) for i in range(tiles)]
    rows = 4 * part
    neighbours = neighbours.T

    depth = NBR * BLK
    edge = ((HALO * BLK + 16, BLK), bf16)
    tile = (HALO, 1, BLK, BLK)
    wire, early, late = pl.pallas_call(
        pack_kernel,
        grid=(1,),
        out_shape=tuple(jax.ShapeDtypeStruct((rows, n * BLK), i16) for n in (nb + 1, nb // 2 + 1, nb // 2)),
        in_specs=[pl.BlockSpec((part, cells), lambda i: (0, 0))] * 2
        + [pl.BlockSpec((2, part, cells), lambda i: (0, 0, 0))],
        out_specs=(VMEM, VMEM, VMEM),
        scratch_shapes=[pltpu.VMEM((rows, cells), f32), pltpu.VMEM((4, rows, BLK), f32)],
        compiler_params=pltpu.CompilerParams(vmem_limit_bytes=60 * 2**20),
        cost_estimate=weigh(1),
    )(biomass, water, rain)
    flow_a, flow_b = pl.pallas_call(
        edge_kernel,
        grid=(1,),
        out_shape=tuple(jax.ShapeDtypeStruct(*edge) for _ in range(2)),
        in_specs=[
            HBM,
            pl.BlockSpec(tile, lambda i: (0, 1, 0, 0)),
            pl.BlockSpec(tile, lambda i: (nb // HALO - 1, 2, 0, 0)),
            SMEM,
        ],
        out_specs=(VMEM, VMEM),
        compiler_params=pltpu.CompilerParams(vmem_limit_bytes=60 * 2**20),
        cost_estimate=weigh(1),
    )(wire, flow_blocks, flow_blocks, neighbours)

    def over(x, j):
        return lax.ppermute(x, "particle", [(i, i ^ j) for i in range(members)])

    far, later = {}, {}
    for j in range(members - 2, 0, -2):
        far[j] = over(early, j)
    beside = over(wire, 1)
    for j in range(members - 2, 0, -2):
        later[j] = over(late, j)
    for j in range(3, members, 2):
        got, flow_a = lax.optimization_barrier((far[j - 1], flow_a))
        far[j] = over(got, 1)
    small = (wire, growth_rate.reshape(nb, BLK), obs_precision.reshape(nb, BLK), observations, ancestors)
    flow, wire, growth, prec, obs, anc, rain23, gaps, few_gaps = call(
        stage_kernel,
        [((nb, depth, BLK), bf16)]
        + [(x.shape, x.dtype) for x in small]
        + [((2, part, cells), f32), ((2 * nb, slots, BLK), bf16), ((2 * nb, part, BLK), f32)],
        [HBM] + [VMEM] * 7 + [SMEM],
    )(far[2], flow_blocks, *small, rain, neighbours)
    for j in range(3, members, 2):
        got, few_gaps = lax.optimization_barrier((later[j - 1], few_gaps))
        later[j] = over(got, 1)
    far, later = ([x[j] for j in range(2, members)] for x in (far, later))
    flow_a = lax.ppermute(flow_a, "tile", swap_a)
    flow_b = lax.ppermute(flow_b, "tile", swap_b)

    field = ((nb, slots, BLK), f32)
    wb, v0, b1, bq, wq, miss, quad, unit1, pay_a, pay_b = call(
        functools.partial(open_kernel, members, unroll),
        [((nb + 2 * HALO, slots, BLK), bf16), field, field, field, field, ((slots, BLK), f32), ((4 * slots, members * rows * 2), bf16), ((slots, BLK), f32)]
        + [((3 * HALO, slots, BLK), bf16)] * 2,
        [VMEM] * (2 * members + 4),
        [
            pltpu.VMEM((8 * slots, members * rows * 2), bf16),
            pltpu.VMEM((6 * slots, members * rows * 2), bf16),
            pltpu.VMEM((2, 2 * HALO, slots, BLK), bf16),
        ],
        cost=10**10,
    )(wire, beside, *far, *later, anc, growth, prec, obs, flow, gaps)
    got_a = lax.ppermute(pay_a, "tile", swap_a)
    got_b = lax.ppermute(pay_b, "tile", swap_b)
    inner, core = nb - 2 * HALO, nb - 2 * WIDE
    indices = [
        pltpu.SMEM(ancestors.shape, jnp.int32),
        pltpu.SemaphoreType.DMA,
    ]

    def blocks(count, height=slots, kind=f32):
        return ((count, height, BLK), kind)

    r1, wb1, v1, b2, w2, wi, bi, vi, miss1, turn_a, turn_b = call(
        functools.partial(inner01_kernel, members, unroll),
        [blocks(nb), blocks(inner, kind=bf16), blocks(inner), blocks(inner), blocks(core)]
        + [blocks(core, part)] * 3
        + [((slots, BLK), f32), edge, edge],
        [VMEM] * (members + 14),
        indices,
    )(
        wire, beside, *later, wb, v0, b1, quad, unit1, flow, gaps, growth, prec, obs, anc, rain23, flow_a, flow_b
    )
    swap_rows = 2 * HALO * part
    b2_edge, w2_edge, ws, bs, v2, total, end_a, end_b = call(
        functools.partial(outer01_kernel, unroll),
        [blocks(2 * HALO), blocks(2 * WIDE)]
        + [blocks(nb + 2 * HALO, part), blocks(nb, part), blocks(nb, part)]
        + [((2 * slots, BLK), f32), ((swap_rows + 2 * slots, BLK), f32), ((swap_rows, BLK), f32)],
        [VMEM] * 24,
        [
            pltpu.VMEM((nb + 2 * HALO, slots, BLK), bf16),
            pltpu.VMEM((nb + 2 * HALO, slots, BLK), bf16),
            pltpu.VMEM((2 * HALO, slots, BLK), f32),
        ]
        + indices
        + [pltpu.VMEM((2 * HALO, part, BLK), f32)],
    )(
        wb, v0, b1, r1, wb1, v1, b2, wi, bi, vi, miss, miss1, got_a, got_b, flow, turn_a, turn_b, gaps, few_gaps,
        growth, prec, obs, anc, rain23,
    )
    last_a = lax.ppermute(end_a, "tile", swap_a)
    last_b = lax.ppermute(end_b, "tile", swap_b)

    terms = [total, last_a[swap_rows:]]
    span = 2
    while span < tiles:
        total = sum(terms[1:], terms[0])
        masks = [span] if span * 2 >= tiles else [span, 2 * span, 3 * span]
        terms = [total] + [lax.ppermute(total, "tile", [(i, i ^ m) for i in range(tiles)]) for m in masks]
        span *= 2 ** (len(masks) // 2 + 1)
    bio_out, wat_out = call(
        functools.partial(close_kernel, unroll),
        [((part, cells), f32)] * 2,
        [VMEM] * 11,
        [pltpu.VMEM((nb + 2 * HALO, part, BLK), f32)] * 2,
    )(ws, bs, v2, last_a, last_b, flow, turn_a, turn_b, few_gaps, growth, rain23)
    (means,) = call(
        functools.partial(means_kernel, unroll, len(terms)), [((CYCLES, 2, cells), f32)], [VMEM] * (len(terms) + 6)
    )(*terms, bq, wq, b2, w2, b2_edge, w2_edge)
    return means, bio_out, wat_out


def solution(mesh):
    placed = (
        P("particle", "tile"),
        P("particle", "tile"),
        P("tile", None, None, None),
        P("tile", None),
        P(None, "particle", "tile"),
        P("tile"),
        P(None, "tile"),
        P("tile"),
        P(),
    )
    return jax.shard_map(
        body,
        mesh=mesh,
        in_specs=placed,
        out_specs=(P(None, None, "tile"), P("particle", "tile"), P("particle", "tile")),
        check_vma=False,
    )
```
